32 devices in a mesh: group: 2 (over x), dp: 16 (over z, y, core).
Axes of the slice: x: 2, y: 2, z: 4, core: 2. Of those that a mesh axis runs over, the one named last changes fastest.
Arguments:
- acts: bfloat16 [16384, 4096], P(('group', 'dp')), parts along dimension 0, may hold values from -120 to 120
- grad_q: bfloat16 [16384, 4096], P(('group', 'dp')), parts along dimension 0, may hold values from -120 to 120
- grad_k: bfloat16 [16384, 1024], P(('group', 'dp')), parts along dimension 0, may hold values from -120 to 120
- grad_v: bfloat16 [16384, 1024], P(('group', 'dp')), parts along dimension 0, may hold values from -120 to 120
- proj_in: bfloat16 [64, 4096], replicated, may hold values from -0.09375 to 0.09375
- proj_q: bfloat16 [64, 4096], replicated, may hold values from -0.09375 to 0.09375
- proj_k: bfloat16 [64, 1024], replicated, may hold values from -0.1875 to 0.1875
- proj_v: bfloat16 [64, 1024], replicated, may hold values from -0.1875 to 0.1875
- query_ids: int32 [32], P(('group', 'dp')), parts along dimension 0, may hold values from 0 to 3
Outputs:
- scores: float32 [128, 16], P(('group', 'dp')), parts along dimension 0
The draws below stay inside these ranges and needn't reach their ends.
There are 2 independent parts, one for each index of `group`. The reference program is written for one: setup_inputs(seed, part) draws one part's arguments, and reference() takes and returns one part's arrays. A program takes and returns all parts, laid end to end along the dimension named above; an argument that names none is the same for every part. Nothing has to cross between parts.
Inputs may be any that keep to these rules, and one draw needn't show every extreme that they name: `query_ids`: each entry numbers a sequence from 0 within the 4 training sequences of the dp index that holds the entry.
All inputs are finite; a program needn't handle non-finite values.
Results may differ from the reference program's by a relative error of at most 0.0003.
Values sent between devices are 32-bit elements; how exact they have to be, the bound alone decides.
No kernel may reach another device: no remote copies, remote signals or barrier semaphores. Data moves between devices by JAX's collectives and lax.ppermute only.
A program may use at most 64 MiB of HBM per device.

```python
import math
import jax
import jax.numpy as jnp
from jax import lax

D = 4096
KV = 1024
R = 64
LEN = 128
SEQ_DEV = 4
Q_DEV = 1
TOKENS = 8192
QUERIES = 16


def shaped_rows(base, key, rows, cols):
    key_row, key_col = jax.random.split(key)
    position = jnp.arange(rows, dtype=jnp.float32) / max(rows - 1, 1)
    rising = 1.0 + 2.0 * position
    row_scale = jnp.exp(jax.random.uniform(key_row, (rows, 1)) * math.log(10.0))
    col_scale = jnp.exp(jax.random.uniform(key_col, (1, cols)) * math.log(10.0))
    return base * rising[:, None] * row_scale * col_scale / 10.0


def draw_acts(key, part):
    key = jax.random.fold_in(key, 11)
    key_base = jax.random.fold_in(key, 0)
    key_shape = jax.random.fold_in(key, 2)
    base = jnp.clip(jax.random.normal(key_base, (TOKENS, D)), -4.0, 4.0)
    return shaped_rows(base, key_shape, TOKENS, D).astype(jnp.bfloat16)


def draw_grad_q(key, part):
    key = jax.random.fold_in(key, 23)
    key_base = jax.random.fold_in(key, 0)
    key_shape = jax.random.fold_in(key, 2)
    base = jnp.clip(jax.random.normal(key_base, (TOKENS, D)), -4.0, 4.0)
    return shaped_rows(base, key_shape, TOKENS, D).astype(jnp.bfloat16)


def draw_grad_k(key, part):
    key = jax.random.fold_in(key, 37)
    key_base = jax.random.fold_in(key, 0)
    key_shape = jax.random.fold_in(key, 2)
    base = jnp.clip(jax.random.normal(key_base, (TOKENS, KV)), -4.0, 4.0)
    return shaped_rows(base, key_shape, TOKENS, KV).astype(jnp.bfloat16)


def draw_grad_v(key, part):
    key = jax.random.fold_in(key, 41)
    key_base = jax.random.fold_in(key, 0)
    key_shape = jax.random.fold_in(key, 2)
    base = jnp.clip(jax.random.normal(key_base, (TOKENS, KV)), -4.0, 4.0)
    return shaped_rows(base, key_shape, TOKENS, KV).astype(jnp.bfloat16)


def place_ends(drawn, rng, least, largest):
    longest = drawn.shape.index(max(drawn.shape))
    spots = []
    for shift in (0, 1):
        where = [jax.random.randint(jax.random.fold_in(rng, axis), (), 0, length) for axis, length in enumerate(drawn.shape)]
        where[longest] = (where[longest] + shift) % drawn.shape[longest]
        spots.append(tuple(where))
    return drawn.at[spots[0]].set(least).at[spots[1]].set(largest)


def centred(own_key, shape, width, most, kind=jnp.bfloat16):
    return jnp.clip(width * jax.random.normal(own_key, shape, jnp.float32), -most, most).astype(kind)


def setup_inputs(seed: int = 0, part: int = 0) -> dict:
    splits = jax.random.split(jax.random.key(seed), 10)
    part_keys = jax.random.split(jax.random.fold_in(splits[9], part), 10)
    return {
        "acts": draw_acts(jax.random.fold_in(jax.random.fold_in(splits[9], part), 71), part),
        "grad_q": draw_grad_q(jax.random.fold_in(jax.random.fold_in(splits[9], part), 71), part),
        "grad_k": draw_grad_k(jax.random.fold_in(jax.random.fold_in(splits[9], part), 71), part),
        "grad_v": draw_grad_v(jax.random.fold_in(jax.random.fold_in(splits[9], part), 71), part),
        "proj_in": centred(splits[4], (R, D), D ** -0.5, 0.09375),
        "proj_q": centred(splits[5], (R, D), D ** -0.5, 0.09375),
        "proj_k": centred(splits[6], (R, KV), KV ** -0.5, 0.1875),
        "proj_v": centred(splits[7], (R, KV), KV ** -0.5, 0.1875),
        "query_ids": place_ends(jax.random.randint(part_keys[8], (QUERIES,), 0, SEQ_DEV), jax.random.fold_in(part_keys[8], 1), 0, SEQ_DEV - 1).astype(jnp.int32),
    }


def project_rows(data, table):
    return lax.dot_general(data.astype(jnp.float32), table.astype(jnp.float32), (((1,), (1,)), ((), ())), preferred_element_type=jnp.float32)

def damped_inverse(matrix):
    order = matrix.shape[0]
    identity = jnp.eye(order, dtype=jnp.float32)
    damping = 0.1 * jnp.trace(matrix) / order
    factor = jnp.linalg.cholesky(matrix + damping * identity)
    return jax.scipy.linalg.cho_solve((factor, True), identity)

def reference(acts, grad_q, grad_k, grad_v, proj_in, proj_q, proj_k, proj_v, query_ids):
    in_coords = project_rows(acts, proj_in)
    out_coords = jnp.stack([project_rows(grad_q, proj_q), project_rows(grad_k, proj_k), project_rows(grad_v, proj_v)], axis=1)
    tokens_all = in_coords.shape[0]
    in_factor = jnp.einsum('tr,ts->rs', in_coords, in_coords, precision=lax.Precision.HIGHEST) / tokens_all
    out_factor = jnp.einsum('tpr,tps->prs', out_coords, out_coords, precision=lax.Precision.HIGHEST) / tokens_all
    in_inverse = damped_inverse(in_factor)
    out_inverse = jax.vmap(damped_inverse)(out_factor)
    sequences = tokens_all // LEN
    in_seq = in_coords.reshape(sequences, LEN, R)
    out_seq = out_coords.reshape(sequences, LEN, 3, R)
    example_grads = jnp.einsum('slpa,slb->spab', out_seq, in_seq, precision=lax.Precision.HIGHEST) / LEN
    chosen = jnp.arange(QUERIES, dtype=jnp.int32) // Q_DEV * SEQ_DEV + query_ids.astype(jnp.int32)
    query_grads = example_grads[chosen]
    left_side = jnp.einsum('pac,spcd->spad', out_inverse, example_grads, precision=lax.Precision.HIGHEST)
    conditioned = jnp.einsum('spad,db->spab', left_side, in_inverse, precision=lax.Precision.HIGHEST)
    return jnp.einsum('spab,qpab->sq', conditioned, query_grads, precision=lax.Precision.HIGHEST)
```

```python
import functools

import jax
import jax.numpy as jnp
from jax import lax
from jax.experimental import pallas as pl
from jax.experimental.pallas import tpu as pltpu
from jax.sharding import PartitionSpec as P

LEN = 128
HIGHEST = lax.Precision.HIGHEST
VMEM_BYTES = 40 * 1024 * 1024
NT = (((1,), (1,)), ((), ()))
TN = (((0,), (0,)), ((), ()))
NN = (((1,), (0,)), ((), ()))


def dot(a, b, dims, precision=HIGHEST):
    return lax.dot_general(a, b, dims, precision=precision, preferred_element_type=jnp.float32)


def pack_square(dst, index, m):
    half = m.shape[0] // 2
    dst[index, :, : m.shape[1]] = m[:half]
    dst[index, :, m.shape[1] :] = m[half:]


def unpack_square(m):
    width = m.shape[1] // 2
    return jnp.concatenate([m[:, :width], m[:, width:]], axis=0)


def front_kernel(
    total_tokens, sequences, width,
    ids, acts, grad_q, grad_k, grad_v, proj_in, proj_q, proj_k, proj_v,
    keep, give1, give2, give3, grams, query,
    acts_v, gq_v, gk_v, gv_v, pi_v, pq_v, pk_v, pv_v, factor_v, sem,
):
    sent = []

    def fetch(src, dst):
        copy = pltpu.make_async_copy(src, dst, sem.at[len(sent)])
        copy.start()
        sent.append(copy)
        return copy

    c_pk = fetch(proj_k, pk_v)
    c_gk = fetch(grad_k, gk_v)
    c_pv = fetch(proj_v, pv_v)
    c_gv = fetch(grad_v, gv_v)
    c_pi = fetch(proj_in, pi_v)
    c_pq = fetch(proj_q, pq_v)
    c_acts, c_gq = [], []
    for s in range(sequences):
        rows = pl.ds(s * LEN, LEN)
        c_acts.append(fetch(acts.at[rows], acts_v.at[rows]))
        c_gq.append(fetch(grad_q.at[rows], gq_v.at[rows]))

    c_pk.wait()
    c_gk.wait()
    coords_k = dot(gk_v[...], pk_v[...], NT, None)
    c_pv.wait()
    c_gv.wait()
    coords_v = dot(gv_v[...], pv_v[...], NT, None)
    c_pi.wait()
    c_pq.wait()
    total = None
    for s in range(sequences):
        rows = pl.ds(s * LEN, LEN)
        c_acts[s].wait()
        coords_in = dot(acts_v[rows], pi_v[...], NT, None)
        c_gq[s].wait()
        coords_q = dot(gq_v[rows], pq_v[...], NT, None)
        here = slice(s * LEN, (s + 1) * LEN)
        coords = jnp.concatenate([coords_in, coords_q, coords_k[here], coords_v[here]], axis=1)
        gram = dot(coords, coords, TN)
        grams[s] = gram[:width] * (1.0 / LEN)
        total = gram if total is None else total + gram
    for p in range(4):
        part = slice(p * width, (p + 1) * width)
        pack_square(factor_v, p, total[part, part] * (1.0 / total_tokens))
    mine = lax.rem(lax.axis_index("dp"), 4)
    for away, dst in enumerate((keep, give1, give2, give3)):
        dst[...] = factor_v[mine ^ away]
    half = width // 2
    for q in range(query.shape[0]):
        chosen = grams[ids[q]]
        query[q, :width] = chosen[:, width : 3 * width]
        query[q, width:, :width] = chosen[:half, 3 * width :]
        query[q, width:, width:] = chosen[half:, 3 * width :]


def invert_kernel(*refs):
    parts, out, stage = refs[:-2], refs[-2], refs[-1]
    m = parts[0][...]
    for part in parts[1:]:
        m = m + part[...]
    m = unpack_square(m)
    order = m.shape[0]
    row_id = lax.broadcasted_iota(jnp.int32, m.shape, 0)
    col_id = lax.broadcasted_iota(jnp.int32, m.shape, 1)
    trace = jnp.sum(jnp.where(row_id == col_id, m, 0.0))
    m = m + jnp.where(row_id == col_id, 0.1 * trace / order, 0.0)
    for k in range(order):
        column = m[:, k : k + 1]
        pivot = 1.0 / m[k : k + 1, k : k + 1]
        row = jnp.where(col_id[:1] == k, 1.0, m[k : k + 1]) * pivot
        rest = jnp.where(col_id == k, 0.0, m) - column * row
        m = jnp.where(row_id == k, row, rest)
    pack_square(stage, 0, m)
    out[...] = stage[0]


def score_kernel(
    pieces, sequences, width, queries,
    inverse0, inverse1, inverse2, inverse3, grams, *refs,
):
    blocks, out = refs[:pieces], refs[pieces]
    factor_v, side_v, left_v, train_v, partial_v = refs[pieces + 1 :]
    me = lax.axis_index("dp")
    mine = lax.rem(me, 4)
    for away, src in enumerate((inverse0, inverse1, inverse2, inverse3)):
        factor_v[mine ^ away] = src[...]
    inverse_in = unpack_square(factor_v[0])
    side_v[...] = jnp.zeros_like(side_v)
    for p in range(3):
        part = pl.ds(p * width, width)
        side_v[pl.ds((p + 1) * width, width), part] = unpack_square(factor_v[p + 1])
    left_v[...] = dot(grams[...].reshape(sequences * width, 4 * width), side_v[...], NN)
    half = width // 2
    for s in range(sequences):
        done = dot(inverse_in, left_v[pl.ds(s * width, width)], NN)
        train_v[s, :width] = done[:, : 2 * width]
        train_v[s, width:, :width] = done[:half, 2 * width :]
        train_v[s, width:, width:] = done[half:, 2 * width :]
    slot = 0
    for block in blocks:
        for i in range(block.shape[0]):
            value = block[i]
            for s in range(sequences):
                product = (train_v[s] * value).reshape(-1, 8, 2 * width)
                partial_v[s, pl.ds(slot * 8, 8)] = jnp.sum(product, axis=0)
            slot += 1
    per_device = queries // lax.axis_size("dp")
    shape = (queries, queries * 8)
    target = lax.broadcasted_iota(jnp.int32, shape, 0)
    source = lax.broadcasted_iota(jnp.int32, shape, 1) // 8
    slot, half_devices = source // per_device, lax.axis_size("dp") // 2
    offset = slot % half_devices * 2 + slot // half_devices
    placed = (offset ^ me) * per_device + source % per_device
    select = jnp.where(target == placed, 1.0, 0.0)
    ones = jnp.ones((8, 2 * width), jnp.float32)
    for s in range(sequences):
        by_query = dot(select, partial_v[s], NN)
        out[pl.ds(s, 1)] = dot(ones, by_query, NT)[:1]


def exchange(x, devices, distance):
    return lax.ppermute(x, "dp", [(i, i ^ distance) for i in range(devices)])


def bit_groups(bits, most):
    return [bits[i : i + most] for i in range(0, len(bits), most)]


def distances(bits):
    return [sum(bits[j] for j in range(len(bits)) if pick >> j & 1) for pick in range(1, 1 << len(bits))]


def per_device(acts, grad_q, grad_k, grad_v, proj_in, proj_q, proj_k, proj_v, query_ids):
    devices = lax.axis_size("dp")
    bits = [1 << j for j in range(devices.bit_length() - 1)]
    tokens, width = acts.shape[0], proj_in.shape[0]
    sequences, own_queries = tokens // LEN, query_ids.shape[0]
    queries = own_queries * devices
    f32 = jnp.float32
    square = jax.ShapeDtypeStruct((width // 2, 2 * width), f32)
    in_vmem = pl.BlockSpec(memory_space=pltpu.VMEM)
    in_hbm = pl.BlockSpec(memory_space=pl.ANY)
    params = pltpu.CompilerParams(vmem_limit_bytes=VMEM_BYTES)
    tables = (acts, grad_q, grad_k, grad_v, proj_in, proj_q, proj_k, proj_v)

    keep, give1, give2, give3, grams, query = pl.pallas_call(
        functools.partial(front_kernel, tokens * devices, sequences, width),
        out_shape=(
            square, square, square, square,
            jax.ShapeDtypeStruct((sequences, width, 4 * width), f32),
            jax.ShapeDtypeStruct((own_queries, 3 * width // 2, 2 * width), f32),
        ),
        in_specs=[pl.BlockSpec(memory_space=pltpu.SMEM)] + [in_hbm] * 8,
        out_specs=(in_vmem,) * 6,
        scratch_shapes=[pltpu.VMEM(t.shape, t.dtype) for t in tables]
        + [pltpu.VMEM((4, width // 2, 2 * width), f32), pltpu.SemaphoreType.DMA((6 + 2 * sequences,))],
        compiler_params=params,
        name="front",
    )(query_ids, *tables)

    blocks = [query]
    for group in bit_groups(bits[1:], 3) + [bits[:1]]:
        sent = blocks[0] if len(blocks) == 1 else jnp.concatenate(blocks, axis=0)
        blocks = blocks + [exchange(sent, devices, d) for d in distances(group)]

    parts = [keep] + [exchange(x, devices, d) for d, x in zip((1, 2, 3), (give1, give2, give3))]
    for group in bit_groups(bits[2:], 2):
        mine = functools.reduce(jnp.add, parts)
        parts = [mine] + [exchange(mine, devices, d) for d in distances(group)]

    inverse = pl.pallas_call(
        invert_kernel,
        out_shape=square,
        in_specs=[in_vmem] * len(parts),
        out_specs=in_vmem,
        scratch_shapes=[pltpu.VMEM((1, width // 2, 2 * width), f32)],
        compiler_params=params,
        name="invert",
    )(*parts)
    inverses = [inverse] + [exchange(inverse, devices, d) for d in (1, 2, 3)]

    return pl.pallas_call(
        functools.partial(score_kernel, len(blocks), sequences, width, queries),
        out_shape=jax.ShapeDtypeStruct((sequences, queries), f32),
        in_specs=[in_vmem] * (5 + len(blocks)),
        out_specs=in_vmem,
        scratch_shapes=[
            pltpu.VMEM((4, width // 2, 2 * width), f32),
            pltpu.VMEM((4 * width, 3 * width), f32),
            pltpu.VMEM((sequences * width, 3 * width), f32),
            pltpu.VMEM((sequences, 3 * width // 2, 2 * width), f32),
            pltpu.VMEM((sequences, queries * 8, 2 * width), f32),
        ],
        compiler_params=params,
        name="scores",
    )(*inverses, grams, *blocks)


def solution(mesh):
    return jax.shard_map(
        per_device,
        mesh=mesh,
        in_specs=(
            P(("group", "dp"), None),
            P(("group", "dp"), None),
            P(("group", "dp"), None),
            P(("group", "dp"), None),
            P(),
            P(),
            P(),
            P(),
            P(("group", "dp")),
        ),
        out_specs=P(("group", "dp"), None),
        check_vma=False,
    )
```

```python
import functools

import jax
import jax.numpy as jnp
from jax import lax
from jax.experimental import pallas as pl
from jax.experimental.pallas import tpu as pltpu
from jax.sharding import PartitionSpec as P

LEN = 128
LANES = 128
PANEL = 8
HIGHEST = lax.Precision.HIGHEST
VMEM_BYTES = 40 * 1024 * 1024
NT = (((1,), (1,)), ((), ()))
TN = (((0,), (0,)), ((), ()))
NN = (((1,), (0,)), ((), ()))


def dot(a, b, dims, precision=HIGHEST):
    return lax.dot_general(a, b, dims, precision=precision, preferred_element_type=jnp.float32)


def front_kernel(
    total_tokens, sequences, width,
    ids, acts, grad_q, grad_k, grad_v, proj_in, proj_q, proj_k, proj_v,
    factors, grams, query,
    acts_v, gq_v, gk_v, gv_v, pi_v, pq_v, pk_v, pv_v, sem,
):
    sent = []

    def fetch(src, dst):
        copy = pltpu.make_async_copy(src, dst, sem.at[len(sent)])
        copy.start()
        sent.append(copy)
        return copy

    c_pk = fetch(proj_k, pk_v)
    c_gk = fetch(grad_k, gk_v)
    c_pv = fetch(proj_v, pv_v)
    c_gv = fetch(grad_v, gv_v)
    c_pi = fetch(proj_in, pi_v)
    c_pq = fetch(proj_q, pq_v)
    c_acts, c_gq = [], []
    for s in range(sequences):
        rows = pl.ds(s * LEN, LEN)
        c_acts.append(fetch(acts.at[rows], acts_v.at[rows]))
        c_gq.append(fetch(grad_q.at[rows], gq_v.at[rows]))

    c_pk.wait()
    c_gk.wait()
    coords_k = dot(gk_v[...], pk_v[...], NT, None)
    c_pv.wait()
    c_gv.wait()
    coords_v = dot(gv_v[...], pv_v[...], NT, None)
    c_pi.wait()
    c_pq.wait()
    total = None
    for s in range(sequences):
        rows = pl.ds(s * LEN, LEN)
        c_acts[s].wait()
        coords_in = dot(acts_v[rows], pi_v[...], NT, None)
        c_gq[s].wait()
        coords_q = dot(gq_v[rows], pq_v[...], NT, None)
        here = slice(s * LEN, (s + 1) * LEN)
        coords = jnp.concatenate([coords_in, coords_q, coords_k[here], coords_v[here]], axis=1)
        gram = dot(coords, coords, TN)
        grams[s] = gram[:width] * (1.0 / LEN)
        total = gram if total is None else total + gram
    half = width // 2
    for p in range(4):
        part = slice(p * width, (p + 1) * width)
        block = total[part, part] * (1.0 / total_tokens)
        lanes = slice(p * half, (p + 1) * half)
        factors[:width, lanes] = block[:, :half]
        factors[width:, lanes] = block[:, half:]
    for q in range(query.shape[0]):
        chosen = grams[ids[q]]
        query[q, :width] = chosen[:, width : 3 * width]
        query[q, width:, :width] = chosen[:half, 3 * width :]
        query[q, width:, width:] = chosen[half:, 3 * width :]


def damped(factors):
    order = factors.shape[0] // 2
    half = order // 2
    row = lax.broadcasted_iota(jnp.int32, factors.shape, 0)
    lane = lax.broadcasted_iota(jnp.int32, factors.shape, 1)
    on_diagonal = row == lane % half + jnp.where(row < order, 0, order + half)
    column_sums = jnp.sum(jnp.where(on_diagonal, factors, 0.0), axis=0, keepdims=True)
    shape = (LANES, LANES)
    same = (
        lax.broadcasted_iota(jnp.int32, shape, 0) // half
        == lax.broadcasted_iota(jnp.int32, shape, 1) // half
    )
    traces = dot(jnp.broadcast_to(column_sums, (8, LANES)), jnp.where(same, 1.0, 0.0), NN)[:1]
    return factors + jnp.where(on_diagonal, traces * (0.1 / order), 0.0)


def invert(factors):
    order = factors.shape[0] // 2
    half = order // 2
    groups = order // 8
    state = [
        [factors[h * order + 8 * g : h * order + 8 * g + 8] for g in range(groups)] for h in range(2)
    ]
    lane = lax.broadcasted_iota(jnp.int32, (8, LANES), 1)
    row = lax.broadcasted_iota(jnp.int32, (8, LANES), 0)
    column_of_lane = lane % half
    first_lane = lane - column_of_lane
    for start in range(0, order, PANEL):
        h, first = start // half, start % half
        spread = [
            [jnp.take_along_axis(state[h][g], first_lane + (first + j), axis=1) for g in range(groups)]
            for j in range(PANEL)
        ]
        in_panel = (column_of_lane >= first) & (column_of_lane < first + PANEL)
        state[h] = [jnp.where(in_panel, 0.0, x) for x in state[h]]
        for j in range(PANEL):
            k = start + j
            g, r = k // 8, k % 8
            column = spread[j]
            pivot = 1.0 / column[g][r : r + 1]
            for t in range(2):
                values = state[t][g][r : r + 1]
                if t == h:
                    values = jnp.where(column_of_lane[:1] == first + j, 1.0, values)
                values = values * pivot
                state[t] = [x - c * values for x, c in zip(state[t], column)]
                state[t][g] = jnp.where(row == r, values, state[t][g])
            for i in range(j + 1, PANEL):
                values = spread[i][g][r : r + 1] * pivot
                spread[i] = [x - c * values for x, c in zip(spread[i], column)]
                spread[i][g] = jnp.where(row == r, values, spread[i][g])
    return [jnp.concatenate(state[h], axis=0) for h in range(2)]


def invert_kernel(sequences, width, first, second, grams, train, side_v, left_v):
    half = width // 2
    low, high = invert(damped(first[...] + second[...]))
    inverse_in = jnp.concatenate([low[:, :half], high[:, :half]], axis=1)
    side_v[...] = jnp.zeros_like(side_v)
    for p in range(3):
        rows = slice((p + 1) * width, (p + 2) * width)
        lanes = slice((p + 1) * half, (p + 2) * half)
        side_v[rows, p * width : p * width + half] = low[:, lanes]
        side_v[rows, p * width + half : (p + 1) * width] = high[:, lanes]
    left_v[...] = dot(grams[...].reshape(sequences * width, 4 * width), side_v[...], NN)
    for s in range(sequences):
        done = dot(inverse_in, left_v[pl.ds(s * width, width)], NN)
        train[s, :width] = done[:, : 2 * width]
        train[s, width:, :width] = done[:half, 2 * width :]
        train[s, width:, width:] = done[half:, 2 * width :]


def score_kernel(offsets, sequences, width, queries, train, *refs):
    blocks, out, partial_v = refs[:-2], refs[-2], refs[-1]
    me = lax.axis_index("dp")
    slot = 0
    for block in blocks:
        for i in range(block.shape[0]):
            value = block[i]
            for s in range(sequences):
                product = (train[s] * value).reshape(-1, 8, 2 * width)
                partial_v[s, pl.ds(slot * 8, 8)] = jnp.sum(product, axis=0)
            slot += 1
    own = queries // lax.axis_size("dp")
    shape = (queries, queries * 8)
    target = lax.broadcasted_iota(jnp.int32, shape, 0)
    source = lax.broadcasted_iota(jnp.int32, shape, 1) // 8
    offset = offsets(source // own)
    select = jnp.where(target == (offset ^ me) * own + source % own, 1.0, 0.0)
    ones = jnp.ones((8, 2 * width), jnp.float32)
    for s in range(sequences):
        by_query = dot(select, partial_v[s], NN)
        out[pl.ds(s, 1)] = dot(ones, by_query, NT)[:1]


def exchange(x, devices, distance):
    return lax.ppermute(x, "dp", [(i, i ^ distance) for i in range(devices)])


def reversed_bits(count, slot):
    out = jnp.zeros_like(slot)
    for j in range(count):
        out = out + (slot >> j & 1) * (1 << (count - 1 - j))
    return out


def per_device(acts, grad_q, grad_k, grad_v, proj_in, proj_q, proj_k, proj_v, query_ids):
    devices = lax.axis_size("dp")
    steps = devices.bit_length() - 1
    tokens, width = acts.shape[0], proj_in.shape[0]
    sequences, own_queries = tokens // LEN, query_ids.shape[0]
    queries = own_queries * devices
    f32 = jnp.float32
    in_vmem = pl.BlockSpec(memory_space=pltpu.VMEM)
    in_hbm = pl.BlockSpec(memory_space=pltpu.HBM)
    params = pltpu.CompilerParams(vmem_limit_bytes=VMEM_BYTES)
    tables = (acts, grad_q, grad_k, grad_v, proj_in, proj_q, proj_k, proj_v)

    factors, grams, query = pl.pallas_call(
        functools.partial(front_kernel, tokens * devices, sequences, width),
        out_shape=(
            jax.ShapeDtypeStruct((2 * width, 2 * width), f32),
            jax.ShapeDtypeStruct((sequences, width, 4 * width), f32),
            jax.ShapeDtypeStruct((own_queries, 3 * width // 2, 2 * width), f32),
        ),
        in_specs=[pl.BlockSpec(memory_space=pltpu.SMEM)] + [in_hbm] * 8,
        out_specs=(in_vmem,) * 3,
        scratch_shapes=[pltpu.VMEM(t.shape, t.dtype) for t in tables]
        + [pltpu.SemaphoreType.DMA((6 + 2 * sequences,))],
        compiler_params=params,
        name="front",
    )(query_ids, *tables)

    blocks, terms = [query], (factors, None)
    for step in range(steps):
        mine = terms[0] if terms[1] is None else terms[0] + terms[1]
        theirs = exchange(mine, devices, 1 << step)
        sent = blocks[0] if step == 0 else jnp.concatenate(blocks, axis=0)
        sent, mine = lax.optimization_barrier((sent, mine))
        blocks.append(exchange(sent, devices, 1 << (steps - 1 - step)))
        terms = (mine, theirs)

    train = pl.pallas_call(
        functools.partial(invert_kernel, sequences, width),
        out_shape=jax.ShapeDtypeStruct((sequences, 3 * width // 2, 2 * width), f32),
        in_specs=[in_vmem] * 3,
        out_specs=in_vmem,
        scratch_shapes=[
            pltpu.VMEM((4 * width, 3 * width), f32),
            pltpu.VMEM((sequences * width, 3 * width), f32),
        ],
        compiler_params=params,
        name="invert",
    )(*terms, grams)

    return pl.pallas_call(
        functools.partial(
            score_kernel, functools.partial(reversed_bits, steps), sequences, width, queries
        ),
        out_shape=jax.ShapeDtypeStruct((sequences, queries), f32),
        in_specs=[in_vmem] * (1 + len(blocks)),
        out_specs=in_vmem,
        scratch_shapes=[pltpu.VMEM((sequences, queries * 8, 2 * width), f32)],
        compiler_params=params,
        name="scores",
    )(train, *blocks)


def solution(mesh):
    return jax.shard_map(
        per_device,
        mesh=mesh,
        in_specs=(
            P(("group", "dp"), None),
            P(("group", "dp"), None),
            P(("group", "dp"), None),
            P(("group", "dp"), None),
            P(),
            P(),
            P(),
            P(),
            P(("group", "dp")),
        ),
        out_specs=P(("group", "dp"), None),
        check_vma=False,
    )
```

```python
import functools

import jax
import jax.numpy as jnp
from jax import lax
from jax.experimental import pallas as pl
from jax.experimental.pallas import tpu as pltpu
from jax.sharding import PartitionSpec as P

LEN = 128
LANES = 128
PANEL = 8
HIGHEST = lax.Precision.HIGHEST
FRONT_VMEM_BYTES = 56 * 1024 * 1024
VMEM_BYTES = 8 * 1024 * 1024
NT = (((1,), (1,)), ((), ()))
TN = (((0,), (0,)), ((), ()))
NN = (((1,), (0,)), ((), ()))


def dot(a, b, dims, precision=HIGHEST):
    return lax.dot_general(a, b, dims, precision=precision, preferred_element_type=jnp.float32)


def places(order):
    shape = (order, 2 * order)
    lane = lax.broadcasted_iota(jnp.int32, shape, 1)
    return lax.broadcasted_iota(jnp.int32, shape, 0), lane % order


def front_kernel(
    total_tokens, sequences, width,
    ids, acts, grad_q, grad_k, grad_v, proj_in, proj_q, proj_k, proj_v,
    factors, grams, query,
    acts_v, gq_v, gk_v, gv_v, pi_v, pq_v, pk_v, pv_v, sem,
):
    sent = []

    def fetch(src, dst):
        copy = pltpu.make_async_copy(src, dst, sem.at[len(sent)])
        copy.start()
        sent.append(copy)
        return copy

    c_pk = fetch(proj_k, pk_v)
    c_gk = fetch(grad_k, gk_v)
    c_pv = fetch(proj_v, pv_v)
    c_gv = fetch(grad_v, gv_v)
    c_pi = fetch(proj_in, pi_v)
    c_pq = fetch(proj_q, pq_v)
    c_acts, c_gq = [], []
    for s in range(sequences):
        rows = pl.ds(s * LEN, LEN)
        c_acts.append(fetch(acts.at[rows], acts_v.at[rows]))
        c_gq.append(fetch(grad_q.at[rows], gq_v.at[rows]))

    c_pk.wait()
    c_gk.wait()
    coords_k = dot(gk_v[...], pk_v[...], NT, None)
    c_pv.wait()
    c_gv.wait()
    coords_v = dot(gv_v[...], pv_v[...], NT, None)
    c_pi.wait()
    c_pq.wait()
    total = None
    for s in range(sequences):
        rows = pl.ds(s * LEN, LEN)
        c_acts[s].wait()
        coords_in = dot(acts_v[rows], pi_v[...], NT, None)
        c_gq[s].wait()
        coords_q = dot(gq_v[rows], pq_v[...], NT, None)
        here = slice(s * LEN, (s + 1) * LEN)
        coords = jnp.concatenate([coords_in, coords_q, coords_k[here], coords_v[here]], axis=1)
        gram = dot(coords, coords, TN)
        grams[s] = gram[:width] * (1.0 / LEN)
        total = gram if total is None else total + gram
    half = width // 2

    def square(p):
        part = slice(p * width, (p + 1) * width)
        return total[part, part] * (1.0 / total_tokens)

    upper = jnp.concatenate([square(0), square(2)], axis=1)
    lower = jnp.concatenate([square(1), square(3)], axis=1)
    row, column = places(width)
    factors[:width] = jnp.where(column >= row, upper, lower)
    diagonal = jnp.sum(jnp.where(column == row, lower, 0.0), axis=0, keepdims=True)
    factors[width:] = jnp.broadcast_to(diagonal, (8, 2 * width))
    for q in range(query.shape[0]):
        chosen = grams[ids[q]]
        query[q, :width] = chosen[:, width : 3 * width]
        query[q, width:, :width] = chosen[:half, 3 * width :]
        query[q, width:, width:] = chosen[half:, 3 * width :]


def damped(packed):
    order = packed.shape[1] // 2
    half = order // 2
    square, diagonal = packed[:order], packed[order : order + 1]
    row, column = places(order)
    turned = square.T
    turned = jnp.concatenate([turned[:order], turned[order:]], axis=1)
    on_diagonal = column == row
    first = jnp.where(column >= row, square, turned)
    second = jnp.where(column < row, square, turned)
    first_diagonal = jnp.sum(jnp.where(on_diagonal, square, 0.0), axis=0, keepdims=True)
    shape = (LANES, LANES)
    same = (
        lax.broadcasted_iota(jnp.int32, shape, 0) // order
        == lax.broadcasted_iota(jnp.int32, shape, 1) // order
    )
    diagonals = jnp.concatenate([first_diagonal, diagonal], axis=0)
    diagonals = jnp.concatenate([diagonals] * 4, axis=0)
    damping = dot(diagonals, jnp.where(same, 0.1 / order, 0.0), NN)
    first = first + jnp.where(on_diagonal, damping[:1], 0.0)
    second = jnp.where(on_diagonal, diagonal + damping[1:2], second)
    is_low = column < half
    low = jnp.where(is_low, first, pltpu.roll(second, half, 1))
    high = jnp.where(is_low, pltpu.roll(first, LANES - half, 1), second)
    return low, high


def invert(low, high):
    order = low.shape[0]
    half = order // 2
    groups = order // 8
    state = [[x[8 * g : 8 * g + 8] for g in range(groups)] for x in (low, high)]
    lane = lax.broadcasted_iota(jnp.int32, (8, LANES), 1)
    row = lax.broadcasted_iota(jnp.int32, (8, LANES), 0)
    column_of_lane = lane % half
    first_lane = lane - column_of_lane
    for start in range(0, order, PANEL):
        h, first = start // half, start % half
        spread = [
            [jnp.take_along_axis(state[h][g], first_lane + (first + j), axis=1) for g in range(groups)]
            for j in range(PANEL)
        ]
        in_panel = (column_of_lane >= first) & (column_of_lane < first + PANEL)
        state[h] = [jnp.where(in_panel, 0.0, x) for x in state[h]]
        for j in range(PANEL):
            k = start + j
            g, r = k // 8, k % 8
            column = spread[j]
            pivot = 1.0 / column[g][r : r + 1]
            for t in range(2):
                values = state[t][g][r : r + 1]
                if t == h:
                    values = jnp.where(column_of_lane[:1] == first + j, 1.0, values)
                values = values * pivot
                state[t] = [x - c * values for x, c in zip(state[t], column)]
                state[t][g] = jnp.where(row == r, values, state[t][g])
            for i in range(j + 1, PANEL):
                values = spread[i][g][r : r + 1] * pivot
                spread[i] = [x - c * values for x, c in zip(spread[i], column)]
                spread[i][g] = jnp.where(row == r, values, spread[i][g])
    return [jnp.concatenate(state[h], axis=0) for h in range(2)]


def invert_kernel(sequences, width, first, second, grams, train, side_v, left_v):
    half = width // 2
    low, high = invert(*damped(first[...] + second[...]))
    inverse_in = jnp.concatenate([low[:, :half], high[:, :half]], axis=1)
    side_v[...] = jnp.zeros_like(side_v)
    for p in range(3):
        rows = slice((p + 1) * width, (p + 2) * width)
        lanes = slice((p + 1) * half, (p + 2) * half)
        side_v[rows, p * width : p * width + half] = low[:, lanes]
        side_v[rows, p * width + half : (p + 1) * width] = high[:, lanes]
    left_v[...] = dot(grams[...].reshape(sequences * width, 4 * width), side_v[...], NN)
    for s in range(sequences):
        done = dot(inverse_in, left_v[pl.ds(s * width, width)], NN)
        train[s, :width] = done[:, : 2 * width]
        train[s, width:, :width] = done[:half, 2 * width :]
        train[s, width:, width:] = done[half:, 2 * width :]


def score_kernel(offsets, sequences, width, queries, train, *refs):
    blocks, out, partial_v = refs[:-2], refs[-2], refs[-1]
    me = lax.axis_index("dp")
    slot = 0
    for block in blocks:
        for i in range(block.shape[0]):
            value = block[i]
            for s in range(sequences):
                product = (train[s] * value).reshape(-1, 8, 2 * width)
                partial_v[s, pl.ds(slot * 8, 8)] = jnp.sum(product, axis=0)
            slot += 1
    own = queries // lax.axis_size("dp")
    shape = (queries, queries * 8)
    target = lax.broadcasted_iota(jnp.int32, shape, 0)
    source = lax.broadcasted_iota(jnp.int32, shape, 1) // 8
    offset = offsets(source // own)
    select = jnp.where(target == (offset ^ me) * own + source % own, 1.0, 0.0)
    ones = jnp.ones((8, 2 * width), jnp.float32)
    for s in range(sequences):
        by_query = dot(select, partial_v[s], NN)
        out[pl.ds(s, 1)] = dot(ones, by_query, NT)[:1]


def exchange(x, devices, distance):
    return lax.ppermute(x, "dp", [(i, i ^ distance) for i in range(devices)])


def reversed_bits(count, slot):
    out = jnp.zeros_like(slot)
    for j in range(count):
        out = out + (slot >> j & 1) * (1 << (count - 1 - j))
    return out


def per_device(acts, grad_q, grad_k, grad_v, proj_in, proj_q, proj_k, proj_v, query_ids):
    devices = lax.axis_size("dp")
    steps = devices.bit_length() - 1
    tokens, width = acts.shape[0], proj_in.shape[0]
    sequences, own_queries = tokens // LEN, query_ids.shape[0]
    queries = own_queries * devices
    f32 = jnp.float32
    in_vmem = pl.BlockSpec(memory_space=pltpu.VMEM)
    in_hbm = pl.BlockSpec(memory_space=pltpu.HBM)
    params = pltpu.CompilerParams(vmem_limit_bytes=VMEM_BYTES)
    tables = (acts, grad_q, grad_k, grad_v, proj_in, proj_q, proj_k, proj_v)

    factors, grams, query = pl.pallas_call(
        functools.partial(front_kernel, tokens * devices, sequences, width),
        out_shape=(
            jax.ShapeDtypeStruct((width + 8, 2 * width), f32),
            jax.ShapeDtypeStruct((sequences, width, 4 * width), f32),
            jax.ShapeDtypeStruct((own_queries, 3 * width // 2, 2 * width), f32),
        ),
        in_specs=[pl.BlockSpec(memory_space=pltpu.SMEM)] + [in_hbm] * 8,
        out_specs=(in_vmem,) * 3,
        scratch_shapes=[pltpu.VMEM(t.shape, t.dtype) for t in tables]
        + [pltpu.SemaphoreType.DMA((6 + 2 * sequences,))],
        compiler_params=pltpu.CompilerParams(vmem_limit_bytes=FRONT_VMEM_BYTES),
        name="front",
    )(query_ids, *tables)

    blocks, terms, waiting = [query], (factors, None), None
    for step in range(steps):
        mine = terms[0] if terms[1] is None else terms[0] + terms[1]
        theirs = exchange(mine, devices, 1 << step)
        if waiting is not None:
            waiting, theirs = lax.optimization_barrier((waiting, theirs))
            blocks.append(waiting)
        sent = blocks[0] if step == 0 else jnp.concatenate(blocks, axis=0)
        waiting = exchange(sent, devices, 1 << (steps - 1 - step))
        terms = (mine, theirs)
    blocks.append(waiting)

    train = pl.pallas_call(
        functools.partial(invert_kernel, sequences, width),
        out_shape=jax.ShapeDtypeStruct((sequences, 3 * width // 2, 2 * width), f32),
        in_specs=[in_vmem] * 3,
        out_specs=in_vmem,
        scratch_shapes=[
            pltpu.VMEM((4 * width, 3 * width), f32),
            pltpu.VMEM((sequences * width, 3 * width), f32),
        ],
        compiler_params=params,
        name="invert",
    )(*terms, grams)

    return pl.pallas_call(
        functools.partial(
            score_kernel, functools.partial(reversed_bits, steps), sequences, width, queries
        ),
        out_shape=jax.ShapeDtypeStruct((sequences, queries), f32),
        in_specs=[in_vmem] * (1 + len(blocks)),
        out_specs=in_vmem,
        scratch_shapes=[pltpu.VMEM((sequences, queries * 8, 2 * width), f32)],
        compiler_params=params,
        name="scores",
    )(train, *blocks)


def solution(mesh):
    return jax.shard_map(
        per_device,
        mesh=mesh,
        in_specs=(
            P(("group", "dp"), None),
            P(("group", "dp"), None),
            P(("group", "dp"), None),
            P(("group", "dp"), None),
            P(),
            P(),
            P(),
            P(),
            P(("group", "dp")),
        ),
        out_specs=P(("group", "dp"), None),
        check_vma=False,
    )
```

```python
import functools

import jax
import jax.numpy as jnp
from jax import lax
from jax.experimental import pallas as pl
from jax.experimental.pallas import tpu as pltpu
from jax.sharding import PartitionSpec as P

LEN = 128
LANES = 128
PANEL = 8
HALF = 256
IN_FLIGHT = 5
HIGHEST = lax.Precision.HIGHEST
FRONT_VMEM_BYTES = 24 * 1024 * 1024
VMEM_BYTES = 8 * 1024 * 1024
NT = (((1,), (1,)), ((), ()))
TN = (((0,), (0,)), ((), ()))
NN = (((1,), (0,)), ((), ()))


def dot(a, b, dims, precision=HIGHEST):
    return lax.dot_general(a, b, dims, precision=precision, preferred_element_type=jnp.float32)


def places(order):
    shape = (order, 2 * order)
    lane = lax.broadcasted_iota(jnp.int32, shape, 1)
    return lax.broadcasted_iota(jnp.int32, shape, 0), lane % order


def front_kernel(
    total_tokens, sequences, width,
    ids, acts, grad_q, grad_k, grad_v, proj_in, proj_q, proj_k, proj_v,
    factors, grams, query,
    acts_v, gq_v, gk_v, gv_v, pi_v, pq_v, pk_v, pv_v, sem,
):
    tokens = acts.shape[0]
    rows = min(HALF, tokens)
    columns = acts.shape[1] // 2
    moves = [(proj_k, pk_v), (grad_k, gk_v), (proj_v, pv_v), (grad_v, gv_v)]
    for first in range(0, tokens, rows):
        for src, dst, table, table_v in ((acts, acts_v, proj_in, pi_v), (grad_q, gq_v, proj_q, pq_v)):
            if first == 0:
                moves.append((table, table_v))
            for k in range(2):
                box = pl.ds(first, rows), pl.ds(k * columns, columns)
                moves.append((src.at[box], dst.at[box]))
    copies = [pltpu.make_async_copy(src, dst, sem.at[i]) for i, (src, dst) in enumerate(moves)]
    for copy in copies[:IN_FLIGHT]:
        copy.start()
    waited = []

    def arrived(count):
        for _ in range(count):
            i = len(waited)
            copies[i].wait()
            if i + IN_FLIGHT < len(copies):
                copies[i + IN_FLIGHT].start()
            waited.append(i)

    arrived(2)
    coords_k = dot(gk_v[...], pk_v[...], NT, None)
    arrived(2)
    coords_v = dot(gv_v[...], pv_v[...], NT, None)
    total = None
    for first in range(0, tokens, rows):
        sides = []
        for data, table in ((acts_v, pi_v), (gq_v, pq_v)):
            if first == 0:
                arrived(1)
            side = None
            for k in range(2):
                arrived(1)
                cut = slice(k * columns, (k + 1) * columns)
                term = dot(data[first : first + rows, cut], table[:, cut], NT, None)
                side = term if side is None else side + term
            sides.append(side)
        for seq in range(first // LEN, (first + rows) // LEN):
            here = slice(seq * LEN - first, (seq + 1) * LEN - first)
            whole = slice(seq * LEN, (seq + 1) * LEN)
            coords = jnp.concatenate([x[here] for x in sides] + [coords_k[whole], coords_v[whole]], axis=1)
            gram = dot(coords, coords, TN)
            grams[seq] = gram[:width] * (1.0 / LEN)
            total = gram if total is None else total + gram
    half = width // 2

    def square(p):
        part = slice(p * width, (p + 1) * width)
        return total[part, part] * (1.0 / total_tokens)

    upper = jnp.concatenate([square(0), square(2)], axis=1)
    lower = jnp.concatenate([square(1), square(3)], axis=1)
    row, column = places(width)
    factors[:width] = jnp.where(column >= row, upper, lower)
    diagonal = jnp.sum(jnp.where(column == row, lower, 0.0), axis=0, keepdims=True)
    factors[width:] = jnp.broadcast_to(diagonal, (8, 2 * width))
    for q in range(query.shape[0]):
        chosen = grams[ids[q]]
        query[q, :width] = chosen[:, width : 3 * width]
        query[q, width:, :width] = chosen[:half, 3 * width :]
        query[q, width:, width:] = chosen[half:, 3 * width :]


def damped(packed):
    order = packed.shape[1] // 2
    half = order // 2
    square, diagonal = packed[:order], packed[order : order + 1]
    row, column = places(order)
    turned = square.T
    turned = jnp.concatenate([turned[:order], turned[order:]], axis=1)
    on_diagonal = column == row
    first = jnp.where(column >= row, square, turned)
    second = jnp.where(column < row, square, turned)
    first_diagonal = jnp.sum(jnp.where(on_diagonal, square, 0.0), axis=0, keepdims=True)
    shape = (LANES, LANES)
    same = (
        lax.broadcasted_iota(jnp.int32, shape, 0) // order
        == lax.broadcasted_iota(jnp.int32, shape, 1) // order
    )
    diagonals = jnp.concatenate([first_diagonal, diagonal], axis=0)
    diagonals = jnp.concatenate([diagonals] * 4, axis=0)
    damping = dot(diagonals, jnp.where(same, 0.1 / order, 0.0), NN)
    first = first + jnp.where(on_diagonal, damping[:1], 0.0)
    second = jnp.where(on_diagonal, diagonal + damping[1:2], second)
    is_low = column < half
    low = jnp.where(is_low, first, pltpu.roll(second, half, 1))
    high = jnp.where(is_low, pltpu.roll(first, LANES - half, 1), second)
    return low, high


def invert(low, high):
    order = low.shape[0]
    half = order // 2
    groups = order // 8
    state = [[x[8 * g : 8 * g + 8] for g in range(groups)] for x in (low, high)]
    lane = lax.broadcasted_iota(jnp.int32, (8, LANES), 1)
    row = lax.broadcasted_iota(jnp.int32, (8, LANES), 0)
    column_of_lane = lane % half
    first_lane = lane - column_of_lane
    for start in range(0, order, PANEL):
        h, first = start // half, start % half
        spread = [
            [jnp.take_along_axis(state[h][g], first_lane + (first + j), axis=1) for g in range(groups)]
            for j in range(PANEL)
        ]
        in_panel = (column_of_lane >= first) & (column_of_lane < first + PANEL)
        state[h] = [jnp.where(in_panel, 0.0, x) for x in state[h]]
        for j in range(PANEL):
            k = start + j
            g, r = k // 8, k % 8
            column = spread[j]
            pivot = 1.0 / column[g][r : r + 1]
            for t in range(2):
                values = state[t][g][r : r + 1]
                if t == h:
                    values = jnp.where(column_of_lane[:1] == first + j, 1.0, values)
                values = values * pivot
                state[t] = [x - c * values for x, c in zip(state[t], column)]
                state[t][g] = jnp.where(row == r, values, state[t][g])
            for i in range(j + 1, PANEL):
                values = spread[i][g][r : r + 1] * pivot
                spread[i] = [x - c * values for x, c in zip(spread[i], column)]
                spread[i][g] = jnp.where(row == r, values, spread[i][g])
    return [jnp.concatenate(state[h], axis=0) for h in range(2)]


def invert_kernel(sequences, width, first, second, grams, train, side_v, left_v):
    half = width // 2
    low, high = invert(*damped(first[...] + second[...]))
    inverse_in = jnp.concatenate([low[:, :half], high[:, :half]], axis=1)
    side_v[...] = jnp.zeros_like(side_v)
    for p in range(3):
        rows = slice((p + 1) * width, (p + 2) * width)
        lanes = slice((p + 1) * half, (p + 2) * half)
        side_v[rows, p * width : p * width + half] = low[:, lanes]
        side_v[rows, p * width + half : (p + 1) * width] = high[:, lanes]
    left_v[...] = dot(grams[...].reshape(sequences * width, 4 * width), side_v[...], NN)
    for s in range(sequences):
        done = dot(inverse_in, left_v[pl.ds(s * width, width)], NN)
        train[s, :width] = done[:, : 2 * width]
        train[s, width:, :width] = done[:half, 2 * width :]
        train[s, width:, width:] = done[half:, 2 * width :]


def score_kernel(offsets, sequences, width, queries, train, *refs):
    blocks, out, partial_v = refs[:-2], refs[-2], refs[-1]
    me = lax.axis_index("dp")
    slot = 0
    for block in blocks:
        for i in range(block.shape[0]):
            value = block[i]
            for s in range(sequences):
                product = (train[s] * value).reshape(-1, 8, 2 * width)
                partial_v[s, pl.ds(slot * 8, 8)] = jnp.sum(product, axis=0)
            slot += 1
    own = queries // lax.axis_size("dp")
    shape = (queries, queries * 8)
    target = lax.broadcasted_iota(jnp.int32, shape, 0)
    source = lax.broadcasted_iota(jnp.int32, shape, 1) // 8
    offset = offsets(source // own)
    select = jnp.where(target == (offset ^ me) * own + source % own, 1.0, 0.0)
    ones = jnp.ones((8, 2 * width), jnp.float32)
    for s in range(sequences):
        by_query = dot(select, partial_v[s], NN)
        out[pl.ds(s, 1)] = dot(ones, by_query, NT)[:1]


def exchange(x, devices, distance):
    return lax.ppermute(x, "dp", [(i, i ^ distance) for i in range(devices)])


def reversed_bits(count, slot):
    out = jnp.zeros_like(slot)
    for j in range(count):
        out = out + (slot >> j & 1) * (1 << (count - 1 - j))
    return out


def per_device(acts, grad_q, grad_k, grad_v, proj_in, proj_q, proj_k, proj_v, query_ids):
    devices = lax.axis_size("dp")
    steps = devices.bit_length() - 1
    tokens, width = acts.shape[0], proj_in.shape[0]
    sequences, own_queries = tokens // LEN, query_ids.shape[0]
    queries = own_queries * devices
    f32 = jnp.float32
    in_vmem = pl.BlockSpec(memory_space=pltpu.VMEM)
    in_hbm = pl.BlockSpec(memory_space=pltpu.HBM)
    params = pltpu.CompilerParams(vmem_limit_bytes=VMEM_BYTES)
    tables = tuple(
        pltpu.with_memory_space_constraint(t, pltpu.HBM)
        for t in (acts, grad_q, grad_k, grad_v, proj_in, proj_q, proj_k, proj_v)
    )

    factors, grams, query = pl.pallas_call(
        functools.partial(front_kernel, tokens * devices, sequences, width),
        out_shape=(
            jax.ShapeDtypeStruct((width + 8, 2 * width), f32),
            jax.ShapeDtypeStruct((sequences, width, 4 * width), f32),
            jax.ShapeDtypeStruct((own_queries, 3 * width // 2, 2 * width), f32),
        ),
        in_specs=[pl.BlockSpec(memory_space=pltpu.SMEM)] + [in_hbm] * 8,
        out_specs=(in_vmem,) * 3,
        scratch_shapes=[pltpu.VMEM(t.shape, t.dtype) for t in tables]
        + [pltpu.SemaphoreType.DMA((6 + 4 * -(-tokens // HALF),))],
        compiler_params=pltpu.CompilerParams(vmem_limit_bytes=FRONT_VMEM_BYTES),
        name="front",
    )(query_ids, *tables)

    blocks, terms, waiting = [query], (factors, None), None
    for step in range(steps):
        mine = terms[0] if terms[1] is None else terms[0] + terms[1]
        theirs = exchange(mine, devices, 1 << step)
        if waiting is not None:
            waiting, theirs = lax.optimization_barrier((waiting, theirs))
            blocks.append(waiting)
        sent = blocks[0] if step == 0 else jnp.concatenate(blocks, axis=0)
        waiting = exchange(sent, devices, 1 << (steps - 1 - step))
        terms = (mine, theirs)
    blocks.append(waiting)

    train = pl.pallas_call(
        functools.partial(invert_kernel, sequences, width),
        out_shape=jax.ShapeDtypeStruct((sequences, 3 * width // 2, 2 * width), f32),
        in_specs=[in_vmem] * 3,
        out_specs=in_vmem,
        scratch_shapes=[
            pltpu.VMEM((4 * width, 3 * width), f32),
            pltpu.VMEM((sequences * width, 3 * width), f32),
        ],
        compiler_params=params,
        name="invert",
    )(*terms, grams)

    return pl.pallas_call(
        functools.partial(
            score_kernel, functools.partial(reversed_bits, steps), sequences, width, queries
        ),
        out_shape=jax.ShapeDtypeStruct((sequences, queries), f32),
        in_specs=[in_vmem] * (1 + len(blocks)),
        out_specs=in_vmem,
        scratch_shapes=[pltpu.VMEM((sequences, queries * 8, 2 * width), f32)],
        compiler_params=params,
        name="scores",
    )(train, *blocks)


def solution(mesh):
    return jax.shard_map(
        per_device,
        mesh=mesh,
        in_specs=(
            P(("group", "dp"), None),
            P(("group", "dp"), None),
            P(("group", "dp"), None),
            P(("group", "dp"), None),
            P(),
            P(),
            P(),
            P(),
            P(("group", "dp")),
        ),
        out_specs=P(("group", "dp"), None),
        check_vma=False,
    )
```

```python
import functools

import jax
import jax.numpy as jnp
from jax import lax
from jax.experimental import pallas as pl
from jax.experimental.pallas import tpu as pltpu
from jax.sharding import PartitionSpec as P

LEN = 128
LANES = 128
PANEL = 8
HALF = 256
IN_FLIGHT = 5
HIGHEST = lax.Precision.HIGHEST
FRONT_VMEM_BYTES = 24 * 1024 * 1024
VMEM_BYTES = 8 * 1024 * 1024
NT = (((1,), (1,)), ((), ()))
TN = (((0,), (0,)), ((), ()))
NN = (((1,), (0,)), ((), ()))


def dot(a, b, dims, precision=HIGHEST):
    return lax.dot_general(a, b, dims, precision=precision, preferred_element_type=jnp.float32)


def places(order):
    shape = (order, 2 * order)
    lane = lax.broadcasted_iota(jnp.int32, shape, 1)
    return lax.broadcasted_iota(jnp.int32, shape, 0), lane % order


def front_kernel(
    total_tokens, sequences, width,
    ids, acts, grad_q, grad_k, grad_v, proj_in, proj_q, proj_k, proj_v,
    factors, grams, query,
    acts_v, gq_v, gk_v, gv_v, pi_v, pq_v, pk_v, pv_v, sem,
):
    tokens = acts.shape[0]
    rows = min(HALF, tokens)
    columns = acts.shape[1] // 2
    moves = [(proj_k, pk_v), (grad_k, gk_v), (proj_v, pv_v), (grad_v, gv_v)]
    for first in range(0, tokens, rows):
        for src, dst, table, table_v in ((acts, acts_v, proj_in, pi_v), (grad_q, gq_v, proj_q, pq_v)):
            if first == 0:
                moves.append((table, table_v))
            for k in range(2):
                box = pl.ds(first, rows), pl.ds(k * columns, columns)
                moves.append((src.at[box], dst.at[box]))
    copies = [pltpu.make_async_copy(src, dst, sem.at[i]) for i, (src, dst) in enumerate(moves)]
    for copy in copies[:IN_FLIGHT]:
        copy.start()
    waited = []

    def arrived(count):
        for _ in range(count):
            i = len(waited)
            copies[i].wait()
            if i + IN_FLIGHT < len(copies):
                copies[i + IN_FLIGHT].start()
            waited.append(i)

    arrived(2)
    coords_k = dot(gk_v[...], pk_v[...], NT, None)
    arrived(2)
    coords_v = dot(gv_v[...], pv_v[...], NT, None)
    total = None
    for first in range(0, tokens, rows):
        sides = []
        for data, table in ((acts_v, pi_v), (gq_v, pq_v)):
            if first == 0:
                arrived(1)
            side = None
            for k in range(2):
                arrived(1)
                cut = slice(k * columns, (k + 1) * columns)
                term = dot(data[first : first + rows, cut], table[:, cut], NT, None)
                side = term if side is None else side + term
            sides.append(side)
        for seq in range(first // LEN, (first + rows) // LEN):
            here = slice(seq * LEN - first, (seq + 1) * LEN - first)
            whole = slice(seq * LEN, (seq + 1) * LEN)
            coords = jnp.concatenate([x[here] for x in sides] + [coords_k[whole], coords_v[whole]], axis=1)
            high = coords.astype(jnp.bfloat16)
            low = (coords - high.astype(jnp.float32)).astype(jnp.bfloat16)
            left = jnp.concatenate([high, low, high], axis=0)
            right = jnp.concatenate([high, high, low], axis=0)
            gram = dot(left, right, TN, None)
            grams[seq] = gram[:width] * (1.0 / LEN)
            total = gram if total is None else total + gram
    half = width // 2

    def square(p):
        part = slice(p * width, (p + 1) * width)
        return total[part, part] * (1.0 / total_tokens)

    upper = jnp.concatenate([square(0), square(2)], axis=1)
    lower = jnp.concatenate([square(1), square(3)], axis=1)
    row, column = places(width)
    factors[:width] = jnp.where(column >= row, upper, lower)
    diagonal = jnp.sum(jnp.where(column == row, lower, 0.0), axis=0, keepdims=True)
    factors[width:] = jnp.broadcast_to(diagonal, (8, 2 * width))
    for q in range(query.shape[0]):
        chosen = grams[ids[q]]
        query[q, :width] = chosen[:, width : 3 * width]
        query[q, width:, :width] = chosen[:half, 3 * width :]
        query[q, width:, width:] = chosen[half:, 3 * width :]


def damped(packed):
    order = packed.shape[1] // 2
    half = order // 2
    square, diagonal = packed[:order], packed[order : order + 1]
    row, column = places(order)
    turned = square.T
    turned = jnp.concatenate([turned[:order], turned[order:]], axis=1)
    on_diagonal = column == row
    first = jnp.where(column >= row, square, turned)
    second = jnp.where(column < row, square, turned)
    first_diagonal = jnp.sum(jnp.where(on_diagonal, square, 0.0), axis=0, keepdims=True)
    shape = (LANES, LANES)
    same = (
        lax.broadcasted_iota(jnp.int32, shape, 0) // order
        == lax.broadcasted_iota(jnp.int32, shape, 1) // order
    )
    diagonals = jnp.concatenate([first_diagonal, diagonal], axis=0)
    diagonals = jnp.concatenate([diagonals] * 4, axis=0)
    damping = dot(diagonals, jnp.where(same, 0.1 / order, 0.0), NN)
    first = first + jnp.where(on_diagonal, damping[:1], 0.0)
    second = jnp.where(on_diagonal, diagonal + damping[1:2], second)
    is_low = column < half
    low = jnp.where(is_low, first, pltpu.roll(second, half, 1))
    high = jnp.where(is_low, pltpu.roll(first, LANES - half, 1), second)
    return low, high


def invert(low, high):
    order = low.shape[0]
    half = order // 2
    groups = order // 8
    state = [[x[8 * g : 8 * g + 8] for g in range(groups)] for x in (low, high)]
    lane = lax.broadcasted_iota(jnp.int32, (8, LANES), 1)
    row = lax.broadcasted_iota(jnp.int32, (8, LANES), 0)
    column_of_lane = lane % half
    first_lane = lane - column_of_lane
    for start in range(0, order, PANEL):
        h, first = start // half, start % half
        spread = [
            [jnp.take_along_axis(state[h][g], first_lane + (first + j), axis=1) for g in range(groups)]
            for j in range(PANEL)
        ]
        in_panel = (column_of_lane >= first) & (column_of_lane < first + PANEL)
        state[h] = [jnp.where(in_panel, 0.0, x) for x in state[h]]
        for j in range(PANEL):
            k = start + j
            g, r = k // 8, k % 8
            column = spread[j]
            pivot = 1.0 / column[g][r : r + 1]
            for t in range(2):
                values = state[t][g][r : r + 1]
                if t == h:
                    values = jnp.where(column_of_lane[:1] == first + j, 1.0, values)
                values = values * pivot
                state[t] = [x - c * values for x, c in zip(state[t], column)]
                state[t][g] = jnp.where(row == r, values, state[t][g])
            for i in range(j + 1, PANEL):
                values = spread[i][g][r : r + 1] * pivot
                spread[i] = [x - c * values for x, c in zip(spread[i], column)]
                spread[i][g] = jnp.where(row == r, values, spread[i][g])
    return [jnp.concatenate(state[h], axis=0) for h in range(2)]


def invert_kernel(sequences, width, first, second, grams, train, side_v, left_v):
    half = width // 2
    low, high = invert(*damped(first[...] + second[...]))
    inverse_in = jnp.concatenate([low[:, :half], high[:, :half]], axis=1)
    side_v[...] = jnp.zeros_like(side_v)
    for p in range(3):
        rows = slice((p + 1) * width, (p + 2) * width)
        lanes = slice((p + 1) * half, (p + 2) * half)
        side_v[rows, p * width : p * width + half] = low[:, lanes]
        side_v[rows, p * width + half : (p + 1) * width] = high[:, lanes]
    left_v[...] = dot(grams[...].reshape(sequences * width, 4 * width), side_v[...], NN)
    for s in range(sequences):
        done = dot(inverse_in, left_v[pl.ds(s * width, width)], NN)
        train[s, :width] = done[:, : 2 * width]
        train[s, width:, :width] = done[:half, 2 * width :]
        train[s, width:, width:] = done[half:, 2 * width :]


def score_kernel(offsets, sequences, width, queries, train, *refs):
    blocks, out, partial_v = refs[:-2], refs[-2], refs[-1]
    me = lax.axis_index("dp")
    slot = 0
    for block in blocks:
        for i in range(block.shape[0]):
            value = block[i]
            for s in range(sequences):
                product = (train[s] * value).reshape(-1, 8, 2 * width)
                partial_v[s, pl.ds(slot * 8, 8)] = jnp.sum(product, axis=0)
            slot += 1
    own = queries // lax.axis_size("dp")
    shape = (queries, queries * 8)
    target = lax.broadcasted_iota(jnp.int32, shape, 0)
    source = lax.broadcasted_iota(jnp.int32, shape, 1) // 8
    offset = offsets(source // own)
    select = jnp.where(target == (offset ^ me) * own + source % own, 1.0, 0.0)
    ones = jnp.ones((8, 2 * width), jnp.float32)
    for s in range(sequences):
        by_query = dot(select, partial_v[s], NN)
        out[pl.ds(s, 1)] = dot(ones, by_query, NT)[:1]


def exchange(x, devices, distance):
    return lax.ppermute(x, "dp", [(i, i ^ distance) for i in range(devices)])


def reversed_bits(count, slot):
    out = jnp.zeros_like(slot)
    for j in range(count):
        out = out + (slot >> j & 1) * (1 << (count - 1 - j))
    return out


def per_device(acts, grad_q, grad_k, grad_v, proj_in, proj_q, proj_k, proj_v, query_ids):
    devices = lax.axis_size("dp")
    steps = devices.bit_length() - 1
    tokens, width = acts.shape[0], proj_in.shape[0]
    sequences, own_queries = tokens // LEN, query_ids.shape[0]
    queries = own_queries * devices
    f32 = jnp.float32
    in_vmem = pl.BlockSpec(memory_space=pltpu.VMEM)
    in_hbm = pl.BlockSpec(memory_space=pltpu.HBM)
    params = pltpu.CompilerParams(vmem_limit_bytes=VMEM_BYTES)
    tables = tuple(
        pltpu.with_memory_space_constraint(t, pltpu.HBM)
        for t in (acts, grad_q, grad_k, grad_v, proj_in, proj_q, proj_k, proj_v)
    )

    factors, grams, query = pl.pallas_call(
        functools.partial(front_kernel, tokens * devices, sequences, width),
        out_shape=(
            jax.ShapeDtypeStruct((width + 8, 2 * width), f32),
            jax.ShapeDtypeStruct((sequences, width, 4 * width), f32),
            jax.ShapeDtypeStruct((own_queries, 3 * width // 2, 2 * width), f32),
        ),
        in_specs=[pl.BlockSpec(memory_space=pltpu.SMEM)] + [in_hbm] * 8,
        out_specs=(in_vmem,) * 3,
        scratch_shapes=[pltpu.VMEM(t.shape, t.dtype) for t in tables]
        + [pltpu.SemaphoreType.DMA((6 + 4 * -(-tokens // HALF),))],
        compiler_params=pltpu.CompilerParams(vmem_limit_bytes=FRONT_VMEM_BYTES),
        name="front",
    )(query_ids, *tables)

    factor_bits = list(range(steps))
    if steps > 2:
        factor_bits[1], factor_bits[2] = 2, 1
    query_bits = list(range(steps))[::-1]
    opens = {0: min(1, steps - 1), 1: steps - 1}
    blocks, waiting = [query], None

    def send_query():
        sent = blocks[0] if len(blocks) == 1 else jnp.concatenate(blocks, axis=0)
        return exchange(sent, devices, 1 << query_bits.pop(0))

    mine = factors
    for step in range(steps):
        theirs = exchange(mine, devices, 1 << factor_bits[step])
        if step == 0:
            waiting = send_query()
        elif step in (opens[0], opens[1]) and query_bits:
            waiting, theirs = lax.optimization_barrier((waiting, theirs))
            blocks.append(waiting)
            waiting = send_query()
        if step < steps - 1:
            mine = mine + theirs
    terms = (mine, theirs)

    train = pl.pallas_call(
        functools.partial(invert_kernel, sequences, width),
        out_shape=jax.ShapeDtypeStruct((sequences, 3 * width // 2, 2 * width), f32),
        in_specs=[in_vmem] * 3,
        out_specs=in_vmem,
        scratch_shapes=[
            pltpu.VMEM((4 * width, 3 * width), f32),
            pltpu.VMEM((sequences * width, 3 * width), f32),
        ],
        compiler_params=params,
        name="invert",
    )(*terms, grams)
    waiting, train = lax.optimization_barrier((waiting, train))
    blocks.append(waiting)
    while query_bits:
        blocks.append(send_query())

    return pl.pallas_call(
        functools.partial(
            score_kernel, functools.partial(reversed_bits, steps), sequences, width, queries
        ),
        out_shape=jax.ShapeDtypeStruct((sequences, queries), f32),
        in_specs=[in_vmem] * (1 + len(blocks)),
        out_specs=in_vmem,
        scratch_shapes=[pltpu.VMEM((sequences, queries * 8, 2 * width), f32)],
        compiler_params=params,
        name="scores",
    )(train, *blocks)


def solution(mesh):
    return jax.shard_map(
        per_device,
        mesh=mesh,
        in_specs=(
            P(("group", "dp"), None),
            P(("group", "dp"), None),
            P(("group", "dp"), None),
            P(("group", "dp"), None),
            P(),
            P(),
            P(),
            P(),
            P(("group", "dp")),
        ),
        out_specs=P(("group", "dp"), None),
        check_vma=False,
    )
```

```python
import functools

import jax
import jax.numpy as jnp
from jax import lax
from jax.experimental import pallas as pl
from jax.experimental.pallas import tpu as pltpu
from jax.sharding import PartitionSpec as P

LEN = 128
LANES = 128
PANEL = 8
HALF = 256
IN_FLIGHT = 5
HIGHEST = lax.Precision.HIGHEST
FRONT_VMEM_BYTES = 24 * 1024 * 1024
VMEM_BYTES = 8 * 1024 * 1024
NT = (((1,), (1,)), ((), ()))
TN = (((0,), (0,)), ((), ()))
NN = (((1,), (0,)), ((), ()))


def dot(a, b, dims, precision=HIGHEST):
    return lax.dot_general(a, b, dims, precision=precision, preferred_element_type=jnp.float32)


def front_kernel(
    total_tokens, sequences, width,
    ids, acts, grad_q, grad_k, grad_v, proj_in, proj_q, proj_k, proj_v,
    factors, grams, query,
    acts_v, gq_v, gk_v, gv_v, pi_v, pq_v, pk_v, pv_v, sem,
):
    tokens = acts.shape[0]
    rows = min(HALF, tokens)
    columns = acts.shape[1] // 2
    moves = [(proj_k, pk_v), (grad_k, gk_v), (proj_v, pv_v), (grad_v, gv_v)]
    for first in range(0, tokens, rows):
        for src, dst, table, table_v in ((acts, acts_v, proj_in, pi_v), (grad_q, gq_v, proj_q, pq_v)):
            if first == 0:
                moves.append((table, table_v))
            for k in range(2):
                box = pl.ds(first, rows), pl.ds(k * columns, columns)
                moves.append((src.at[box], dst.at[box]))
    copies = [pltpu.make_async_copy(src, dst, sem.at[i]) for i, (src, dst) in enumerate(moves)]
    for copy in copies[:IN_FLIGHT]:
        copy.start()
    waited = []

    def arrived(count):
        for _ in range(count):
            i = len(waited)
            copies[i].wait()
            if i + IN_FLIGHT < len(copies):
                copies[i + IN_FLIGHT].start()
            waited.append(i)

    arrived(2)
    coords_k = dot(gk_v[...], pk_v[...], NT, None)
    arrived(2)
    coords_v = dot(gv_v[...], pv_v[...], NT, None)
    total = None
    for first in range(0, tokens, rows):
        sides = []
        for data, table in ((acts_v, pi_v), (gq_v, pq_v)):
            if first == 0:
                arrived(1)
            side = None
            for k in range(2):
                arrived(1)
                cut = slice(k * columns, (k + 1) * columns)
                term = dot(data[first : first + rows, cut], table[:, cut], NT, None)
                side = term if side is None else side + term
            sides.append(side)
        for seq in range(first // LEN, (first + rows) // LEN):
            here = slice(seq * LEN - first, (seq + 1) * LEN - first)
            whole = slice(seq * LEN, (seq + 1) * LEN)
            coords = jnp.concatenate([x[here] for x in sides] + [coords_k[whole], coords_v[whole]], axis=1)
            high = coords.astype(jnp.bfloat16)
            low = (coords - high.astype(jnp.float32)).astype(jnp.bfloat16)
            left = jnp.concatenate([high, low, high], axis=0)
            right = jnp.concatenate([high, high, low], axis=0)
            gram = dot(left, right, TN, None)
            grams[seq] = gram[:width] * (1.0 / LEN)
            total = gram if total is None else total + gram
    half = width // 2

    for p in range(4):
        part = slice(p * width, (p + 1) * width)
        block = total[part, part] * (1.0 / total_tokens)
        lanes = slice(p * half, (p + 1) * half)
        factors[:width, lanes] = block[:, :half]
        factors[width:, lanes] = block[:, half:]
    for q in range(query.shape[0]):
        chosen = grams[ids[q]]
        query[q, :width] = chosen[:, width : 3 * width]
        query[q, width:, :width] = chosen[:half, 3 * width :]
        query[q, width:, width:] = chosen[half:, 3 * width :]


def damped(factors):
    order = factors.shape[0] // 2
    half = order // 2
    row = lax.broadcasted_iota(jnp.int32, factors.shape, 0)
    lane = lax.broadcasted_iota(jnp.int32, factors.shape, 1)
    on_diagonal = row == lane % half + jnp.where(row < order, 0, order + half)
    column_sums = jnp.sum(jnp.where(on_diagonal, factors, 0.0), axis=0, keepdims=True)
    shape = (LANES, LANES)
    same = (
        lax.broadcasted_iota(jnp.int32, shape, 0) // half
        == lax.broadcasted_iota(jnp.int32, shape, 1) // half
    )
    damping = dot(jnp.broadcast_to(column_sums, (8, LANES)), jnp.where(same, 0.1 / order, 0.0), NN)[:1]
    factors = factors + jnp.where(on_diagonal, damping, 0.0)
    return factors[:order], factors[order:]


def invert(low, high):
    order = low.shape[0]
    half = order // 2
    groups = order // 8
    state = [[x[8 * g : 8 * g + 8] for g in range(groups)] for x in (low, high)]
    lane = lax.broadcasted_iota(jnp.int32, (8, LANES), 1)
    row = lax.broadcasted_iota(jnp.int32, (8, LANES), 0)
    column_of_lane = lane % half
    first_lane = lane - column_of_lane
    for start in range(0, order, PANEL):
        h, first = start // half, start % half
        spread = [
            [jnp.take_along_axis(state[h][g], first_lane + (first + j), axis=1) for g in range(groups)]
            for j in range(PANEL)
        ]
        in_panel = (column_of_lane >= first) & (column_of_lane < first + PANEL)
        state[h] = [jnp.where(in_panel, 0.0, x) for x in state[h]]
        for j in range(PANEL):
            k = start + j
            g, r = k // 8, k % 8
            column = spread[j]
            pivot = 1.0 / column[g][r : r + 1]
            for t in range(2):
                values = state[t][g][r : r + 1]
                if t == h:
                    values = jnp.where(column_of_lane[:1] == first + j, 1.0, values)
                values = values * pivot
                state[t] = [x - c * values for x, c in zip(state[t], column)]
                state[t][g] = jnp.where(row == r, values, state[t][g])
            for i in range(j + 1, PANEL):
                values = spread[i][g][r : r + 1] * pivot
                spread[i] = [x - c * values for x, c in zip(spread[i], column)]
                spread[i][g] = jnp.where(row == r, values, spread[i][g])
    return [jnp.concatenate(state[h], axis=0) for h in range(2)]


def invert_kernel(sequences, width, factors, grams, train, side_v, left_v):
    half = width // 2
    low, high = invert(*damped(factors[...]))
    inverse_in = jnp.concatenate([low[:, :half], high[:, :half]], axis=1)
    side_v[...] = jnp.zeros_like(side_v)
    for p in range(3):
        rows = slice((p + 1) * width, (p + 2) * width)
        lanes = slice((p + 1) * half, (p + 2) * half)
        side_v[rows, p * width : p * width + half] = low[:, lanes]
        side_v[rows, p * width + half : (p + 1) * width] = high[:, lanes]
    left_v[...] = dot(grams[...].reshape(sequences * width, 4 * width), side_v[...], NN)
    for s in range(sequences):
        done = dot(inverse_in, left_v[pl.ds(s * width, width)], NN)
        train[s, :width] = done[:, : 2 * width]
        train[s, width:, :width] = done[:half, 2 * width :]
        train[s, width:, width:] = done[half:, 2 * width :]


def score_kernel(offsets, sequences, width, queries, train, *refs):
    blocks, out, partial_v = refs[:-2], refs[-2], refs[-1]
    me = lax.axis_index("dp")
    slot = 0
    for block in blocks:
        for i in range(block.shape[0]):
            value = block[i]
            for s in range(sequences):
                product = (train[s] * value).reshape(-1, 8, 2 * width)
                partial_v[s, pl.ds(slot * 8, 8)] = jnp.sum(product, axis=0)
            slot += 1
    own = queries // lax.axis_size("dp")
    shape = (queries, queries * 8)
    target = lax.broadcasted_iota(jnp.int32, shape, 0)
    source = lax.broadcasted_iota(jnp.int32, shape, 1) // 8
    offset = offsets(source // own)
    select = jnp.where(target == (offset ^ me) * own + source % own, 1.0, 0.0)
    ones = jnp.ones((8, 2 * width), jnp.float32)
    for s in range(sequences):
        by_query = dot(select, partial_v[s], NN)
        out[pl.ds(s, 1)] = dot(ones, by_query, NT)[:1]


def exchange(x, devices, distance):
    return lax.ppermute(x, "dp", [(i, i ^ distance) for i in range(devices)])


def reversed_bits(count, slot):
    out = jnp.zeros_like(slot)
    for j in range(count):
        out = out + (slot >> j & 1) * (1 << (count - 1 - j))
    return out


def per_device(acts, grad_q, grad_k, grad_v, proj_in, proj_q, proj_k, proj_v, query_ids):
    devices = lax.axis_size("dp")
    steps = devices.bit_length() - 1
    tokens, width = acts.shape[0], proj_in.shape[0]
    sequences, own_queries = tokens // LEN, query_ids.shape[0]
    queries = own_queries * devices
    f32 = jnp.float32
    in_vmem = pl.BlockSpec(memory_space=pltpu.VMEM)
    in_hbm = pl.BlockSpec(memory_space=pltpu.HBM)
    params = pltpu.CompilerParams(vmem_limit_bytes=VMEM_BYTES)
    tables = tuple(
        pltpu.with_memory_space_constraint(t, pltpu.HBM)
        for t in (acts, grad_q, grad_k, grad_v, proj_in, proj_q, proj_k, proj_v)
    )

    factors, grams, query = pl.pallas_call(
        functools.partial(front_kernel, tokens * devices, sequences, width),
        out_shape=(
            jax.ShapeDtypeStruct((2 * width, 2 * width), f32),
            jax.ShapeDtypeStruct((sequences, width, 4 * width), f32),
            jax.ShapeDtypeStruct((own_queries, 3 * width // 2, 2 * width), f32),
        ),
        in_specs=[pl.BlockSpec(memory_space=pltpu.SMEM)] + [in_hbm] * 8,
        out_specs=(in_vmem,) * 3,
        scratch_shapes=[pltpu.VMEM(t.shape, t.dtype) for t in tables]
        + [pltpu.SemaphoreType.DMA((6 + 4 * -(-tokens // HALF),))],
        compiler_params=pltpu.CompilerParams(vmem_limit_bytes=FRONT_VMEM_BYTES),
        name="front",
    )(query_ids, *tables)

    query_bits = list(range(steps))[::-1]
    blocks = [query]

    def send_query():
        sent = blocks[0] if len(blocks) == 1 else jnp.concatenate(blocks, axis=0)
        return exchange(sent, devices, 1 << query_bits.pop(0))

    waiting = send_query()
    chunks = factors.reshape(devices, 2 * width // devices, 2 * width)
    received = lax.all_to_all(chunks, "dp", 0, 0)
    waiting, received = lax.optimization_barrier((waiting, received))
    blocks.append(waiting)
    waiting = send_query()
    mine = jnp.broadcast_to(jnp.sum(received, axis=0, keepdims=True), chunks.shape)
    gathered = lax.all_to_all(mine, "dp", 0, 0)
    waiting, gathered = lax.optimization_barrier((waiting, gathered))
    blocks.append(waiting)
    waiting = send_query()
    factors = gathered.reshape(2 * width, 2 * width)

    train = pl.pallas_call(
        functools.partial(invert_kernel, sequences, width),
        out_shape=jax.ShapeDtypeStruct((sequences, 3 * width // 2, 2 * width), f32),
        in_specs=[in_vmem] * 2,
        out_specs=in_vmem,
        scratch_shapes=[
            pltpu.VMEM((4 * width, 3 * width), f32),
            pltpu.VMEM((sequences * width, 3 * width), f32),
        ],
        compiler_params=params,
        name="invert",
    )(factors, grams)
    waiting, train = lax.optimization_barrier((waiting, train))
    blocks.append(waiting)
    while query_bits:
        blocks.append(send_query())

    return pl.pallas_call(
        functools.partial(
            score_kernel, functools.partial(reversed_bits, steps), sequences, width, queries
        ),
        out_shape=jax.ShapeDtypeStruct((sequences, queries), f32),
        in_specs=[in_vmem] * (1 + len(blocks)),
        out_specs=in_vmem,
        scratch_shapes=[pltpu.VMEM((sequences, queries * 8, 2 * width), f32)],
        compiler_params=params,
        name="scores",
    )(train, *blocks)


def solution(mesh):
    return jax.shard_map(
        per_device,
        mesh=mesh,
        in_specs=(
            P(("group", "dp"), None),
            P(("group", "dp"), None),
            P(("group", "dp"), None),
            P(("group", "dp"), None),
            P(),
            P(),
            P(),
            P(),
            P(("group", "dp")),
        ),
        out_specs=P(("group", "dp"), None),
        check_vma=False,
    )
```

```python
import functools

import jax
import jax.numpy as jnp
from jax import lax
from jax.experimental import pallas as pl
from jax.experimental.pallas import tpu as pltpu
from jax.sharding import PartitionSpec as P

LEN = 128
LANES = 128
PANEL = 8
HALF = 256
IN_FLIGHT = 5
OPENS = (1, 2)
HIGHEST = lax.Precision.HIGHEST
FRONT_VMEM_BYTES = 24 * 1024 * 1024
VMEM_BYTES = 8 * 1024 * 1024
NT = (((1,), (1,)), ((), ()))
TN = (((0,), (0,)), ((), ()))
NN = (((1,), (0,)), ((), ()))


def dot(a, b, dims, precision=HIGHEST):
    return lax.dot_general(a, b, dims, precision=precision, preferred_element_type=jnp.float32)


def places(order):
    shape = (order, 2 * order)
    lane = lax.broadcasted_iota(jnp.int32, shape, 1)
    return lax.broadcasted_iota(jnp.int32, shape, 0), lane % order


def front_kernel(
    total_tokens, sequences, width,
    ids, acts, grad_q, grad_k, grad_v, proj_in, proj_q, proj_k, proj_v,
    factors, grams, query,
    acts_v, gq_v, gk_v, gv_v, pi_v, pq_v, pk_v, pv_v, sem,
):
    tokens = acts.shape[0]
    rows = min(HALF, tokens)
    columns = acts.shape[1] // 2
    moves = [(proj_k, pk_v), (grad_k, gk_v), (proj_v, pv_v), (grad_v, gv_v)]
    for first in range(0, tokens, rows):
        for src, dst, table, table_v in ((acts, acts_v, proj_in, pi_v), (grad_q, gq_v, proj_q, pq_v)):
            if first == 0:
                moves.append((table, table_v))
            for k in range(2):
                box = pl.ds(first, rows), pl.ds(k * columns, columns)
                moves.append((src.at[box], dst.at[box]))
    copies = [pltpu.make_async_copy(src, dst, sem.at[i]) for i, (src, dst) in enumerate(moves)]
    for copy in copies[:IN_FLIGHT]:
        copy.start()
    waited = []

    def arrived(count):
        for _ in range(count):
            i = len(waited)
            copies[i].wait()
            if i + IN_FLIGHT < len(copies):
                copies[i + IN_FLIGHT].start()
            waited.append(i)

    arrived(2)
    coords_k = dot(pk_v[...], gk_v[...], NT, None)
    arrived(2)
    coords_v = dot(pv_v[...], gv_v[...], NT, None)
    left = lax.broadcasted_iota(jnp.int32, (width, 2 * width), 1) < width
    upper = lower = None
    for first in range(0, tokens, rows):
        sides = []
        for data, table in ((acts_v, pi_v), (gq_v, pq_v)):
            if first == 0:
                arrived(1)
            side = None
            for k in range(2):
                arrived(1)
                cut = slice(k * columns, (k + 1) * columns)
                term = dot(table[:, cut], data[first : first + rows, cut], NT, None)
                side = term if side is None else side + term
            sides.append(side)
        whole = slice(first, first + rows)
        coords = jnp.concatenate(sides + [coords_k[:, whole], coords_v[:, whole]], axis=0)
        high = coords.astype(jnp.bfloat16)
        low = (coords - high.astype(jnp.float32)).astype(jnp.bfloat16)
        for seq in range(rows // LEN):
            here = slice(seq * LEN, (seq + 1) * LEN)
            one = jnp.concatenate([high[:, here], low[:, here], high[:, here]], axis=1)
            other = jnp.concatenate([high[:, here], high[:, here], low[:, here]], axis=1)
            gram = dot(one, other, NT, None)
            grams[first // LEN + seq] = gram[:width] * (1.0 / LEN)
            squares = [gram[p * width : (p + 1) * width, p // 2 * 2 * width : (p // 2 + 1) * 2 * width] for p in range(4)]
            in_q = jnp.where(left, squares[0], squares[1])
            k_v = jnp.where(left, squares[2], squares[3])
            upper = in_q if upper is None else upper + in_q
            lower = k_v if lower is None else lower + k_v
    row, column = places(width)
    scale = 1.0 / total_tokens
    factors[:width] = jnp.where(column >= row, upper, lower) * scale
    diagonal = jnp.sum(jnp.where(column == row, lower, 0.0), axis=0, keepdims=True) * scale
    factors[width:] = jnp.broadcast_to(diagonal, (8, 2 * width))
    half = width // 2
    for q in range(query.shape[0]):
        chosen = grams[ids[q]]
        query[q, :width] = chosen[:, 2 * width :]
        in_q = chosen[:, : 2 * width]
        query[q, width:] = jnp.where(left[:half], pltpu.roll(in_q[:half], width, 1), in_q[half:])


def damped(packed):
    order = packed.shape[1] // 2
    half = order // 2
    square, diagonal = packed[:order], packed[order : order + 1]
    row, column = places(order)
    turned = square.T
    turned = jnp.concatenate([turned[:order], turned[order:]], axis=1)
    on_diagonal = column == row
    first = jnp.where(column >= row, square, turned)
    second = jnp.where(column < row, square, turned)
    first_diagonal = jnp.sum(jnp.where(on_diagonal, square, 0.0), axis=0, keepdims=True)
    shape = (LANES, LANES)
    same = (
        lax.broadcasted_iota(jnp.int32, shape, 0) // order
        == lax.broadcasted_iota(jnp.int32, shape, 1) // order
    )
    diagonals = jnp.concatenate([first_diagonal, diagonal], axis=0)
    diagonals = jnp.concatenate([diagonals] * 4, axis=0)
    damping = dot(diagonals, jnp.where(same, 0.1 / order, 0.0), NN)
    first = first + jnp.where(on_diagonal, damping[:1], 0.0)
    second = jnp.where(on_diagonal, diagonal + damping[1:2], second)
    is_low = column < half
    low = jnp.where(is_low, first, pltpu.roll(second, half, 1))
    high = jnp.where(is_low, pltpu.roll(first, LANES - half, 1), second)
    return low, high


def invert(low, high):
    order = low.shape[0]
    half = order // 2
    groups = order // 8
    state = [[x[8 * g : 8 * g + 8] for g in range(groups)] for x in (low, high)]
    lane = lax.broadcasted_iota(jnp.int32, (8, LANES), 1)
    row = lax.broadcasted_iota(jnp.int32, (8, LANES), 0)
    column_of_lane = lane % half
    first_lane = lane - column_of_lane
    for start in range(0, order, PANEL):
        h, first = start // half, start % half
        spread = [
            [jnp.take_along_axis(state[h][g], first_lane + (first + j), axis=1) for g in range(groups)]
            for j in range(PANEL)
        ]
        in_panel = (column_of_lane >= first) & (column_of_lane < first + PANEL)
        state[h] = [jnp.where(in_panel, 0.0, x) for x in state[h]]
        for j in range(PANEL):
            k = start + j
            g, r = k // 8, k % 8
            column = spread[j]
            pivot = 1.0 / column[g][r : r + 1]
            for t in range(2):
                values = state[t][g][r : r + 1]
                if t == h:
                    values = jnp.where(column_of_lane[:1] == first + j, 1.0, values)
                values = values * pivot
                state[t] = [x - c * values for x, c in zip(state[t], column)]
                state[t][g] = jnp.where(row == r, values, state[t][g])
            for i in range(j + 1, PANEL):
                values = spread[i][g][r : r + 1] * pivot
                spread[i] = [x - c * values for x, c in zip(spread[i], column)]
                spread[i][g] = jnp.where(row == r, values, spread[i][g])
    return [jnp.concatenate(state[h], axis=0) for h in range(2)]


def invert_kernel(sequences, width, first, second, grams, train, side_v, left_v):
    half = width // 2
    low, high = invert(*damped(first[...] + second[...]))
    by_lanes = [
        jnp.concatenate([low[:, p * half : (p + 1) * half], high[:, p * half : (p + 1) * half]], axis=1)
        for p in range(4)
    ]
    inverse_in, inverse_k, inverse_q, inverse_v = by_lanes
    side_v[...] = jnp.zeros_like(side_v)
    side_v[width : 2 * width, 2 * width : 3 * width] = inverse_q
    side_v[width : 2 * width, 3 * width :] = inverse_q
    side_v[2 * width : 3 * width, :width] = inverse_k
    side_v[3 * width :, width : 2 * width] = inverse_v
    left_v[...] = dot(grams[...].reshape(sequences * width, 4 * width), side_v[...], NN)
    on_left = lax.broadcasted_iota(jnp.int32, (half, 2 * width), 1) < width
    for s in range(sequences):
        done = dot(inverse_in, left_v[pl.ds(s * width, width)], NN)
        train[s, :width] = done[:, : 2 * width]
        train[s, width:] = jnp.where(on_left, done[:half, 2 * width :], done[half:, 2 * width :])


def score_kernel(offsets, sequences, width, queries, train, *refs):
    blocks, out, partial_v = refs[:-2], refs[-2], refs[-1]
    me = lax.axis_index("dp")
    slot = 0
    for block in blocks:
        for i in range(block.shape[0]):
            value = block[i]
            for s in range(sequences):
                product = (train[s] * value).reshape(-1, 8, 2 * width)
                partial_v[s, pl.ds(slot * 8, 8)] = jnp.sum(product, axis=0)
            slot += 1
    own = queries // lax.axis_size("dp")
    shape = (queries, queries * 8)
    target = lax.broadcasted_iota(jnp.int32, shape, 0)
    source = lax.broadcasted_iota(jnp.int32, shape, 1) // 8
    offset = offsets(source // own)
    select = jnp.where(target == (offset ^ me) * own + source % own, 1.0, 0.0)
    ones = jnp.ones((8, 2 * width), jnp.float32)
    for s in range(sequences):
        by_query = dot(select, partial_v[s], NN)
        out[pl.ds(s, 1)] = dot(ones, by_query, NT)[:1]


def exchange(x, devices, distance):
    return lax.ppermute(x, "dp", [(i, i ^ distance) for i in range(devices)])


def reversed_bits(count, slot):
    out = jnp.zeros_like(slot)
    for j in range(count):
        out = out + (slot >> j & 1) * (1 << (count - 1 - j))
    return out


def per_device(acts, grad_q, grad_k, grad_v, proj_in, proj_q, proj_k, proj_v, query_ids):
    devices = lax.axis_size("dp")
    steps = devices.bit_length() - 1
    tokens, width = acts.shape[0], proj_in.shape[0]
    sequences, own_queries = tokens // LEN, query_ids.shape[0]
    queries = own_queries * devices
    f32 = jnp.float32
    in_vmem = pl.BlockSpec(memory_space=pltpu.VMEM)
    in_hbm = pl.BlockSpec(memory_space=pltpu.HBM)
    params = pltpu.CompilerParams(vmem_limit_bytes=VMEM_BYTES)
    tables = tuple(
        pltpu.with_memory_space_constraint(t, pltpu.HBM)
        for t in (acts, grad_q, grad_k, grad_v, proj_in, proj_q, proj_k, proj_v)
    )

    factors, grams, query = pl.pallas_call(
        functools.partial(front_kernel, tokens * devices, sequences, width),
        out_shape=(
            jax.ShapeDtypeStruct((width + 8, 2 * width), f32),
            jax.ShapeDtypeStruct((sequences, width, 4 * width), f32),
            jax.ShapeDtypeStruct((own_queries, 3 * width // 2, 2 * width), f32),
        ),
        in_specs=[pl.BlockSpec(memory_space=pltpu.SMEM)] + [in_hbm] * 8,
        out_specs=(in_vmem,) * 3,
        scratch_shapes=[pltpu.VMEM(t.shape, t.dtype) for t in tables]
        + [pltpu.SemaphoreType.DMA((6 + 4 * -(-tokens // HALF),))],
        compiler_params=pltpu.CompilerParams(vmem_limit_bytes=FRONT_VMEM_BYTES),
        name="front",
    )(query_ids, *tables)

    factor_bits = list(range(steps))
    if steps > 2:
        factor_bits[1], factor_bits[2] = 2, 1
    blocks, waiting, sent_queries = [query], None, 0

    def send_query():
        nonlocal sent_queries
        sent = blocks[0] if len(blocks) == 1 else jnp.concatenate(blocks, axis=0)
        sent_queries += 1
        return exchange(sent, devices, 1 << (steps - sent_queries))

    mine = factors
    for step in range(steps):
        theirs = exchange(mine, devices, 1 << factor_bits[step])
        if step == 0:
            waiting = send_query()
        elif step in OPENS and sent_queries < steps:
            waiting, _ = lax.optimization_barrier((waiting, theirs))
            blocks.append(waiting)
            waiting = send_query()
        if step < steps - 1:
            mine = mine + theirs
    terms = (mine, theirs)

    train = pl.pallas_call(
        functools.partial(invert_kernel, sequences, width),
        out_shape=jax.ShapeDtypeStruct((sequences, 3 * width // 2, 2 * width), f32),
        in_specs=[in_vmem] * 3,
        out_specs=in_vmem,
        scratch_shapes=[
            pltpu.VMEM((4 * width, 4 * width), f32),
            pltpu.VMEM((sequences * width, 4 * width), f32),
        ],
        compiler_params=params,
        name="invert",
    )(*terms, grams)
    waiting, _ = lax.optimization_barrier((waiting, train))
    blocks.append(waiting)
    while sent_queries < steps:
        blocks.append(send_query())

    return pl.pallas_call(
        functools.partial(
            score_kernel, functools.partial(reversed_bits, steps), sequences, width, queries
        ),
        out_shape=jax.ShapeDtypeStruct((sequences, queries), f32),
        in_specs=[in_vmem] * (1 + len(blocks)),
        out_specs=in_vmem,
        scratch_shapes=[pltpu.VMEM((sequences, queries * 8, 2 * width), f32)],
        compiler_params=params,
        name="scores",
    )(train, *blocks)


def solution(mesh):
    return jax.shard_map(
        per_device,
        mesh=mesh,
        in_specs=(
            P(("group", "dp"), None),
            P(("group", "dp"), None),
            P(("group", "dp"), None),
            P(("group", "dp"), None),
            P(),
            P(),
            P(),
            P(),
            P(("group", "dp")),
        ),
        out_specs=P(("group", "dp"), None),
        check_vma=False,
    )
```

```python
import functools

import jax
import jax.numpy as jnp
from jax import lax
from jax.experimental import pallas as pl
from jax.experimental.pallas import tpu as pltpu
from jax.sharding import PartitionSpec as P

LEN = 128
LANES = 128
PANEL = 8
HALF = 256
IN_FLIGHT = 5
OPENS = (1, 2, 3)
HIGHEST = lax.Precision.HIGHEST
FRONT_VMEM_BYTES = 24 * 1024 * 1024
VMEM_BYTES = 8 * 1024 * 1024
NT = (((1,), (1,)), ((), ()))
TN = (((0,), (0,)), ((), ()))
NN = (((1,), (0,)), ((), ()))


def dot(a, b, dims, precision=HIGHEST):
    return lax.dot_general(a, b, dims, precision=precision, preferred_element_type=jnp.float32)


def places(order):
    shape = (order, 2 * order)
    lane = lax.broadcasted_iota(jnp.int32, shape, 1)
    return lax.broadcasted_iota(jnp.int32, shape, 0), lane % order


def front_kernel(
    total_tokens, sequences, width,
    ids, acts, grad_q, grad_k, grad_v, proj_in, proj_q, proj_k, proj_v,
    factors, grams, query,
    acts_v, gq_v, gk_v, gv_v, pi_v, pq_v, pk_v, pv_v, sem,
):
    tokens = acts.shape[0]
    rows = min(HALF, tokens)
    moves = [(proj_k, pk_v), (grad_k, gk_v), (proj_v, pv_v), (grad_v, gv_v)]
    for first in range(0, tokens, rows):
        for src, dst, table, table_v in ((acts, acts_v, proj_in, pi_v), (grad_q, gq_v, proj_q, pq_v)):
            if first == 0:
                moves.append((table, table_v))
            box = pl.ds(first, rows)
            moves.append((src.at[box], dst.at[box]))
    copies = [pltpu.make_async_copy(src, dst, sem.at[i]) for i, (src, dst) in enumerate(moves)]
    for copy in copies[:IN_FLIGHT]:
        copy.start()
    waited = []

    def arrived(count):
        for _ in range(count):
            i = len(waited)
            copies[i].wait()
            if i + IN_FLIGHT < len(copies):
                copies[i + IN_FLIGHT].start()
            waited.append(i)

    left = lax.broadcasted_iota(jnp.int32, (width, 2 * width), 1) < width
    sums = [None, None]

    def gram_blocks(first, sides):
        coords = jnp.concatenate(sides, axis=0)
        high = coords.astype(jnp.bfloat16)
        low = (coords - high.astype(jnp.float32)).astype(jnp.bfloat16)
        for seq in range(rows // LEN):
            here = slice(seq * LEN, (seq + 1) * LEN)
            one = jnp.concatenate([high[:, here], low[:, here], high[:, here]], axis=1)
            other = jnp.concatenate([high[:, here], high[:, here], low[:, here]], axis=1)
            gram = dot(one, other, NT, None)
            grams[first // LEN + seq] = gram[:width] * (1.0 / LEN)
            squares = [gram[p * width : (p + 1) * width, p // 2 * 2 * width : (p // 2 + 1) * 2 * width] for p in range(4)]
            for i in range(2):
                pair = jnp.where(left, squares[2 * i], squares[2 * i + 1])
                sums[i] = pair if sums[i] is None else sums[i] + pair

    arrived(2)
    coords_k = dot(pk_v[...], gk_v[...], NT, None)
    arrived(2)
    coords_v = dot(pv_v[...], gv_v[...], NT, None)
    ready = None
    for first in range(0, tokens, rows):
        whole = slice(first, first + rows)
        sides = []
        for data, table in ((acts_v, pi_v), (gq_v, pq_v)):
            arrived(2 if first == 0 else 1)
            sides.append(dot(table[...], data[whole], NT, None))
            if ready is not None:
                gram_blocks(*ready)
                ready = None
        ready = first, sides + [coords_k[:, whole], coords_v[:, whole]]
    gram_blocks(*ready)
    upper, lower = sums
    row, column = places(width)
    scale = 1.0 / total_tokens
    factors[:width] = jnp.where(column >= row, upper, lower) * scale
    diagonal = jnp.sum(jnp.where(column == row, lower, 0.0), axis=0, keepdims=True) * scale
    factors[width:] = jnp.broadcast_to(diagonal, (8, 2 * width))
    half = width // 2
    for q in range(query.shape[0]):
        chosen = grams[ids[q]]
        query[q, :width] = chosen[:, 2 * width :]
        in_q = chosen[:, : 2 * width]
        query[q, width:] = jnp.where(left[:half], pltpu.roll(in_q[:half], width, 1), in_q[half:])


def damped(packed):
    order = packed.shape[1] // 2
    half = order // 2
    square, diagonal = packed[:order], packed[order : order + 1]
    row, column = places(order)
    turned = square.T
    turned = jnp.concatenate([turned[:order], turned[order:]], axis=1)
    on_diagonal = column == row
    first = jnp.where(column >= row, square, turned)
    second = jnp.where(column < row, square, turned)
    first_diagonal = jnp.sum(jnp.where(on_diagonal, square, 0.0), axis=0, keepdims=True)
    shape = (LANES, LANES)
    same = (
        lax.broadcasted_iota(jnp.int32, shape, 0) // order
        == lax.broadcasted_iota(jnp.int32, shape, 1) // order
    )
    diagonals = jnp.concatenate([first_diagonal, diagonal], axis=0)
    diagonals = jnp.concatenate([diagonals] * 4, axis=0)
    damping = dot(diagonals, jnp.where(same, 0.1 / order, 0.0), NN)
    first = first + jnp.where(on_diagonal, damping[:1], 0.0)
    second = jnp.where(on_diagonal, diagonal + damping[1:2], second)
    is_low = column < half
    low = jnp.where(is_low, first, pltpu.roll(second, half, 1))
    high = jnp.where(is_low, pltpu.roll(first, LANES - half, 1), second)
    return low, high


def invert(low, high):
    order = low.shape[0]
    half = order // 2
    groups = order // 8
    state = [[x[8 * g : 8 * g + 8] for g in range(groups)] for x in (low, high)]
    lane = lax.broadcasted_iota(jnp.int32, (8, LANES), 1)
    row = lax.broadcasted_iota(jnp.int32, (8, LANES), 0)
    column_of_lane = lane % half
    first_lane = lane - column_of_lane
    for start in range(0, order, PANEL):
        h, first = start // half, start % half
        spread = [
            [jnp.take_along_axis(state[h][g], first_lane + (first + j), axis=1) for g in range(groups)]
            for j in range(PANEL)
        ]
        in_panel = (column_of_lane >= first) & (column_of_lane < first + PANEL)
        state[h] = [jnp.where(in_panel, 0.0, x) for x in state[h]]
        for j in range(PANEL):
            k = start + j
            g, r = k // 8, k % 8
            column = spread[j]
            pivot = 1.0 / column[g][r : r + 1]
            for t in range(2):
                values = state[t][g][r : r + 1]
                if t == h:
                    values = jnp.where(column_of_lane[:1] == first + j, 1.0, values)
                values = values * pivot
                state[t] = [x - c * values for x, c in zip(state[t], column)]
                state[t][g] = jnp.where(row == r, values, state[t][g])
            for i in range(j + 1, PANEL):
                values = spread[i][g][r : r + 1] * pivot
                spread[i] = [x - c * values for x, c in zip(spread[i], column)]
                spread[i][g] = jnp.where(row == r, values, spread[i][g])
    return [jnp.concatenate(state[h], axis=0) for h in range(2)]


def invert_kernel(sequences, width, first, second, grams, train, side_v, left_v):
    half = width // 2
    low, high = invert(*damped(first[...] + second[...]))
    by_lanes = [
        jnp.concatenate([low[:, p * half : (p + 1) * half], high[:, p * half : (p + 1) * half]], axis=1)
        for p in range(4)
    ]
    inverse_in, inverse_k, inverse_q, inverse_v = by_lanes
    side_v[...] = jnp.zeros_like(side_v)
    side_v[width : 2 * width, 2 * width : 3 * width] = inverse_q
    side_v[width : 2 * width, 3 * width :] = inverse_q
    side_v[2 * width : 3 * width, :width] = inverse_k
    side_v[3 * width :, width : 2 * width] = inverse_v
    left_v[...] = dot(grams[...].reshape(sequences * width, 4 * width), side_v[...], NN)
    on_left = lax.broadcasted_iota(jnp.int32, (half, 2 * width), 1) < width
    for s in range(sequences):
        done = dot(inverse_in, left_v[pl.ds(s * width, width)], NN)
        train[s, :width] = done[:, : 2 * width]
        train[s, width:] = jnp.where(on_left, done[:half, 2 * width :], done[half:, 2 * width :])


def score_kernel(offsets, sequences, width, queries, train, *refs):
    blocks, out, partial_v = refs[:-2], refs[-2], refs[-1]
    me = lax.axis_index("dp")
    slot = 0
    for block in blocks:
        for i in range(block.shape[0]):
            value = block[i]
            for s in range(sequences):
                product = (train[s] * value).reshape(-1, 8, 2 * width)
                partial_v[s, pl.ds(slot * 8, 8)] = jnp.sum(product, axis=0)
            slot += 1
    own = queries // lax.axis_size("dp")
    shape = (queries, queries * 8)
    target = lax.broadcasted_iota(jnp.int32, shape, 0)
    source = lax.broadcasted_iota(jnp.int32, shape, 1) // 8
    offset = offsets(source // own)
    select = jnp.where(target == (offset ^ me) * own + source % own, 1.0, 0.0)
    ones = jnp.ones((8, 2 * width), jnp.float32)
    for s in range(sequences):
        by_query = dot(select, partial_v[s], NN)
        out[pl.ds(s, 1)] = dot(ones, by_query, NT)[:1]


def exchange(x, devices, distance):
    return lax.ppermute(x, "dp", [(i, i ^ distance) for i in range(devices)])


def reversed_bits(count, slot):
    out = jnp.zeros_like(slot)
    for j in range(count):
        out = out + (slot >> j & 1) * (1 << (count - 1 - j))
    return out


def per_device(acts, grad_q, grad_k, grad_v, proj_in, proj_q, proj_k, proj_v, query_ids):
    devices = lax.axis_size("dp")
    steps = devices.bit_length() - 1
    tokens, width = acts.shape[0], proj_in.shape[0]
    sequences, own_queries = tokens // LEN, query_ids.shape[0]
    queries = own_queries * devices
    f32 = jnp.float32
    in_vmem = pl.BlockSpec(memory_space=pltpu.VMEM)
    in_hbm = pl.BlockSpec(memory_space=pltpu.HBM)
    params = pltpu.CompilerParams(vmem_limit_bytes=VMEM_BYTES)
    tables = tuple(
        pltpu.with_memory_space_constraint(t, pltpu.HBM)
        for t in (acts, grad_q, grad_k, grad_v, proj_in, proj_q, proj_k, proj_v)
    )

    factors, grams, query = pl.pallas_call(
        functools.partial(front_kernel, tokens * devices, sequences, width),
        out_shape=(
            jax.ShapeDtypeStruct((width + 8, 2 * width), f32),
            jax.ShapeDtypeStruct((sequences, width, 4 * width), f32),
            jax.ShapeDtypeStruct((own_queries, 3 * width // 2, 2 * width), f32),
        ),
        in_specs=[pl.BlockSpec(memory_space=pltpu.SMEM)] + [in_hbm] * 8,
        out_specs=(in_vmem,) * 3,
        scratch_shapes=[pltpu.VMEM(t.shape, t.dtype) for t in tables]
        + [pltpu.SemaphoreType.DMA((6 + 2 * -(-tokens // HALF),))],
        compiler_params=pltpu.CompilerParams(vmem_limit_bytes=FRONT_VMEM_BYTES),
        name="front",
    )(query_ids, *tables)

    factor_bits = list(range(steps))
    if steps > 2:
        factor_bits[1], factor_bits[2] = 2, 1
    blocks, waiting, sent_queries = [query], None, 0

    def send_query():
        nonlocal sent_queries
        sent = blocks[0] if len(blocks) == 1 else jnp.concatenate(blocks, axis=0)
        sent_queries += 1
        return exchange(sent, devices, 1 << (steps - sent_queries))

    mine = factors
    for step in range(steps):
        theirs = exchange(mine, devices, 1 << factor_bits[step])
        total = mine + theirs if step < steps - 1 else theirs
        if step == 0:
            waiting = send_query()
        elif step in OPENS and sent_queries < steps:
            waiting, _ = lax.optimization_barrier((waiting, total))
            blocks.append(waiting)
            waiting = send_query()
        if step < steps - 1:
            mine = total
    terms = (mine, theirs)

    train = pl.pallas_call(
        functools.partial(invert_kernel, sequences, width),
        out_shape=jax.ShapeDtypeStruct((sequences, 3 * width // 2, 2 * width), f32),
        in_specs=[in_vmem] * 3,
        out_specs=in_vmem,
        scratch_shapes=[
            pltpu.VMEM((4 * width, 4 * width), f32),
            pltpu.VMEM((sequences * width, 4 * width), f32),
        ],
        compiler_params=params,
        name="invert",
    )(*terms, grams)
    blocks.append(waiting)
    while sent_queries < steps:
        blocks.append(send_query())

    return pl.pallas_call(
        functools.partial(
            score_kernel, functools.partial(reversed_bits, steps), sequences, width, queries
        ),
        out_shape=jax.ShapeDtypeStruct((sequences, queries), f32),
        in_specs=[in_vmem] * (1 + len(blocks)),
        out_specs=in_vmem,
        scratch_shapes=[pltpu.VMEM((sequences, queries * 8, 2 * width), f32)],
        compiler_params=params,
        name="scores",
    )(train, *blocks)


def solution(mesh):
    return jax.shard_map(
        per_device,
        mesh=mesh,
        in_specs=(
            P(("group", "dp"), None),
            P(("group", "dp"), None),
            P(("group", "dp"), None),
            P(("group", "dp"), None),
            P(),
            P(),
            P(),
            P(),
            P(("group", "dp")),
        ),
        out_specs=P(("group", "dp"), None),
        check_vma=False,
    )
```

```python
import functools

import jax
import jax.numpy as jnp
from jax import lax
from jax.experimental import pallas as pl
from jax.experimental.pallas import tpu as pltpu
from jax.sharding import PartitionSpec as P

LEN = 128
LANES = 128
PANEL = 8
HALF = 256
IN_FLIGHT = 5
HIGHEST = lax.Precision.HIGHEST
FRONT_VMEM_BYTES = 24 * 1024 * 1024
VMEM_BYTES = 8 * 1024 * 1024
NT = (((1,), (1,)), ((), ()))
TN = (((0,), (0,)), ((), ()))
NN = (((1,), (0,)), ((), ()))


def dot(a, b, dims, precision=HIGHEST):
    return lax.dot_general(a, b, dims, precision=precision, preferred_element_type=jnp.float32)


def places(order):
    shape = (order, 2 * order)
    lane = lax.broadcasted_iota(jnp.int32, shape, 1)
    return lax.broadcasted_iota(jnp.int32, shape, 0), lane % order


def front_kernel(
    total_tokens, sequences, width,
    ids, acts, grad_q, grad_k, grad_v, proj_in, proj_q, proj_k, proj_v,
    message, grams,
    acts_v, gq_v, gk_v, gv_v, pi_v, pq_v, pk_v, pv_v, sem,
):
    tokens = acts.shape[0]
    rows = min(HALF, tokens)
    moves = [(proj_k, pk_v), (grad_k, gk_v), (proj_v, pv_v), (grad_v, gv_v)]
    for first in range(0, tokens, rows):
        for src, dst, table, table_v in ((acts, acts_v, proj_in, pi_v), (grad_q, gq_v, proj_q, pq_v)):
            if first == 0:
                moves.append((table, table_v))
            box = pl.ds(first, rows)
            moves.append((src.at[box], dst.at[box]))
    copies = [pltpu.make_async_copy(src, dst, sem.at[i]) for i, (src, dst) in enumerate(moves)]
    for copy in copies[:IN_FLIGHT]:
        copy.start()
    waited = []

    def arrived(count):
        for _ in range(count):
            i = len(waited)
            copies[i].wait()
            if i + IN_FLIGHT < len(copies):
                copies[i + IN_FLIGHT].start()
            waited.append(i)

    left = lax.broadcasted_iota(jnp.int32, (width, 2 * width), 1) < width
    sums = [None, None]

    def gram_blocks(first, sides):
        coords = jnp.concatenate(sides, axis=0)
        high = coords.astype(jnp.bfloat16)
        low = (coords - high.astype(jnp.float32)).astype(jnp.bfloat16)
        for seq in range(rows // LEN):
            here = slice(seq * LEN, (seq + 1) * LEN)
            one = jnp.concatenate([high[:, here], low[:, here], high[:, here]], axis=1)
            other = jnp.concatenate([high[:, here], high[:, here], low[:, here]], axis=1)
            gram = dot(one, other, NT, None)
            grams[first // LEN + seq] = gram[:width] * (1.0 / LEN)
            squares = [gram[p * width : (p + 1) * width, p // 2 * 2 * width : (p // 2 + 1) * 2 * width] for p in range(4)]
            for i in range(2):
                pair = jnp.where(left, squares[2 * i], squares[2 * i + 1])
                sums[i] = pair if sums[i] is None else sums[i] + pair

    arrived(2)
    coords_k = dot(pk_v[...], gk_v[...], NT, None)
    arrived(2)
    coords_v = dot(pv_v[...], gv_v[...], NT, None)
    ready = None
    for first in range(0, tokens, rows):
        whole = slice(first, first + rows)
        sides = []
        for data, table in ((acts_v, pi_v), (gq_v, pq_v)):
            arrived(2 if first == 0 else 1)
            sides.append(dot(table[...], data[whole], NT, None))
            if ready is not None:
                gram_blocks(*ready)
                ready = None
        ready = first, sides + [coords_k[:, whole], coords_v[:, whole]]
    gram_blocks(*ready)
    upper, lower = sums
    row, column = places(width)
    scale = 1.0 / total_tokens
    message[:width] = jnp.where(column >= row, upper, lower) * scale
    diagonal = jnp.sum(jnp.where(column == row, lower, 0.0), axis=0, keepdims=True) * scale
    message[width : width + 8] = jnp.broadcast_to(diagonal, (8, 2 * width))
    half = width // 2
    for q in range(ids.shape[0]):
        chosen = grams[ids[q]]
        in_q = chosen[:, : 2 * width]
        start = width + 8 + q * 3 * half
        message[start : start + width] = chosen[:, 2 * width :]
        message[start + width : start + 3 * half] = jnp.where(
            left[:half], pltpu.roll(in_q[:half], width, 1), in_q[half:]
        )


def damped(packed):
    order = packed.shape[1] // 2
    half = order // 2
    square, diagonal = packed[:order], packed[order : order + 1]
    row, column = places(order)
    turned = square.T
    turned = jnp.concatenate([turned[:order], turned[order:]], axis=1)
    on_diagonal = column == row
    first = jnp.where(column >= row, square, turned)
    second = jnp.where(column < row, square, turned)
    first_diagonal = jnp.sum(jnp.where(on_diagonal, square, 0.0), axis=0, keepdims=True)
    shape = (LANES, LANES)
    same = (
        lax.broadcasted_iota(jnp.int32, shape, 0) // order
        == lax.broadcasted_iota(jnp.int32, shape, 1) // order
    )
    diagonals = jnp.concatenate([first_diagonal, diagonal], axis=0)
    diagonals = jnp.concatenate([diagonals] * 4, axis=0)
    damping = dot(diagonals, jnp.where(same, 0.1 / order, 0.0), NN)
    first = first + jnp.where(on_diagonal, damping[:1], 0.0)
    second = jnp.where(on_diagonal, diagonal + damping[1:2], second)
    is_low = column < half
    low = jnp.where(is_low, first, pltpu.roll(second, half, 1))
    high = jnp.where(is_low, pltpu.roll(first, LANES - half, 1), second)
    return low, high


def invert(low, high):
    order = low.shape[0]
    half = order // 2
    groups = order // 8
    state = [[x[8 * g : 8 * g + 8] for g in range(groups)] for x in (low, high)]
    lane = lax.broadcasted_iota(jnp.int32, (8, LANES), 1)
    row = lax.broadcasted_iota(jnp.int32, (8, LANES), 0)
    column_of_lane = lane % half
    first_lane = lane - column_of_lane
    for start in range(0, order, PANEL):
        h, first = start // half, start % half
        spread = [
            [jnp.take_along_axis(state[h][g], first_lane + (first + j), axis=1) for g in range(groups)]
            for j in range(PANEL)
        ]
        in_panel = (column_of_lane >= first) & (column_of_lane < first + PANEL)
        state[h] = [jnp.where(in_panel, 0.0, x) for x in state[h]]
        for j in range(PANEL):
            k = start + j
            g, r = k // 8, k % 8
            column = spread[j]
            pivot = 1.0 / column[g][r : r + 1]
            for t in range(2):
                values = state[t][g][r : r + 1]
                if t == h:
                    values = jnp.where(column_of_lane[:1] == first + j, 1.0, values)
                values = values * pivot
                state[t] = [x - c * values for x, c in zip(state[t], column)]
                state[t][g] = jnp.where(row == r, values, state[t][g])
            for i in range(j + 1, PANEL):
                values = spread[i][g][r : r + 1] * pivot
                spread[i] = [x - c * values for x, c in zip(spread[i], column)]
                spread[i][g] = jnp.where(row == r, values, spread[i][g])
    return [jnp.concatenate(state[h], axis=0) for h in range(2)]


def invert_kernel(sequences, width, first, second, grams, train, side_v, left_v):
    half = width // 2
    low, high = invert(*damped(first[...] + second[...]))
    by_lanes = [
        jnp.concatenate([low[:, p * half : (p + 1) * half], high[:, p * half : (p + 1) * half]], axis=1)
        for p in range(4)
    ]
    inverse_in, inverse_k, inverse_q, inverse_v = by_lanes
    side_v[...] = jnp.zeros_like(side_v)
    side_v[width : 2 * width, 2 * width : 3 * width] = inverse_q
    side_v[width : 2 * width, 3 * width :] = inverse_q
    side_v[2 * width : 3 * width, :width] = inverse_k
    side_v[3 * width :, width : 2 * width] = inverse_v
    left_v[...] = dot(grams[...].reshape(sequences * width, 4 * width), side_v[...], NN)
    on_left = lax.broadcasted_iota(jnp.int32, (half, 2 * width), 1) < width
    for s in range(sequences):
        done = dot(inverse_in, left_v[pl.ds(s * width, width)], NN)
        train[s, :width] = done[:, : 2 * width]
        train[s, width:] = jnp.where(on_left, done[:half, 2 * width :], done[half:, 2 * width :])


def products(train, blocks, partial):
    slot = 0
    for block in blocks:
        for i in range(block.shape[0]):
            value = block[i]
            for s in range(train.shape[0]):
                product = (train[s] * value).reshape(-1, 8, train.shape[2])
                partial[s, pl.ds(slot * 8, 8)] = jnp.sum(product, axis=0)
            slot += 1


def early_kernel(train, *refs):
    products(train, refs[:-1], refs[-1])


def score_kernel(offsets, queries, train, early, block, out, late):
    products(train, (block,), late)
    me = lax.axis_index("dp")
    own = queries // lax.axis_size("dp")
    ones = jnp.ones((8, train.shape[2]), jnp.float32)
    selects, first = [], 0
    for partial in (early, late):
        shape = (queries, partial.shape[1])
        target = lax.broadcasted_iota(jnp.int32, shape, 0)
        source = lax.broadcasted_iota(jnp.int32, shape, 1) // 8 + first
        first += partial.shape[1] // 8
        offset = offsets(source // own)
        selects.append(jnp.where(target == (offset ^ me) * own + source % own, 1.0, 0.0))
    for s in range(train.shape[0]):
        by_query = dot(selects[0], early[s], NN) + dot(selects[1], late[s], NN)
        out[pl.ds(s, 1)] = dot(ones, by_query, NT)[:1]


def exchange(x, devices, distance):
    return lax.ppermute(x, "dp", [(i, i ^ distance) for i in range(devices)])


def reversed_bits(count, slot):
    out = jnp.zeros_like(slot)
    for j in range(count):
        out = out + (slot >> j & 1) * (1 << (count - 1 - j))
    return out


def per_device(acts, grad_q, grad_k, grad_v, proj_in, proj_q, proj_k, proj_v, query_ids):
    devices = lax.axis_size("dp")
    steps = devices.bit_length() - 1
    tokens, width = acts.shape[0], proj_in.shape[0]
    sequences, own_queries = tokens // LEN, query_ids.shape[0]
    queries = own_queries * devices
    f32 = jnp.float32
    in_vmem = pl.BlockSpec(memory_space=pltpu.VMEM)
    in_hbm = pl.BlockSpec(memory_space=pltpu.HBM)
    params = pltpu.CompilerParams(vmem_limit_bytes=VMEM_BYTES)
    tables = tuple(
        pltpu.with_memory_space_constraint(t, pltpu.HBM)
        for t in (acts, grad_q, grad_k, grad_v, proj_in, proj_q, proj_k, proj_v)
    )

    message, grams = pl.pallas_call(
        functools.partial(front_kernel, tokens * devices, sequences, width),
        out_shape=(
            jax.ShapeDtypeStruct((width + 8 + own_queries * 3 * width // 2, 2 * width), f32),
            jax.ShapeDtypeStruct((sequences, width, 4 * width), f32),
        ),
        in_specs=[pl.BlockSpec(memory_space=pltpu.SMEM)] + [in_hbm] * 8,
        out_specs=(in_vmem,) * 2,
        scratch_shapes=[pltpu.VMEM(t.shape, t.dtype) for t in tables]
        + [pltpu.SemaphoreType.DMA((6 + 2 * -(-tokens // HALF),))],
        compiler_params=pltpu.CompilerParams(vmem_limit_bytes=FRONT_VMEM_BYTES),
        name="front",
    )(query_ids, *tables)

    cut = width + 8
    received = exchange(message, devices, devices // 2)
    blocks = [x[cut:].reshape(own_queries, -1, 2 * width) for x in (message, received)]
    mine, theirs = message[:cut], received[:cut]
    sent_queries, waiting = 1, None

    def send_query():
        nonlocal sent_queries
        sent_queries += 1
        return exchange(jnp.concatenate(blocks, axis=0), devices, 1 << (steps - sent_queries))

    for bit in list(range(1, steps - 1)) + [0]:
        mine = mine + theirs
        if sent_queries < steps - 1:
            if waiting is not None:
                waiting, _ = lax.optimization_barrier((waiting, mine))
                blocks.append(waiting)
            waiting = send_query()
        theirs = exchange(mine, devices, 1 << bit)
    terms = (mine, theirs)

    train = pl.pallas_call(
        functools.partial(invert_kernel, sequences, width),
        out_shape=jax.ShapeDtypeStruct((sequences, 3 * width // 2, 2 * width), f32),
        in_specs=[in_vmem] * 3,
        out_specs=in_vmem,
        scratch_shapes=[
            pltpu.VMEM((4 * width, 4 * width), f32),
            pltpu.VMEM((sequences * width, 4 * width), f32),
        ],
        compiler_params=params,
        name="invert",
    )(*terms, grams)
    if waiting is not None:
        waiting, _ = lax.optimization_barrier((waiting, train))
        blocks.append(waiting)
    last = send_query()

    def partial_shape(slots):
        return (sequences, slots * 8, 2 * width)

    early = pl.pallas_call(
        early_kernel,
        out_shape=jax.ShapeDtypeStruct(partial_shape(queries // 2), f32),
        in_specs=[in_vmem] * (1 + len(blocks)),
        out_specs=in_vmem,
        compiler_params=params,
        name="early",
    )(train, *blocks)
    return pl.pallas_call(
        functools.partial(score_kernel, functools.partial(reversed_bits, steps), queries),
        out_shape=jax.ShapeDtypeStruct((sequences, queries), f32),
        in_specs=[in_vmem] * 3,
        out_specs=in_vmem,
        scratch_shapes=[pltpu.VMEM(partial_shape(queries // 2), f32)],
        compiler_params=params,
        name="scores",
    )(train, early, last)


def solution(mesh):
    return jax.shard_map(
        per_device,
        mesh=mesh,
        in_specs=(
            P(("group", "dp"), None),
            P(("group", "dp"), None),
            P(("group", "dp"), None),
            P(("group", "dp"), None),
            P(),
            P(),
            P(),
            P(),
            P(("group", "dp")),
        ),
        out_specs=P(("group", "dp"), None),
        check_vma=False,
    )
```

```python
import functools

import jax
import jax.numpy as jnp
from jax import lax
from jax.experimental import pallas as pl
from jax.experimental.pallas import tpu as pltpu
from jax.sharding import PartitionSpec as P

LEN = 128
LANES = 128
PANEL = 8
HALF = 256
IN_FLIGHT = 5
HIGHEST = lax.Precision.HIGHEST
FRONT_VMEM_BYTES = 24 * 1024 * 1024
VMEM_BYTES = 16 * 1024 * 1024
NT = (((1,), (1,)), ((), ()))
TN = (((0,), (0,)), ((), ()))
NN = (((1,), (0,)), ((), ()))


def dot(a, b, dims, precision=HIGHEST):
    return lax.dot_general(a, b, dims, precision=precision, preferred_element_type=jnp.float32)


def places(order):
    shape = (order, 2 * order)
    lane = lax.broadcasted_iota(jnp.int32, shape, 1)
    return lax.broadcasted_iota(jnp.int32, shape, 0), lane % order


def front_kernel(
    total_tokens, sequences, width,
    ids, acts, grad_q, grad_k, grad_v, proj_in, proj_q, proj_k, proj_v,
    factors, grams, query,
    acts_v, gq_v, gk_v, gv_v, pi_v, pq_v, pk_v, pv_v, sem,
):
    tokens = acts.shape[0]
    rows = min(HALF, tokens)
    moves = [(proj_k, pk_v), (grad_k, gk_v), (proj_v, pv_v), (grad_v, gv_v)]
    for first in range(0, tokens, rows):
        for src, dst, table, table_v in ((acts, acts_v, proj_in, pi_v), (grad_q, gq_v, proj_q, pq_v)):
            if first == 0:
                moves.append((table, table_v))
            box = pl.ds(first, rows)
            moves.append((src.at[box], dst.at[box]))
    copies = [pltpu.make_async_copy(src, dst, sem.at[i]) for i, (src, dst) in enumerate(moves)]
    for copy in copies[:IN_FLIGHT]:
        copy.start()
    waited = []

    def arrived(count):
        for _ in range(count):
            i = len(waited)
            copies[i].wait()
            if i + IN_FLIGHT < len(copies):
                copies[i + IN_FLIGHT].start()
            waited.append(i)

    left = lax.broadcasted_iota(jnp.int32, (width, 2 * width), 1) < width
    sums = [None, None]

    def gram_blocks(first, sides):
        coords = jnp.concatenate(sides, axis=0)
        high = coords.astype(jnp.bfloat16)
        low = (coords - high.astype(jnp.float32)).astype(jnp.bfloat16)
        for seq in range(rows // LEN):
            here = slice(seq * LEN, (seq + 1) * LEN)
            one = jnp.concatenate([high[:, here], low[:, here], high[:, here]], axis=1)
            other = jnp.concatenate([high[:, here], high[:, here], low[:, here]], axis=1)
            gram = dot(one, other, NT, None)
            grams[first // LEN + seq] = gram[:width] * (1.0 / LEN)
            squares = [gram[p * width : (p + 1) * width, p // 2 * 2 * width : (p // 2 + 1) * 2 * width] for p in range(4)]
            for i in range(2):
                pair = jnp.where(left, squares[2 * i], squares[2 * i + 1])
                sums[i] = pair if sums[i] is None else sums[i] + pair

    arrived(2)
    coords_k = dot(pk_v[...], gk_v[...], NT, None)
    arrived(2)
    coords_v = dot(pv_v[...], gv_v[...], NT, None)
    ready = None
    for first in range(0, tokens, rows):
        whole = slice(first, first + rows)
        sides = []
        for data, table in ((acts_v, pi_v), (gq_v, pq_v)):
            arrived(2 if first == 0 else 1)
            sides.append(dot(table[...], data[whole], NT, None))
            if ready is not None:
                gram_blocks(*ready)
                ready = None
        ready = first, sides + [coords_k[:, whole], coords_v[:, whole]]
    gram_blocks(*ready)
    upper, lower = sums
    row, column = places(width)
    scale = 1.0 / total_tokens
    factors[:width] = jnp.where(column >= row, upper, lower) * scale
    diagonal = jnp.sum(jnp.where(column == row, lower, 0.0), axis=0, keepdims=True) * scale
    factors[width:] = jnp.broadcast_to(diagonal, (8, 2 * width))
    half = width // 2
    for q in range(query.shape[0]):
        chosen = grams[ids[q]]
        query[q, :width] = chosen[:, 2 * width :]
        in_q = chosen[:, : 2 * width]
        query[q, width:] = jnp.where(left[:half], pltpu.roll(in_q[:half], width, 1), in_q[half:])


def damped(packed):
    order = packed.shape[1] // 2
    half = order // 2
    square, diagonal = packed[:order], packed[order : order + 1]
    row, column = places(order)
    turned = square.T
    turned = jnp.concatenate([turned[:order], turned[order:]], axis=1)
    on_diagonal = column == row
    first = jnp.where(column >= row, square, turned)
    second = jnp.where(column < row, square, turned)
    first_diagonal = jnp.sum(jnp.where(on_diagonal, square, 0.0), axis=0, keepdims=True)
    shape = (LANES, LANES)
    same = (
        lax.broadcasted_iota(jnp.int32, shape, 0) // order
        == lax.broadcasted_iota(jnp.int32, shape, 1) // order
    )
    diagonals = jnp.concatenate([first_diagonal, diagonal], axis=0)
    diagonals = jnp.concatenate([diagonals] * 4, axis=0)
    damping = dot(diagonals, jnp.where(same, 0.1 / order, 0.0), NN)
    first = first + jnp.where(on_diagonal, damping[:1], 0.0)
    second = jnp.where(on_diagonal, diagonal + damping[1:2], second)
    is_low = column < half
    low = jnp.where(is_low, first, pltpu.roll(second, half, 1))
    high = jnp.where(is_low, pltpu.roll(first, LANES - half, 1), second)
    return low, high


def invert(low, high):
    order = low.shape[0]
    half = order // 2
    groups = order // 8
    state = [[x[8 * g : 8 * g + 8] for g in range(groups)] for x in (low, high)]
    lane = lax.broadcasted_iota(jnp.int32, (8, LANES), 1)
    row = lax.broadcasted_iota(jnp.int32, (8, LANES), 0)
    column_of_lane = lane % half
    first_lane = lane - column_of_lane
    for start in range(0, order, PANEL):
        h, first = start // half, start % half
        spread = [
            [jnp.take_along_axis(state[h][g], first_lane + (first + j), axis=1) for g in range(groups)]
            for j in range(PANEL)
        ]
        in_panel = (column_of_lane >= first) & (column_of_lane < first + PANEL)
        state[h] = [jnp.where(in_panel, 0.0, x) for x in state[h]]
        for j in range(PANEL):
            k = start + j
            g, r = k // 8, k % 8
            column = spread[j]
            pivot = 1.0 / column[g][r : r + 1]
            for t in range(2):
                values = state[t][g][r : r + 1]
                if t == h:
                    values = jnp.where(column_of_lane[:1] == first + j, 1.0, values)
                values = values * pivot
                state[t] = [x - c * values for x, c in zip(state[t], column)]
                state[t][g] = jnp.where(row == r, values, state[t][g])
            for i in range(j + 1, PANEL):
                values = spread[i][g][r : r + 1] * pivot
                spread[i] = [x - c * values for x, c in zip(spread[i], column)]
                spread[i][g] = jnp.where(row == r, values, spread[i][g])
    return [jnp.concatenate(state[h], axis=0) for h in range(2)]


def invert_kernel(sequences, width, first, second, grams, train, side_v, left_v):
    half = width // 2
    summed_here = lax.axis_index("dp") % 2 == 0
    low, high = invert(*damped(jnp.where(summed_here, first[...], second[...])))
    by_lanes = [
        jnp.concatenate([low[:, p * half : (p + 1) * half], high[:, p * half : (p + 1) * half]], axis=1)
        for p in range(4)
    ]
    inverse_in, inverse_k, inverse_q, inverse_v = by_lanes
    side_v[...] = jnp.zeros_like(side_v)
    side_v[width : 2 * width, 2 * width : 3 * width] = inverse_q
    side_v[width : 2 * width, 3 * width :] = inverse_q
    side_v[2 * width : 3 * width, :width] = inverse_k
    side_v[3 * width :, width : 2 * width] = inverse_v
    left_v[...] = dot(grams[...].reshape(sequences * width, 4 * width), side_v[...], NN)
    on_left = lax.broadcasted_iota(jnp.int32, (half, 2 * width), 1) < width
    for s in range(sequences):
        done = dot(inverse_in, left_v[pl.ds(s * width, width)], NN)
        train[s, :width] = done[:, : 2 * width]
        train[s, width:] = jnp.where(on_left, done[:half, 2 * width :], done[half:, 2 * width :])


def score_kernel(offsets, own, train, *refs):
    blocks, out, partial = refs[:4], refs[4], refs[5]
    gatherer = lax.axis_index("dp") | 1

    def products(block, first):
        for i in range(block.shape[0]):
            value = block[i]
            offset, which = offsets[(first + i) // own], (first + i) % own
            place = pl.ds(pl.multiple_of(((gatherer ^ offset) * own + which) * 8, 8), 8)
            for s in range(train.shape[0]):
                product = (train[s] * value).reshape(-1, 8, train.shape[2])
                partial[s, place] = jnp.sum(product, axis=0)

    for core in range(2):
        @pl.when(lax.axis_index("dp") % 2 == core)
        def _():
            early, late = (blocks[2:], blocks[:2])[core]
            products(early, 0)
            products(late, early.shape[0])

    ones = jnp.ones((8, train.shape[2]), jnp.float32)
    for s in range(train.shape[0]):
        by_query = jnp.sum(partial[s].reshape(-1, 8, train.shape[2]), axis=1)
        out[pl.ds(s, 1)] = dot(ones, by_query, NT)[:1]


def per_device(acts, grad_q, grad_k, grad_v, proj_in, proj_q, proj_k, proj_v, query_ids):
    devices = lax.axis_size("dp")
    steps = devices.bit_length() - 1
    tokens, width = acts.shape[0], proj_in.shape[0]
    sequences, own_queries = tokens // LEN, query_ids.shape[0]
    queries = own_queries * devices
    f32 = jnp.float32
    in_vmem = pl.BlockSpec(memory_space=pltpu.VMEM)
    in_hbm = pl.BlockSpec(memory_space=pltpu.HBM)
    params = pltpu.CompilerParams(vmem_limit_bytes=VMEM_BYTES)
    tables = tuple(
        pltpu.with_memory_space_constraint(t, pltpu.HBM)
        for t in (acts, grad_q, grad_k, grad_v, proj_in, proj_q, proj_k, proj_v)
    )

    factors, grams, query = pl.pallas_call(
        functools.partial(front_kernel, tokens * devices, sequences, width),
        out_shape=(
            jax.ShapeDtypeStruct((width + 8, 2 * width), f32),
            jax.ShapeDtypeStruct((sequences, width, 4 * width), f32),
            jax.ShapeDtypeStruct((own_queries, 3 * width // 2, 2 * width), f32),
        ),
        in_specs=[pl.BlockSpec(memory_space=pltpu.SMEM)] + [in_hbm] * 8,
        out_specs=(in_vmem,) * 3,
        scratch_shapes=[pltpu.VMEM(t.shape, t.dtype) for t in tables]
        + [pltpu.SemaphoreType.DMA((6 + 2 * -(-tokens // HALF),))],
        compiler_params=pltpu.CompilerParams(vmem_limit_bytes=FRONT_VMEM_BYTES),
        name="front",
    )(query_ids, *tables)

    def among(x, core, distance):
        return lax.ppermute(x, "dp", [(i, i ^ distance) for i in range(core, devices, 2)])

    given, guest = among(factors, 1, 1), among(query, 0, 1)
    guest, _ = lax.optimization_barrier((guest, given))
    mine, blocks, order = factors + given, [query, guest], [0]
    for bit in range(1, steps):
        mine = mine + among(mine, 0, 1 << bit)
        sent = jnp.concatenate(blocks, axis=0)
        order.append(steps - bit)
        blocks.append(among(sent, 1, 1 << order[-1]))
    last = blocks.pop()
    theirs = among(mine, 0, 1)
    copied = among(lax.optimization_barrier((sent, mine))[0], 1, 1)
    theirs, _ = lax.optimization_barrier((theirs, sent))
    offsets = [
        sum(1 << bit for j, bit in enumerate(order) if slot >> j & 1) for slot in range(devices)
    ]

    train = pl.pallas_call(
        functools.partial(invert_kernel, sequences, width),
        out_shape=jax.ShapeDtypeStruct((sequences, 3 * width // 2, 2 * width), f32),
        in_specs=[in_vmem] * 3,
        out_specs=in_vmem,
        scratch_shapes=[
            pltpu.VMEM((4 * width, 4 * width), f32),
            pltpu.VMEM((sequences * width, 4 * width), f32),
        ],
        compiler_params=params,
        name="invert",
    )(mine, theirs, grams)
    last, _ = lax.optimization_barrier((last, train))
    last_copied = among(last, 1, 1)

    return pl.pallas_call(
        functools.partial(score_kernel, offsets, own_queries),
        out_shape=jax.ShapeDtypeStruct((sequences, queries), f32),
        in_specs=[in_vmem] * 5,
        out_specs=in_vmem,
        scratch_shapes=[pltpu.VMEM((sequences, queries * 8, 2 * width), f32)],
        compiler_params=params,
        name="scores",
    )(train, sent, last, copied, last_copied)


def solution(mesh):
    return jax.shard_map(
        per_device,
        mesh=mesh,
        in_specs=(
            P(("group", "dp"), None),
            P(("group", "dp"), None),
            P(("group", "dp"), None),
            P(("group", "dp"), None),
            P(),
            P(),
            P(),
            P(),
            P(("group", "dp")),
        ),
        out_specs=P(("group", "dp"), None),
        check_vma=False,
    )
```

```python
import functools

import jax
import jax.numpy as jnp
from jax import lax
from jax.experimental import pallas as pl
from jax.experimental.pallas import tpu as pltpu
from jax.sharding import PartitionSpec as P

LEN = 128
LANES = 128
PANEL = 8
HALF = 256
IN_FLIGHT = 5
OPENS = (1, 2)
HIGHEST = lax.Precision.HIGHEST
FRONT_VMEM_BYTES = 24 * 1024 * 1024
VMEM_BYTES = 8 * 1024 * 1024
NT = (((1,), (1,)), ((), ()))
TN = (((0,), (0,)), ((), ()))
NN = (((1,), (0,)), ((), ()))


def dot(a, b, dims, precision=HIGHEST):
    return lax.dot_general(a, b, dims, precision=precision, preferred_element_type=jnp.float32)


def places(order):
    shape = (order, 2 * order)
    lane = lax.broadcasted_iota(jnp.int32, shape, 1)
    return lax.broadcasted_iota(jnp.int32, shape, 0), lane % order


def dot_split(a, b, dims):
    a_high, b_high = a.astype(jnp.bfloat16), b.astype(jnp.bfloat16)
    a_low = (a - a_high.astype(jnp.float32)).astype(jnp.bfloat16)
    b_low = (b - b_high.astype(jnp.float32)).astype(jnp.bfloat16)
    return (
        dot(a_high, b_high, dims, None) + dot(a_low, b_high, dims, None) + dot(a_high, b_low, dims, None)
    )


def reciprocal(x):
    y = pl.reciprocal(x, approx=True)
    for _ in range(2):
        y = y * (2.0 - x * y)
    return y


def front_kernel(
    total_tokens, sequences, width,
    ids, acts, grad_q, grad_k, grad_v, proj_in, proj_q, proj_k, proj_v,
    factors, grams, query,
    acts_v, gq_v, gk_v, gv_v, pi_v, pq_v, pk_v, pv_v, sem,
):
    tokens = acts.shape[0]
    rows = min(HALF, tokens)
    moves = [(proj_k, pk_v), (grad_k, gk_v), (proj_v, pv_v), (grad_v, gv_v)]
    for first in range(0, tokens, rows):
        for src, dst, table, table_v in ((acts, acts_v, proj_in, pi_v), (grad_q, gq_v, proj_q, pq_v)):
            if first == 0:
                moves.append((table, table_v))
            box = pl.ds(first, rows)
            moves.append((src.at[box], dst.at[box]))
    copies = [pltpu.make_async_copy(src, dst, sem.at[i]) for i, (src, dst) in enumerate(moves)]
    for copy in copies[:IN_FLIGHT]:
        copy.start()
    waited = []

    def arrived(count):
        for _ in range(count):
            i = len(waited)
            copies[i].wait()
            if i + IN_FLIGHT < len(copies):
                copies[i + IN_FLIGHT].start()
            waited.append(i)

    left = lax.broadcasted_iota(jnp.int32, (width, 2 * width), 1) < width
    sums = [None, None]

    def gram_blocks(first, sides):
        coords = jnp.concatenate(sides, axis=0)
        high = coords.astype(jnp.bfloat16)
        low = (coords - high.astype(jnp.float32)).astype(jnp.bfloat16)
        for seq in range(rows // LEN):
            here = slice(seq * LEN, (seq + 1) * LEN)
            one = jnp.concatenate([high[:, here], low[:, here], high[:, here]], axis=1)
            other = jnp.concatenate([high[:, here], high[:, here], low[:, here]], axis=1)
            gram = dot(one, other, NT, None)
            grams[first // LEN + seq] = gram[:width] * (1.0 / LEN)
            squares = [gram[p * width : (p + 1) * width, p // 2 * 2 * width : (p // 2 + 1) * 2 * width] for p in range(4)]
            for i in range(2):
                pair = jnp.where(left, squares[2 * i], squares[2 * i + 1])
                sums[i] = pair if sums[i] is None else sums[i] + pair

    arrived(2)
    coords_k = dot(pk_v[...], gk_v[...], NT, None)
    arrived(2)
    coords_v = dot(pv_v[...], gv_v[...], NT, None)
    ready = None
    for first in range(0, tokens, rows):
        whole = slice(first, first + rows)
        sides = []
        for data, table in ((acts_v, pi_v), (gq_v, pq_v)):
            arrived(2 if first == 0 else 1)
            sides.append(dot(table[...], data[whole], NT, None))
            if ready is not None:
                gram_blocks(*ready)
                ready = None
        ready = first, sides + [coords_k[:, whole], coords_v[:, whole]]
    gram_blocks(*ready)
    upper, lower = sums
    row, column = places(width)
    scale = 1.0 / total_tokens
    factors[:width] = jnp.where(column >= row, upper, lower) * scale
    diagonal = jnp.sum(jnp.where(column == row, lower, 0.0), axis=0, keepdims=True) * scale
    factors[width:] = jnp.broadcast_to(diagonal, (8, 2 * width))
    half = width // 2
    for q in range(query.shape[0]):
        chosen = grams[ids[q]]
        query[q, :width] = chosen[:, 2 * width :]
        in_q = chosen[:, : 2 * width]
        query[q, width:] = jnp.where(left[:half], pltpu.roll(in_q[:half], width, 1), in_q[half:])


def damped(packed):
    order = packed.shape[1] // 2
    half = order // 2
    square, diagonal = packed[:order], packed[order : order + 1]
    row, column = places(order)
    turned = square.T
    turned = jnp.concatenate([turned[:order], turned[order:]], axis=1)
    on_diagonal = column == row
    first = jnp.where(column >= row, square, turned)
    second = jnp.where(column < row, square, turned)
    first_diagonal = jnp.sum(jnp.where(on_diagonal, square, 0.0), axis=0, keepdims=True)
    shape = (LANES, LANES)
    same = (
        lax.broadcasted_iota(jnp.int32, shape, 0) // order
        == lax.broadcasted_iota(jnp.int32, shape, 1) // order
    )
    diagonals = jnp.concatenate([first_diagonal, diagonal], axis=0)
    diagonals = jnp.concatenate([diagonals] * 4, axis=0)
    damping = dot(diagonals, jnp.where(same, 0.1 / order, 0.0), NN)
    first = first + jnp.where(on_diagonal, damping[:1], 0.0)
    second = jnp.where(on_diagonal, diagonal + damping[1:2], second)
    is_low = column < half
    low = jnp.where(is_low, first, pltpu.roll(second, half, 1))
    high = jnp.where(is_low, pltpu.roll(first, LANES - half, 1), second)
    return low, high


def invert(low, high):
    order = low.shape[0]
    half = order // 2
    groups = order // 8
    state = [[x[8 * g : 8 * g + 8] for g in range(groups)] for x in (low, high)]
    lane = lax.broadcasted_iota(jnp.int32, (8, LANES), 1)
    row = lax.broadcasted_iota(jnp.int32, (8, LANES), 0)
    column_of_lane = lane % half
    first_lane = lane - column_of_lane
    for start in range(0, order, PANEL):
        h, first = start // half, start % half
        spread = [
            [jnp.take_along_axis(state[h][g], first_lane + (first + j), axis=1) for g in range(groups)]
            for j in range(PANEL)
        ]
        in_panel = (column_of_lane >= first) & (column_of_lane < first + PANEL)
        state[h] = [jnp.where(in_panel, 0.0, x) for x in state[h]]
        for j in range(PANEL):
            k = start + j
            g, r = k // 8, k % 8
            column = spread[j]
            pivot = reciprocal(column[g][r : r + 1])
            for t in range(2):
                values = state[t][g][r : r + 1]
                if t == h:
                    values = jnp.where(column_of_lane[:1] == first + j, 1.0, values)
                values = values * pivot
                state[t] = [x - c * values for x, c in zip(state[t], column)]
                state[t][g] = jnp.where(row == r, values, state[t][g])
            for i in range(j + 1, PANEL):
                values = spread[i][g][r : r + 1] * pivot
                spread[i] = [x - c * values for x, c in zip(spread[i], column)]
                spread[i][g] = jnp.where(row == r, values, spread[i][g])
    return [jnp.concatenate(state[h], axis=0) for h in range(2)]


def invert_kernel(sequences, width, first, second, grams, train, side_v, left_v):
    half = width // 2
    low, high = invert(*damped(first[...] + second[...]))
    by_lanes = [
        jnp.concatenate([low[:, p * half : (p + 1) * half], high[:, p * half : (p + 1) * half]], axis=1)
        for p in range(4)
    ]
    inverse_in, inverse_k, inverse_q, inverse_v = by_lanes
    side_v[...] = jnp.zeros_like(side_v)
    side_v[width : 2 * width, 2 * width : 3 * width] = inverse_q
    side_v[width : 2 * width, 3 * width :] = inverse_q
    side_v[2 * width : 3 * width, :width] = inverse_k
    side_v[3 * width :, width : 2 * width] = inverse_v
    left_v[...] = dot_split(grams[...].reshape(sequences * width, 4 * width), side_v[...], NN)
    on_left = lax.broadcasted_iota(jnp.int32, (half, 2 * width), 1) < width
    for s in range(sequences):
        done = dot_split(inverse_in, left_v[pl.ds(s * width, width)], NN)
        train[s, :width] = done[:, : 2 * width]
        train[s, width:] = jnp.where(on_left, done[:half, 2 * width :], done[half:, 2 * width :])


def score_kernel(offsets, own, train, *refs):
    blocks, out, partial = refs[:-2], refs[-2], refs[-1]
    me = lax.axis_index("dp")
    slot = 0
    for block in blocks:
        for i in range(block.shape[0]):
            value = block[i]
            place = ((me ^ offsets[slot // own]) * own + slot % own) * 8
            for s in range(train.shape[0]):
                product = (train[s] * value).reshape(-1, 8, train.shape[2])
                partial[s, pl.ds(pl.multiple_of(place, 8), 8)] = jnp.sum(product, axis=0)
            slot += 1
    ones = jnp.ones((8, train.shape[2]), jnp.float32)
    for s in range(train.shape[0]):
        by_query = jnp.sum(partial[s].reshape(-1, 8, train.shape[2]), axis=1)
        out[pl.ds(s, 1)] = dot(ones, by_query, NT)[:1]


def exchange(x, devices, distance):
    return lax.ppermute(x, "dp", [(i, i ^ distance) for i in range(devices)])


def per_device(acts, grad_q, grad_k, grad_v, proj_in, proj_q, proj_k, proj_v, query_ids):
    devices = lax.axis_size("dp")
    steps = devices.bit_length() - 1
    tokens, width = acts.shape[0], proj_in.shape[0]
    sequences, own_queries = tokens // LEN, query_ids.shape[0]
    queries = own_queries * devices
    f32 = jnp.float32
    in_vmem = pl.BlockSpec(memory_space=pltpu.VMEM)
    in_hbm = pl.BlockSpec(memory_space=pltpu.HBM)
    params = pltpu.CompilerParams(vmem_limit_bytes=VMEM_BYTES)
    tables = tuple(
        pltpu.with_memory_space_constraint(t, pltpu.HBM)
        for t in (acts, grad_q, grad_k, grad_v, proj_in, proj_q, proj_k, proj_v)
    )

    factors, grams, query = pl.pallas_call(
        functools.partial(front_kernel, tokens * devices, sequences, width),
        out_shape=(
            jax.ShapeDtypeStruct((width + 8, 2 * width), f32),
            jax.ShapeDtypeStruct((sequences, width, 4 * width), f32),
            jax.ShapeDtypeStruct((own_queries, 3 * width // 2, 2 * width), f32),
        ),
        in_specs=[pl.BlockSpec(memory_space=pltpu.SMEM)] + [in_hbm] * 8,
        out_specs=(in_vmem,) * 3,
        scratch_shapes=[pltpu.VMEM(t.shape, t.dtype) for t in tables]
        + [pltpu.SemaphoreType.DMA((6 + 2 * -(-tokens // HALF),))],
        compiler_params=pltpu.CompilerParams(vmem_limit_bytes=FRONT_VMEM_BYTES),
        name="front",
    )(query_ids, *tables)

    factor_bits = list(range(steps))
    if steps > 2:
        factor_bits[1], factor_bits[2] = 2, 1
    blocks, waiting, sent_queries = [query], None, 0

    def send_query():
        nonlocal sent_queries
        sent = blocks[0] if len(blocks) == 1 else jnp.concatenate(blocks, axis=0)
        sent_queries += 1
        return exchange(sent, devices, 1 << (steps - sent_queries))

    mine = factors
    for step in range(steps):
        theirs = exchange(mine, devices, 1 << factor_bits[step])
        if step == 0:
            waiting = send_query()
        elif step - 1 in OPENS and sent_queries < steps:
            waiting, _ = lax.optimization_barrier((waiting, mine))
            blocks.append(waiting)
            waiting = send_query()
        if step < steps - 1:
            mine = mine + theirs
    terms = (mine, theirs)
    offsets = [
        sum(1 << (steps - 1 - j) for j in range(steps) if slot >> j & 1) for slot in range(devices)
    ]

    while sent_queries < steps:
        waiting, _ = lax.optimization_barrier((waiting, theirs))
        blocks.append(waiting)
        waiting = send_query()
    blocks.append(waiting)

    train = pl.pallas_call(
        functools.partial(invert_kernel, sequences, width),
        out_shape=jax.ShapeDtypeStruct((sequences, 3 * width // 2, 2 * width), f32),
        in_specs=[in_vmem] * 3,
        out_specs=in_vmem,
        scratch_shapes=[
            pltpu.VMEM((4 * width, 4 * width), f32),
            pltpu.VMEM((sequences * width, 4 * width), f32),
        ],
        compiler_params=params,
        name="invert",
    )(*terms, grams)
    return pl.pallas_call(
        functools.partial(score_kernel, offsets, own_queries),
        out_shape=jax.ShapeDtypeStruct((sequences, queries), f32),
        in_specs=[in_vmem] * (1 + len(blocks)),
        out_specs=in_vmem,
        scratch_shapes=[pltpu.VMEM((sequences, queries * 8, 2 * width), f32)],
        compiler_params=params,
        name="scores",
    )(train, *blocks)


def solution(mesh):
    return jax.shard_map(
        per_device,
        mesh=mesh,
        in_specs=(
            P(("group", "dp"), None),
            P(("group", "dp"), None),
            P(("group", "dp"), None),
            P(("group", "dp"), None),
            P(),
            P(),
            P(),
            P(),
            P(("group", "dp")),
        ),
        out_specs=P(("group", "dp"), None),
        check_vma=False,
    )
```

```python
import functools

import jax
import jax.numpy as jnp
from jax import lax
from jax.experimental import pallas as pl
from jax.experimental.pallas import tpu as pltpu
from jax.sharding import PartitionSpec as P

LEN = 128
LANES = 128
PANEL = 8
HALF = 256
IN_FLIGHT = 5
OPENS = (1, 2)
HIGHEST = lax.Precision.HIGHEST
FRONT_VMEM_BYTES = 24 * 1024 * 1024
VMEM_BYTES = 8 * 1024 * 1024
NT = (((1,), (1,)), ((), ()))
TN = (((0,), (0,)), ((), ()))
NN = (((1,), (0,)), ((), ()))


def dot(a, b, dims, precision=HIGHEST):
    return lax.dot_general(a, b, dims, precision=precision, preferred_element_type=jnp.float32)


def places(order):
    shape = (order, 2 * order)
    lane = lax.broadcasted_iota(jnp.int32, shape, 1)
    return lax.broadcasted_iota(jnp.int32, shape, 0), lane % order


def dot_split(a, b, dims):
    a_high, b_high = a.astype(jnp.bfloat16), b.astype(jnp.bfloat16)
    a_low = (a - a_high.astype(jnp.float32)).astype(jnp.bfloat16)
    b_low = (b - b_high.astype(jnp.float32)).astype(jnp.bfloat16)
    return (
        dot(a_high, b_high, dims, None) + dot(a_low, b_high, dims, None) + dot(a_high, b_low, dims, None)
    )


def front_kernel(
    total_tokens, sequences, width,
    ids, acts, grad_q, grad_k, grad_v, proj_in, proj_q, proj_k, proj_v,
    factors, grams, query,
    acts_v, gq_v, gk_v, gv_v, pi_v, pq_v, pk_v, pv_v, sem,
):
    tokens = acts.shape[0]
    rows = min(HALF, tokens)
    moves = [(proj_k, pk_v), (grad_k, gk_v), (proj_v, pv_v), (grad_v, gv_v)]
    for first in range(0, tokens, rows):
        for src, dst, table, table_v in ((acts, acts_v, proj_in, pi_v), (grad_q, gq_v, proj_q, pq_v)):
            if first == 0:
                moves.append((table, table_v))
            box = pl.ds(first, rows)
            moves.append((src.at[box], dst.at[box]))
    copies = [pltpu.make_async_copy(src, dst, sem.at[i]) for i, (src, dst) in enumerate(moves)]
    for copy in copies[:IN_FLIGHT]:
        copy.start()
    waited = []

    def arrived(count):
        for _ in range(count):
            i = len(waited)
            copies[i].wait()
            if i + IN_FLIGHT < len(copies):
                copies[i + IN_FLIGHT].start()
            waited.append(i)

    left = lax.broadcasted_iota(jnp.int32, (width, 2 * width), 1) < width
    sums = [None, None]

    def gram_blocks(first, sides):
        coords = jnp.concatenate(sides, axis=0)
        high = coords.astype(jnp.bfloat16)
        low = (coords - high.astype(jnp.float32)).astype(jnp.bfloat16)
        for seq in range(rows // LEN):
            here = slice(seq * LEN, (seq + 1) * LEN)
            one = jnp.concatenate([high[:, here], low[:, here], high[:, here]], axis=1)
            other = jnp.concatenate([high[:, here], high[:, here], low[:, here]], axis=1)
            gram = dot(one, other, NT, None)
            grams[first // LEN + seq] = gram[:width] * (1.0 / LEN)
            squares = [gram[p * width : (p + 1) * width, p // 2 * 2 * width : (p // 2 + 1) * 2 * width] for p in range(4)]
            for i in range(2):
                pair = jnp.where(left, squares[2 * i], squares[2 * i + 1])
                sums[i] = pair if sums[i] is None else sums[i] + pair

    def projected(table, data, turned):
        return dot(data, table, NT, None).T if turned else dot(table, data, NT, None)

    arrived(4)
    coords_k = projected(pk_v[...], gk_v[...], False)
    coords_v = projected(pv_v[...], gv_v[...], True)
    ready = None
    for first in range(0, tokens, rows):
        whole = slice(first, first + rows)
        arrived(4 if first == 0 else 2)
        sides = [projected(pi_v[...], acts_v[whole], False), projected(pq_v[...], gq_v[whole], True)]
        if ready is not None:
            gram_blocks(*ready)
        ready = first, sides + [coords_k[:, whole], coords_v[:, whole]]
    gram_blocks(*ready)
    upper, lower = sums
    row, column = places(width)
    scale = 1.0 / total_tokens
    factors[:width] = jnp.where(column >= row, upper, lower) * scale
    diagonal = jnp.sum(jnp.where(column == row, lower, 0.0), axis=0, keepdims=True) * scale
    factors[width:] = jnp.broadcast_to(diagonal, (8, 2 * width))
    half = width // 2
    for q in range(query.shape[0]):
        chosen = grams[ids[q]]
        query[q, :width] = chosen[:, 2 * width :]
        in_q = chosen[:, : 2 * width]
        query[q, width:] = jnp.where(left[:half], pltpu.roll(in_q[:half], width, 1), in_q[half:])


def damped(packed):
    order = packed.shape[1] // 2
    half = order // 2
    square, diagonal = packed[:order], packed[order : order + 1]
    row, column = places(order)
    turned = square.T
    turned = jnp.concatenate([turned[:order], turned[order:]], axis=1)
    on_diagonal = column == row
    first = jnp.where(column >= row, square, turned)
    second = jnp.where(column < row, square, turned)
    first_diagonal = jnp.sum(jnp.where(on_diagonal, square, 0.0), axis=0, keepdims=True)
    shape = (LANES, LANES)
    same = (
        lax.broadcasted_iota(jnp.int32, shape, 0) // order
        == lax.broadcasted_iota(jnp.int32, shape, 1) // order
    )
    diagonals = jnp.concatenate([first_diagonal, diagonal], axis=0)
    diagonals = jnp.concatenate([diagonals] * 4, axis=0)
    damping = dot(diagonals, jnp.where(same, 0.1 / order, 0.0), NN)
    first = first + jnp.where(on_diagonal, damping[:1], 0.0)
    second = jnp.where(on_diagonal, diagonal + damping[1:2], second)
    is_low = column < half
    low = jnp.where(is_low, first, pltpu.roll(second, half, 1))
    high = jnp.where(is_low, pltpu.roll(first, LANES - half, 1), second)
    return low, high


def spread_row(x, r):
    return jnp.broadcast_to(x[r : r + 1], x.shape)


def invert(low, high):
    order = low.shape[0]
    half = order // 2
    groups = order // 8
    state = [[x[8 * g : 8 * g + 8] for g in range(groups)] for x in (low, high)]
    lane = lax.broadcasted_iota(jnp.int32, (8, LANES), 1)
    row = lax.broadcasted_iota(jnp.int32, (8, LANES), 0)
    column_of_lane = lane % half
    first_lane = lane - column_of_lane
    for start in range(0, order, PANEL):
        h, first = start // half, start % half
        spread = [
            [jnp.take_along_axis(state[h][g], first_lane + (first + j), axis=1) for g in range(groups)]
            for j in range(PANEL)
        ]
        in_panel = (column_of_lane >= first) & (column_of_lane < first + PANEL)
        state[h] = [jnp.where(in_panel, 0.0, x) for x in state[h]]
        for j in range(0, PANEL, 2):
            k = start + j
            g, r = k // 8, k % 8
            first_column, second_column = spread[j], spread[j + 1]
            a, c = spread_row(first_column[g], r), spread_row(first_column[g], r + 1)
            b, d = spread_row(second_column[g], r), spread_row(second_column[g], r + 1)
            scale = 1.0 / (a * d - b * c)

            def eliminate(x, unit=None):
                top, bottom = spread_row(x[g], r), spread_row(x[g], r + 1)
                if unit is not None:
                    top = jnp.where(column_of_lane == unit, 1.0, top)
                    bottom = jnp.where(column_of_lane == unit + 1, 1.0, bottom)
                one, two = (d * top - b * bottom) * scale, (a * bottom - c * top) * scale
                done = [x[i] - first_column[i] * one - second_column[i] * two for i in range(groups)]
                done[g] = jnp.where(row == r, one, jnp.where(row == r + 1, two, done[g]))
                return done

            state = [eliminate(state[t], first + j if t == h else None) for t in range(2)]
            for i in range(j + 2, PANEL):
                spread[i] = eliminate(spread[i])
    return [jnp.concatenate(state[h], axis=0) for h in range(2)]


def invert_kernel(sequences, width, first, second, grams, train, side_v, left_v):
    half = width // 2
    low, high = invert(*damped(first[...] + second[...]))
    by_lanes = [
        jnp.concatenate([low[:, p * half : (p + 1) * half], high[:, p * half : (p + 1) * half]], axis=1)
        for p in range(4)
    ]
    inverse_in, inverse_k, inverse_q, inverse_v = by_lanes
    side_v[...] = jnp.zeros_like(side_v)
    side_v[width : 2 * width, 2 * width : 3 * width] = inverse_q
    side_v[width : 2 * width, 3 * width :] = inverse_q
    side_v[2 * width : 3 * width, :width] = inverse_k
    side_v[3 * width :, width : 2 * width] = inverse_v
    left_v[...] = dot_split(grams[...].reshape(sequences * width, 4 * width), side_v[...], NN)
    on_left = lax.broadcasted_iota(jnp.int32, (half, 2 * width), 1) < width
    for s in range(sequences):
        done = dot_split(inverse_in, left_v[pl.ds(s * width, width)], NN)
        train[s, :width] = done[:, : 2 * width]
        train[s, width:] = jnp.where(on_left, done[:half, 2 * width :], done[half:, 2 * width :])


def score_kernel(offsets, own, train, *refs):
    blocks, out, partial = refs[:-2], refs[-2], refs[-1]
    me = lax.axis_index("dp")
    slot = 0
    for block in blocks:
        for i in range(block.shape[0]):
            value = block[i]
            place = ((me ^ offsets[slot // own]) * own + slot % own) * 8
            for s in range(train.shape[0]):
                product = (train[s] * value).reshape(-1, 8, train.shape[2])
                partial[s, pl.ds(pl.multiple_of(place, 8), 8)] = jnp.sum(product, axis=0)
            slot += 1
    ones = jnp.ones((8, train.shape[2]), jnp.float32)
    for s in range(train.shape[0]):
        by_query = jnp.sum(partial[s].reshape(-1, 8, train.shape[2]), axis=1)
        out[pl.ds(s, 1)] = dot(ones, by_query, NT)[:1]


def exchange(x, devices, distance):
    return lax.ppermute(x, "dp", [(i, i ^ distance) for i in range(devices)])


def per_device(acts, grad_q, grad_k, grad_v, proj_in, proj_q, proj_k, proj_v, query_ids):
    devices = lax.axis_size("dp")
    steps = devices.bit_length() - 1
    tokens, width = acts.shape[0], proj_in.shape[0]
    sequences, own_queries = tokens // LEN, query_ids.shape[0]
    queries = own_queries * devices
    f32 = jnp.float32
    in_vmem = pl.BlockSpec(memory_space=pltpu.VMEM)
    in_hbm = pl.BlockSpec(memory_space=pltpu.HBM)
    params = pltpu.CompilerParams(vmem_limit_bytes=VMEM_BYTES)
    tables = tuple(
        pltpu.with_memory_space_constraint(t, pltpu.HBM)
        for t in (acts, grad_q, grad_k, grad_v, proj_in, proj_q, proj_k, proj_v)
    )

    factors, grams, query = pl.pallas_call(
        functools.partial(front_kernel, tokens * devices, sequences, width),
        out_shape=(
            jax.ShapeDtypeStruct((width + 8, 2 * width), f32),
            jax.ShapeDtypeStruct((sequences, width, 4 * width), f32),
            jax.ShapeDtypeStruct((own_queries, 3 * width // 2, 2 * width), f32),
        ),
        in_specs=[pl.BlockSpec(memory_space=pltpu.SMEM)] + [in_hbm] * 8,
        out_specs=(in_vmem,) * 3,
        scratch_shapes=[pltpu.VMEM(t.shape, t.dtype) for t in tables]
        + [pltpu.SemaphoreType.DMA((6 + 2 * -(-tokens // HALF),))],
        compiler_params=pltpu.CompilerParams(vmem_limit_bytes=FRONT_VMEM_BYTES),
        name="front",
    )(query_ids, *tables)

    factor_bits = list(range(steps))
    if steps > 2:
        factor_bits[1], factor_bits[2] = 2, 1
    blocks, waiting, sent_queries = [query], None, 0

    def send_query():
        nonlocal sent_queries
        sent = blocks[0] if len(blocks) == 1 else jnp.concatenate(blocks, axis=0)
        sent_queries += 1
        return exchange(sent, devices, 1 << (steps - sent_queries))

    mine = factors
    for step in range(steps):
        theirs = exchange(mine, devices, 1 << factor_bits[step])
        if step == 0:
            waiting = send_query()
        elif step - 1 in OPENS and sent_queries < steps:
            waiting, _ = lax.optimization_barrier((waiting, mine))
            blocks.append(waiting)
            waiting = send_query()
        if step < steps - 1:
            mine = mine + theirs
    terms = (mine, theirs)
    offsets = [
        sum(1 << (steps - 1 - j) for j in range(steps) if slot >> j & 1) for slot in range(devices)
    ]

    while sent_queries < steps:
        waiting, _ = lax.optimization_barrier((waiting, theirs))
        blocks.append(waiting)
        waiting = send_query()
    blocks.append(waiting)

    train = pl.pallas_call(
        functools.partial(invert_kernel, sequences, width),
        out_shape=jax.ShapeDtypeStruct((sequences, 3 * width // 2, 2 * width), f32),
        in_specs=[in_vmem] * 3,
        out_specs=in_vmem,
        scratch_shapes=[
            pltpu.VMEM((4 * width, 4 * width), f32),
            pltpu.VMEM((sequences * width, 4 * width), f32),
        ],
        compiler_params=params,
        name="invert",
    )(*terms, grams)
    return pl.pallas_call(
        functools.partial(score_kernel, offsets, own_queries),
        out_shape=jax.ShapeDtypeStruct((sequences, queries), f32),
        in_specs=[in_vmem] * (1 + len(blocks)),
        out_specs=in_vmem,
        scratch_shapes=[pltpu.VMEM((sequences, queries * 8, 2 * width), f32)],
        compiler_params=params,
        name="scores",
    )(train, *blocks)


def solution(mesh):
    return jax.shard_map(
        per_device,
        mesh=mesh,
        in_specs=(
            P(("group", "dp"), None),
            P(("group", "dp"), None),
            P(("group", "dp"), None),
            P(("group", "dp"), None),
            P(),
            P(),
            P(),
            P(),
            P(("group", "dp")),
        ),
        out_specs=P(("group", "dp"), None),
        check_vma=False,
    )
```

```python
import functools

import jax
import jax.numpy as jnp
from jax import lax
from jax.experimental import pallas as pl
from jax.experimental.pallas import tpu as pltpu
from jax.sharding import PartitionSpec as P

LEN = 128
LANES = 128
PANEL = 8
HALF = 128
IN_FLIGHT = 6
OPENS = (1, 2)
HIGHEST = lax.Precision.HIGHEST
FRONT_VMEM_BYTES = 24 * 1024 * 1024
VMEM_BYTES = 8 * 1024 * 1024
NT = (((1,), (1,)), ((), ()))
TN = (((0,), (0,)), ((), ()))
NN = (((1,), (0,)), ((), ()))


def dot(a, b, dims, precision=HIGHEST):
    return lax.dot_general(a, b, dims, precision=precision, preferred_element_type=jnp.float32)


def places(order):
    shape = (order, 2 * order)
    lane = lax.broadcasted_iota(jnp.int32, shape, 1)
    return lax.broadcasted_iota(jnp.int32, shape, 0), lane % order


def dot_split(a, b, dims):
    a_high, b_high = a.astype(jnp.bfloat16), b.astype(jnp.bfloat16)
    a_low = (a - a_high.astype(jnp.float32)).astype(jnp.bfloat16)
    b_low = (b - b_high.astype(jnp.float32)).astype(jnp.bfloat16)
    return (
        dot(a_high, b_high, dims, None) + dot(a_low, b_high, dims, None) + dot(a_high, b_low, dims, None)
    )


def front_kernel(
    total_tokens, sequences, width,
    ids, acts, grad_q, grad_k, grad_v, proj_in, proj_q, proj_k, proj_v,
    keep, give, grams, query,
    acts_v, gq_v, gk_v, gv_v, pi_v, pq_v, pk_v, pv_v, factors, sem,
):
    tokens = acts.shape[0]
    rows = min(HALF, tokens)
    moves = [(proj_k, pk_v), (grad_k, gk_v), (proj_v, pv_v), (grad_v, gv_v)]
    for first in range(0, tokens, rows):
        for src, dst, table, table_v in ((acts, acts_v, proj_in, pi_v), (grad_q, gq_v, proj_q, pq_v)):
            if first == 0:
                moves.append((table, table_v))
            box = pl.ds(first, rows)
            moves.append((src.at[box], dst.at[box]))
    copies = [pltpu.make_async_copy(src, dst, sem.at[i]) for i, (src, dst) in enumerate(moves)]
    for copy in copies[:IN_FLIGHT]:
        copy.start()
    waited = []

    def arrived(count):
        for _ in range(count):
            i = len(waited)
            copies[i].wait()
            if i + IN_FLIGHT < len(copies):
                copies[i + IN_FLIGHT].start()
            waited.append(i)

    left = lax.broadcasted_iota(jnp.int32, (width, 2 * width), 1) < width
    sums = [None, None]

    def gram_blocks(first, sides):
        coords = jnp.concatenate(sides, axis=0)
        high = coords.astype(jnp.bfloat16)
        low = (coords - high.astype(jnp.float32)).astype(jnp.bfloat16)
        for seq in range(rows // LEN):
            here = slice(seq * LEN, (seq + 1) * LEN)
            one = jnp.concatenate([high[:, here], low[:, here], high[:, here]], axis=1)
            other = jnp.concatenate([high[:, here], high[:, here], low[:, here]], axis=1)
            gram = dot(one, other, NT, None)
            grams[first // LEN + seq] = gram[:width] * (1.0 / LEN)
            squares = [gram[p * width : (p + 1) * width, p // 2 * 2 * width : (p // 2 + 1) * 2 * width] for p in range(4)]
            for i in range(2):
                pair = jnp.where(left, squares[2 * i], squares[2 * i + 1])
                sums[i] = pair if sums[i] is None else sums[i] + pair

    def projected(table, data, turned):
        return dot(data, table, NT, None).T if turned else dot(table, data, NT, None)

    arrived(4)
    coords_k = projected(pk_v[...], gk_v[...], False)
    coords_v = projected(pv_v[...], gv_v[...], True)
    ready = None
    for first in range(0, tokens, rows):
        whole = slice(first, first + rows)
        arrived(4 if first == 0 else 2)
        sides = [projected(pi_v[...], acts_v[whole], False), projected(pq_v[...], gq_v[whole], True)]
        if ready is not None:
            gram_blocks(*ready)
        ready = first, sides + [coords_k[:, whole], coords_v[:, whole]]
    gram_blocks(*ready)
    upper, lower = sums
    row, column = places(width)
    scale = 1.0 / total_tokens
    factors[:width] = jnp.where(column >= row, upper, lower) * scale
    diagonal = jnp.sum(jnp.where(column == row, lower, 0.0), axis=0, keepdims=True) * scale
    factors[width:] = jnp.broadcast_to(diagonal, (factors.shape[0] - width, 2 * width))
    part = keep.shape[0]
    core = lax.axis_index("dp") & 1
    keep[...] = factors[pl.ds(pl.multiple_of(core * part, 8), part)]
    give[...] = factors[pl.ds(pl.multiple_of((1 - core) * part, 8), part)]
    half = width // 2
    for q in range(query.shape[0]):
        chosen = grams[ids[q]]
        query[q, :width] = chosen[:, 2 * width :]
        in_q = chosen[:, : 2 * width]
        query[q, width:] = jnp.where(left[:half], pltpu.roll(in_q[:half], width, 1), in_q[half:])


def damped(packed):
    order = packed.shape[1] // 2
    half = order // 2
    square, diagonal = packed[:order], packed[order : order + 1]
    row, column = places(order)
    turned = square.T
    turned = jnp.concatenate([turned[:order], turned[order:]], axis=1)
    on_diagonal = column == row
    first = jnp.where(column >= row, square, turned)
    second = jnp.where(column < row, square, turned)
    second = jnp.where(on_diagonal, diagonal, second)
    first_diagonal = jnp.sum(jnp.where(on_diagonal, square, 0.0), axis=0, keepdims=True)
    shape = (LANES, LANES)
    same = (
        lax.broadcasted_iota(jnp.int32, shape, 0) // order
        == lax.broadcasted_iota(jnp.int32, shape, 1) // order
    )
    diagonals = jnp.concatenate([first_diagonal, diagonal], axis=0)
    diagonals = jnp.concatenate([diagonals] * 4, axis=0)
    scales = 1.0 / dot(diagonals, jnp.where(same, 1.0 / order, 0.0), NN)
    damping = jnp.where(on_diagonal, 0.1, 0.0)
    first = first * scales[:1] + damping
    second = second * scales[1:2] + damping
    is_low = column < half
    low = jnp.where(is_low, first, pltpu.roll(second, half, 1))
    high = jnp.where(is_low, pltpu.roll(first, LANES - half, 1), second)
    scale = jnp.where(is_low[:8], spread_row(scales, 0), pltpu.roll(spread_row(scales, 1), half, 1))
    return low, high, scale


def spread_row(x, r):
    return jnp.broadcast_to(x[r : r + 1], x.shape)


def invert(low, high, scale):
    order = low.shape[0]
    half = order // 2
    groups = order // 8
    state = [[x[8 * g : 8 * g + 8] for g in range(groups)] for x in (low, high)]
    lane = lax.broadcasted_iota(jnp.int32, (8, LANES), 1)
    row = lax.broadcasted_iota(jnp.int32, (8, LANES), 0)
    column_of_lane = lane % half
    first_lane = lane - column_of_lane
    for start in range(0, order, PANEL):
        h, first = start // half, start % half
        spread = [
            [jnp.take_along_axis(state[h][g], first_lane + (first + j), axis=1) for g in range(groups)]
            for j in range(PANEL)
        ]
        in_panel = (column_of_lane >= first) & (column_of_lane < first + PANEL)
        state[h] = [jnp.where(in_panel, 0.0, x) for x in state[h]]
        for j in range(0, PANEL, 2):
            k = start + j
            g, r = k // 8, k % 8
            first_column, second_column = spread[j], spread[j + 1]
            a, c = spread_row(first_column[g], r), spread_row(first_column[g], r + 1)
            b, d = spread_row(second_column[g], r), spread_row(second_column[g], r + 1)
            inverse_det = 1.0 / (a * d - b * c)

            def eliminate(x, unit=None):
                top, bottom = spread_row(x[g], r), spread_row(x[g], r + 1)
                if unit is not None:
                    top = jnp.where(column_of_lane == unit, 1.0, top)
                    bottom = jnp.where(column_of_lane == unit + 1, 1.0, bottom)
                one, two = (d * top - b * bottom) * inverse_det, (a * bottom - c * top) * inverse_det
                done = [x[i] - first_column[i] * one - second_column[i] * two for i in range(groups)]
                done[g] = jnp.where(row == r, one, jnp.where(row == r + 1, two, done[g]))
                return done

            state = [eliminate(state[t], first + j if t == h else None) for t in range(2)]
            for i in range(j + 2, PANEL):
                spread[i] = eliminate(spread[i])
    return [jnp.concatenate([x * scale for x in half_state], axis=0) for half_state in state]


def invert_kernel(sequences, width, first, second, grams, train, side_v, left_v):
    half = width // 2
    on_zero = lax.axis_index("dp") & 1 == 0
    mine, theirs = first[...], second[...]
    packed = [jnp.where(on_zero, mine, theirs), jnp.where(on_zero, theirs, mine)]
    low, high = invert(*damped(jnp.concatenate(packed, axis=0)))
    by_lanes = [
        jnp.concatenate([low[:, p * half : (p + 1) * half], high[:, p * half : (p + 1) * half]], axis=1)
        for p in range(4)
    ]
    inverse_in, inverse_k, inverse_q, inverse_v = by_lanes
    side_v[...] = jnp.zeros_like(side_v)
    side_v[width : 2 * width, 2 * width : 3 * width] = inverse_q
    side_v[width : 2 * width, 3 * width :] = inverse_q
    side_v[2 * width : 3 * width, :width] = inverse_k
    side_v[3 * width :, width : 2 * width] = inverse_v
    left_v[...] = dot_split(grams[...].reshape(sequences * width, 4 * width), side_v[...], NN)
    on_left = lax.broadcasted_iota(jnp.int32, (half, 2 * width), 1) < width
    for s in range(sequences):
        done = dot_split(inverse_in, left_v[pl.ds(s * width, width)], NN)
        train[s, :width] = done[:, : 2 * width]
        train[s, width:] = jnp.where(on_left, done[:half, 2 * width :], done[half:, 2 * width :])


def score_kernel(offsets, own, train, *refs):
    blocks, out, partial = refs[:-2], refs[-2], refs[-1]
    me = lax.axis_index("dp")
    slot = 0
    for block in blocks:
        for i in range(block.shape[0]):
            value = block[i]
            place = ((me ^ offsets[slot // own]) * own + slot % own) * 8
            for s in range(train.shape[0]):
                product = (train[s] * value).reshape(-1, 8, train.shape[2])
                partial[s, pl.ds(pl.multiple_of(place, 8), 8)] = jnp.sum(product, axis=0)
            slot += 1
    ones = jnp.ones((8, train.shape[2]), jnp.float32)
    for s in range(train.shape[0]):
        by_query = jnp.sum(partial[s].reshape(-1, 8, train.shape[2]), axis=1)
        out[pl.ds(s, 1)] = dot(ones, by_query, NT)[:1]


def exchange(x, devices, distance):
    return lax.ppermute(x, "dp", [(i, i ^ distance) for i in range(devices)])


def per_device(acts, grad_q, grad_k, grad_v, proj_in, proj_q, proj_k, proj_v, query_ids):
    devices = lax.axis_size("dp")
    steps = devices.bit_length() - 1
    tokens, width = acts.shape[0], proj_in.shape[0]
    sequences, own_queries = tokens // LEN, query_ids.shape[0]
    queries = own_queries * devices
    f32 = jnp.float32
    in_vmem = pl.BlockSpec(memory_space=pltpu.VMEM)
    in_hbm = pl.BlockSpec(memory_space=pltpu.HBM)
    params = pltpu.CompilerParams(vmem_limit_bytes=VMEM_BYTES)
    tables = tuple(
        pltpu.with_memory_space_constraint(t, pltpu.HBM)
        for t in (acts, grad_q, grad_k, grad_v, proj_in, proj_q, proj_k, proj_v)
    )

    share = jax.ShapeDtypeStruct((width // 2 + 8, 2 * width), f32)
    keep, give, grams, query = pl.pallas_call(
        functools.partial(front_kernel, tokens * devices, sequences, width),
        out_shape=(
            share,
            share,
            jax.ShapeDtypeStruct((sequences, width, 4 * width), f32),
            jax.ShapeDtypeStruct((own_queries, 3 * width // 2, 2 * width), f32),
        ),
        in_specs=[pl.BlockSpec(memory_space=pltpu.SMEM)] + [in_hbm] * 8,
        out_specs=(in_vmem,) * 4,
        scratch_shapes=[pltpu.VMEM(t.shape, t.dtype) for t in tables]
        + [pltpu.VMEM((width + 16, 2 * width), f32), pltpu.SemaphoreType.DMA((6 + 2 * -(-tokens // HALF),))],
        compiler_params=pltpu.CompilerParams(vmem_limit_bytes=FRONT_VMEM_BYTES),
        name="front",
    )(query_ids, *tables)

    factor_bits = list(range(steps))
    if steps > 2:
        factor_bits[1], factor_bits[2] = 2, 1
    blocks, waiting, sent_queries = [query], None, 0

    def send_query():
        nonlocal sent_queries
        sent = blocks[0] if len(blocks) == 1 else jnp.concatenate(blocks, axis=0)
        sent_queries += 1
        return exchange(sent, devices, 1 << (steps - sent_queries))

    mine = keep
    for step in range(steps):
        theirs = exchange(mine if step else give, devices, 1 << factor_bits[step])
        if step == 0:
            waiting = send_query()
        elif step - 1 in OPENS and sent_queries < steps:
            waiting, _ = lax.optimization_barrier((waiting, mine))
            blocks.append(waiting)
            waiting = send_query()
        mine = mine + theirs
    theirs = exchange(mine, devices, 1)
    terms = (mine, theirs)
    offsets = [
        sum(1 << (steps - 1 - j) for j in range(steps) if slot >> j & 1) for slot in range(devices)
    ]

    while sent_queries < steps:
        waiting, _ = lax.optimization_barrier((waiting, theirs))
        blocks.append(waiting)
        waiting = send_query()
    blocks.append(waiting)

    train = pl.pallas_call(
        functools.partial(invert_kernel, sequences, width),
        out_shape=jax.ShapeDtypeStruct((sequences, 3 * width // 2, 2 * width), f32),
        in_specs=[in_vmem] * 3,
        out_specs=in_vmem,
        scratch_shapes=[
            pltpu.VMEM((4 * width, 4 * width), f32),
            pltpu.VMEM((sequences * width, 4 * width), f32),
        ],
        compiler_params=params,
        name="invert",
    )(*terms, grams)
    return pl.pallas_call(
        functools.partial(score_kernel, offsets, own_queries),
        out_shape=jax.ShapeDtypeStruct((sequences, queries), f32),
        in_specs=[in_vmem] * (1 + len(blocks)),
        out_specs=in_vmem,
        scratch_shapes=[pltpu.VMEM((sequences, queries * 8, 2 * width), f32)],
        compiler_params=params,
        name="scores",
    )(train, *blocks)


def solution(mesh):
    return jax.shard_map(
        per_device,
        mesh=mesh,
        in_specs=(
            P(("group", "dp"), None),
            P(("group", "dp"), None),
            P(("group", "dp"), None),
            P(("group", "dp"), None),
            P(),
            P(),
            P(),
            P(),
            P(("group", "dp")),
        ),
        out_specs=P(("group", "dp"), None),
        check_vma=False,
    )
```

```python
import functools

import jax
import jax.numpy as jnp
from jax import lax
from jax.experimental import pallas as pl
from jax.experimental.pallas import tpu as pltpu
from jax.sharding import PartitionSpec as P

LEN = 128
LANES = 128
PANEL = 8
HALF = 128
IN_FLIGHT = 6
OPENS = (1, 2)
HIGHEST = lax.Precision.HIGHEST
FRONT_VMEM_BYTES = 24 * 1024 * 1024
VMEM_BYTES = 8 * 1024 * 1024
NT = (((1,), (1,)), ((), ()))
TN = (((0,), (0,)), ((), ()))
NN = (((1,), (0,)), ((), ()))


def dot(a, b, dims, precision=HIGHEST):
    return lax.dot_general(a, b, dims, precision=precision, preferred_element_type=jnp.float32)


def places(order):
    shape = (order, 2 * order)
    lane = lax.broadcasted_iota(jnp.int32, shape, 1)
    return lax.broadcasted_iota(jnp.int32, shape, 0), lane % order


def dot_split(a, b, dims):
    a_high, b_high = a.astype(jnp.bfloat16), b.astype(jnp.bfloat16)
    a_low = (a - a_high.astype(jnp.float32)).astype(jnp.bfloat16)
    b_low = (b - b_high.astype(jnp.float32)).astype(jnp.bfloat16)
    return (
        dot(a_high, b_high, dims, None) + dot(a_low, b_high, dims, None) + dot(a_high, b_low, dims, None)
    )


def front_kernel(
    total_tokens, sequences, width,
    ids, acts, grad_q, grad_k, grad_v, proj_in, proj_q, proj_k, proj_v,
    factors, grams, query,
    acts_v, gq_v, gk_v, gv_v, pi_v, pq_v, pk_v, pv_v, sem,
):
    tokens = acts.shape[0]
    rows = min(HALF, tokens)
    moves = [(proj_k, pk_v), (grad_k, gk_v), (proj_v, pv_v), (grad_v, gv_v)]
    for first in range(0, tokens, rows):
        for src, dst, table, table_v in ((acts, acts_v, proj_in, pi_v), (grad_q, gq_v, proj_q, pq_v)):
            if first == 0:
                moves.append((table, table_v))
            box = pl.ds(first, rows)
            moves.append((src.at[box], dst.at[box]))
    copies = [pltpu.make_async_copy(src, dst, sem.at[i]) for i, (src, dst) in enumerate(moves)]
    for copy in copies[:IN_FLIGHT]:
        copy.start()
    waited = []

    def arrived(count):
        for _ in range(count):
            i = len(waited)
            copies[i].wait()
            if i + IN_FLIGHT < len(copies):
                copies[i + IN_FLIGHT].start()
            waited.append(i)

    left = lax.broadcasted_iota(jnp.int32, (width, 2 * width), 1) < width
    sums = [None, None]

    def gram_blocks(first, sides):
        coords = jnp.concatenate(sides, axis=0)
        high = coords.astype(jnp.bfloat16)
        low = (coords - high.astype(jnp.float32)).astype(jnp.bfloat16)
        for seq in range(rows // LEN):
            here = slice(seq * LEN, (seq + 1) * LEN)
            one = jnp.concatenate([high[:, here], low[:, here], high[:, here]], axis=1)
            other = jnp.concatenate([high[:, here], high[:, here], low[:, here]], axis=1)
            gram = dot(one, other, NT, None)
            grams[first // LEN + seq] = gram[:width] * (1.0 / LEN)
            squares = [gram[p * width : (p + 1) * width, p // 2 * 2 * width : (p // 2 + 1) * 2 * width] for p in range(4)]
            for i in range(2):
                pair = jnp.where(left, squares[2 * i], squares[2 * i + 1])
                sums[i] = pair if sums[i] is None else sums[i] + pair

    def projected(table, data, turned):
        return dot(data, table, NT, None).T if turned else dot(table, data, NT, None)

    arrived(4)
    coords_k = projected(pk_v[...], gk_v[...], False)
    coords_v = projected(pv_v[...], gv_v[...], True)
    ready = None
    for first in range(0, tokens, rows):
        whole = slice(first, first + rows)
        arrived(4 if first == 0 else 2)
        sides = [projected(pi_v[...], acts_v[whole], False), projected(pq_v[...], gq_v[whole], True)]
        if ready is not None:
            gram_blocks(*ready)
        ready = first, sides + [coords_k[:, whole], coords_v[:, whole]]
    gram_blocks(*ready)
    upper, lower = sums
    row, column = places(width)
    scale = 1.0 / total_tokens
    factors[:width] = jnp.where(column >= row, upper, lower) * scale
    diagonal = jnp.sum(jnp.where(column == row, lower, 0.0), axis=0, keepdims=True) * scale
    factors[width:] = jnp.broadcast_to(diagonal, (factors.shape[0] - width, 2 * width))
    half = width // 2
    for q in range(query.shape[0]):
        chosen = grams[ids[q]]
        query[q, :width] = chosen[:, 2 * width :]
        in_q = chosen[:, : 2 * width]
        query[q, width:] = jnp.where(left[:half], pltpu.roll(in_q[:half], width, 1), in_q[half:])


def damped(packed):
    order = packed.shape[1] // 2
    half = order // 2
    square, diagonal = packed[:order], packed[order : order + 1]
    row, column = places(order)
    turned = square.T
    turned = jnp.concatenate([turned[:order], turned[order:]], axis=1)
    on_diagonal = column == row
    first = jnp.where(column >= row, square, turned)
    second = jnp.where(column < row, square, turned)
    second = jnp.where(on_diagonal, diagonal, second)
    first_diagonal = jnp.sum(jnp.where(on_diagonal, square, 0.0), axis=0, keepdims=True)
    shape = (LANES, LANES)
    same = (
        lax.broadcasted_iota(jnp.int32, shape, 0) // order
        == lax.broadcasted_iota(jnp.int32, shape, 1) // order
    )
    diagonals = jnp.concatenate([first_diagonal, diagonal], axis=0)
    diagonals = jnp.concatenate([diagonals] * 4, axis=0)
    scales = 1.0 / dot(diagonals, jnp.where(same, 1.0 / order, 0.0), NN)
    damping = jnp.where(on_diagonal, 0.1, 0.0)
    first = first * scales[:1] + damping
    second = second * scales[1:2] + damping
    is_low = column < half
    low = jnp.where(is_low, first, pltpu.roll(second, half, 1))
    high = jnp.where(is_low, pltpu.roll(first, LANES - half, 1), second)
    scale = jnp.where(is_low[:8], spread_row(scales, 0), pltpu.roll(spread_row(scales, 1), half, 1))
    return low, high, scale


def spread_row(x, r):
    return jnp.broadcast_to(x[r : r + 1], x.shape)


def invert(low, high, scale):
    order = low.shape[0]
    half = order // 2
    groups = order // 8
    state = [[x[8 * g : 8 * g + 8] for g in range(groups)] for x in (low, high)]
    lane = lax.broadcasted_iota(jnp.int32, (8, LANES), 1)
    row = lax.broadcasted_iota(jnp.int32, (8, LANES), 0)
    column_of_lane = lane % half
    first_lane = lane - column_of_lane
    for start in range(0, order, PANEL):
        h, first = start // half, start % half
        spread = [
            [jnp.take_along_axis(state[h][g], first_lane + (first + j), axis=1) for g in range(groups)]
            for j in range(PANEL)
        ]
        in_panel = (column_of_lane >= first) & (column_of_lane < first + PANEL)
        state[h] = [jnp.where(in_panel, 0.0, x) for x in state[h]]
        for j in range(0, PANEL, 2):
            k = start + j
            g, r = k // 8, k % 8
            first_column, second_column = spread[j], spread[j + 1]
            a, c = spread_row(first_column[g], r), spread_row(first_column[g], r + 1)
            b, d = spread_row(second_column[g], r), spread_row(second_column[g], r + 1)
            inverse_det = 1.0 / (a * d - b * c)

            def eliminate(x, unit=None):
                top, bottom = spread_row(x[g], r), spread_row(x[g], r + 1)
                if unit is not None:
                    top = jnp.where(column_of_lane == unit, 1.0, top)
                    bottom = jnp.where(column_of_lane == unit + 1, 1.0, bottom)
                one, two = (d * top - b * bottom) * inverse_det, (a * bottom - c * top) * inverse_det
                done = [x[i] - first_column[i] * one - second_column[i] * two for i in range(groups)]
                done[g] = jnp.where(row == r, one, jnp.where(row == r + 1, two, done[g]))
                return done

            state = [eliminate(state[t], first + j if t == h else None) for t in range(2)]
            for i in range(j + 2, PANEL):
                spread[i] = eliminate(spread[i])
    return [jnp.concatenate([x * scale for x in half_state], axis=0) for half_state in state]


def invert_kernel(sequences, width, first, second, grams, train, side_v, left_v):
    half = width // 2
    summed_here = lax.axis_index("dp") & 1 == 1
    low, high = invert(*damped(jnp.where(summed_here, first[...], second[...])))
    by_lanes = [
        jnp.concatenate([low[:, p * half : (p + 1) * half], high[:, p * half : (p + 1) * half]], axis=1)
        for p in range(4)
    ]
    inverse_in, inverse_k, inverse_q, inverse_v = by_lanes
    side_v[...] = jnp.zeros_like(side_v)
    side_v[width : 2 * width, 2 * width : 3 * width] = inverse_q
    side_v[width : 2 * width, 3 * width :] = inverse_q
    side_v[2 * width : 3 * width, :width] = inverse_k
    side_v[3 * width :, width : 2 * width] = inverse_v
    left_v[...] = dot_split(grams[...].reshape(sequences * width, 4 * width), side_v[...], NN)
    on_left = lax.broadcasted_iota(jnp.int32, (half, 2 * width), 1) < width
    for s in range(sequences):
        done = dot_split(inverse_in, left_v[pl.ds(s * width, width)], NN)
        train[s, :width] = done[:, : 2 * width]
        train[s, width:] = jnp.where(on_left, done[:half, 2 * width :], done[half:, 2 * width :])


def score_kernel(offsets, own, train, *refs):
    blocks, out, partial = refs[:-2], refs[-2], refs[-1]
    me = lax.axis_index("dp")
    slot = 0
    for block in blocks:
        for i in range(block.shape[0]):
            value = block[i]
            place = ((me ^ offsets[slot // own]) * own + slot % own) * 8
            for s in range(train.shape[0]):
                product = (train[s] * value).reshape(-1, 8, train.shape[2])
                partial[s, pl.ds(pl.multiple_of(place, 8), 8)] = jnp.sum(product, axis=0)
            slot += 1
    ones = jnp.ones((8, train.shape[2]), jnp.float32)
    for s in range(train.shape[0]):
        by_query = jnp.sum(partial[s].reshape(-1, 8, train.shape[2]), axis=1)
        out[pl.ds(s, 1)] = dot(ones, by_query, NT)[:1]


def exchange(x, devices, distance, core=None):
    moves = [core is None or i % 2 == core for i in range(devices)]
    return lax.ppermute(x, "dp", [(i, i ^ distance if moves[i] else i) for i in range(devices)])


def per_device(acts, grad_q, grad_k, grad_v, proj_in, proj_q, proj_k, proj_v, query_ids):
    devices = lax.axis_size("dp")
    steps = devices.bit_length() - 1
    tokens, width = acts.shape[0], proj_in.shape[0]
    sequences, own_queries = tokens // LEN, query_ids.shape[0]
    queries = own_queries * devices
    f32 = jnp.float32
    in_vmem = pl.BlockSpec(memory_space=pltpu.VMEM)
    in_hbm = pl.BlockSpec(memory_space=pltpu.HBM)
    params = pltpu.CompilerParams(vmem_limit_bytes=VMEM_BYTES)
    tables = tuple(
        pltpu.with_memory_space_constraint(t, pltpu.HBM)
        for t in (acts, grad_q, grad_k, grad_v, proj_in, proj_q, proj_k, proj_v)
    )

    factors, grams, query = pl.pallas_call(
        functools.partial(front_kernel, tokens * devices, sequences, width),
        out_shape=(
            jax.ShapeDtypeStruct((width + 8, 2 * width), f32),
            jax.ShapeDtypeStruct((sequences, width, 4 * width), f32),
            jax.ShapeDtypeStruct((own_queries, 3 * width // 2, 2 * width), f32),
        ),
        in_specs=[pl.BlockSpec(memory_space=pltpu.SMEM)] + [in_hbm] * 8,
        out_specs=(in_vmem,) * 3,
        scratch_shapes=[pltpu.VMEM(t.shape, t.dtype) for t in tables]
        + [pltpu.SemaphoreType.DMA((6 + 2 * -(-tokens // HALF),))],
        compiler_params=pltpu.CompilerParams(vmem_limit_bytes=FRONT_VMEM_BYTES),
        name="front",
    )(query_ids, *tables)

    factor_bits = list(range(steps))
    if steps > 2:
        factor_bits[1], factor_bits[2] = 2, 1
    blocks, waiting, sent_queries = [query], None, 0

    def send_query():
        nonlocal sent_queries
        sent = blocks[0] if len(blocks) == 1 else jnp.concatenate(blocks, axis=0)
        sent_queries += 1
        return exchange(sent, devices, 1 << (steps - sent_queries))

    mine = factors
    for step in range(steps):
        theirs = exchange(mine, devices, 1 << factor_bits[step], core=1 if step else None)
        if step == 0:
            waiting = send_query()
        elif step - 1 in OPENS and sent_queries < steps:
            waiting, _ = lax.optimization_barrier((waiting, mine))
            blocks.append(waiting)
            waiting = send_query()
        mine = mine + theirs
    theirs = exchange(mine, devices, 1)
    terms = (mine, theirs)
    offsets = [
        sum(1 << (steps - 1 - j) for j in range(steps) if slot >> j & 1) for slot in range(devices)
    ]

    while sent_queries < steps:
        waiting, _ = lax.optimization_barrier((waiting, theirs))
        blocks.append(waiting)
        waiting = send_query()
    blocks.append(waiting)

    train = pl.pallas_call(
        functools.partial(invert_kernel, sequences, width),
        out_shape=jax.ShapeDtypeStruct((sequences, 3 * width // 2, 2 * width), f32),
        in_specs=[in_vmem] * 3,
        out_specs=in_vmem,
        scratch_shapes=[
            pltpu.VMEM((4 * width, 4 * width), f32),
            pltpu.VMEM((sequences * width, 4 * width), f32),
        ],
        compiler_params=params,
        name="invert",
    )(*terms, grams)
    return pl.pallas_call(
        functools.partial(score_kernel, offsets, own_queries),
        out_shape=jax.ShapeDtypeStruct((sequences, queries), f32),
        in_specs=[in_vmem] * (1 + len(blocks)),
        out_specs=in_vmem,
        scratch_shapes=[pltpu.VMEM((sequences, queries * 8, 2 * width), f32)],
        compiler_params=params,
        name="scores",
    )(train, *blocks)


def solution(mesh):
    return jax.shard_map(
        per_device,
        mesh=mesh,
        in_specs=(
            P(("group", "dp"), None),
            P(("group", "dp"), None),
            P(("group", "dp"), None),
            P(("group", "dp"), None),
            P(),
            P(),
            P(),
            P(),
            P(("group", "dp")),
        ),
        out_specs=P(("group", "dp"), None),
        check_vma=False,
    )
```

```python
import functools

import jax
import jax.numpy as jnp
from jax import lax
from jax.experimental import pallas as pl
from jax.experimental.pallas import tpu as pltpu
from jax.sharding import PartitionSpec as P

LEN = 128
LANES = 128
PANEL = 8
HALF = 128
IN_FLIGHT = 6
OPENS = (1, 2)
HIGHEST = lax.Precision.HIGHEST
FRONT_VMEM_BYTES = 24 * 1024 * 1024
VMEM_BYTES = 8 * 1024 * 1024
NT = (((1,), (1,)), ((), ()))
TN = (((0,), (0,)), ((), ()))
NN = (((1,), (0,)), ((), ()))


def dot(a, b, dims, precision=HIGHEST):
    return lax.dot_general(a, b, dims, precision=precision, preferred_element_type=jnp.float32)


def places(order):
    shape = (order, 2 * order)
    lane = lax.broadcasted_iota(jnp.int32, shape, 1)
    return lax.broadcasted_iota(jnp.int32, shape, 0), lane % order


def dot_split(a, b, dims):
    a_high, b_high = a.astype(jnp.bfloat16), b.astype(jnp.bfloat16)
    a_low = (a - a_high.astype(jnp.float32)).astype(jnp.bfloat16)
    b_low = (b - b_high.astype(jnp.float32)).astype(jnp.bfloat16)
    return (
        dot(a_high, b_high, dims, None) + dot(a_low, b_high, dims, None) + dot(a_high, b_low, dims, None)
    )


def front_kernel(
    total_tokens, sequences, width,
    ids, acts, grad_q, grad_k, grad_v, proj_in, proj_q, proj_k, proj_v,
    factors, grams, query,
    acts_v, gq_v, gk_v, gv_v, pi_v, pq_v, pk_v, pv_v, sem,
):
    tokens = acts.shape[0]
    rows = min(HALF, tokens)
    moves = [(proj_k, pk_v), (grad_k, gk_v), (proj_v, pv_v), (grad_v, gv_v)]
    for first in range(0, tokens, rows):
        for src, dst, table, table_v in ((acts, acts_v, proj_in, pi_v), (grad_q, gq_v, proj_q, pq_v)):
            if first == 0:
                moves.append((table, table_v))
            box = pl.ds(first, rows)
            moves.append((src.at[box], dst.at[box]))
    copies = [pltpu.make_async_copy(src, dst, sem.at[i]) for i, (src, dst) in enumerate(moves)]
    for copy in copies[:IN_FLIGHT]:
        copy.start()
    waited = []

    def arrived(count):
        for _ in range(count):
            i = len(waited)
            copies[i].wait()
            if i + IN_FLIGHT < len(copies):
                copies[i + IN_FLIGHT].start()
            waited.append(i)

    left = lax.broadcasted_iota(jnp.int32, (width, 2 * width), 1) < width
    sums = [None, None]

    def gram_blocks(first, sides):
        coords = jnp.concatenate(sides, axis=0)
        high = coords.astype(jnp.bfloat16)
        low = (coords - high.astype(jnp.float32)).astype(jnp.bfloat16)
        for seq in range(rows // LEN):
            here = slice(seq * LEN, (seq + 1) * LEN)
            one = jnp.concatenate([high[:, here], low[:, here], high[:, here]], axis=1)
            other = jnp.concatenate([high[:, here], high[:, here], low[:, here]], axis=1)
            gram = dot(one, other, NT, None)
            grams[first // LEN + seq] = gram[:width] * (1.0 / LEN)
            squares = [gram[p * width : (p + 1) * width, p // 2 * 2 * width : (p // 2 + 1) * 2 * width] for p in range(4)]
            for i in range(2):
                pair = jnp.where(left, squares[2 * i], squares[2 * i + 1])
                sums[i] = pair if sums[i] is None else sums[i] + pair

    def projected(table, data, turned):
        return dot(data, table, NT, None).T if turned else dot(table, data, NT, None)

    arrived(4)
    coords_k = projected(pk_v[...], gk_v[...], False)
    coords_v = projected(pv_v[...], gv_v[...], True)
    ready = None
    for first in range(0, tokens, rows):
        whole = slice(first, first + rows)
        arrived(4 if first == 0 else 2)
        sides = [projected(pi_v[...], acts_v[whole], False), projected(pq_v[...], gq_v[whole], True)]
        if ready is not None:
            gram_blocks(*ready)
        ready = first, sides + [coords_k[:, whole], coords_v[:, whole]]
    gram_blocks(*ready)
    upper, lower = sums
    row, column = places(width)
    scale = 1.0 / total_tokens
    factors[:width] = jnp.where(column >= row, upper, lower) * scale
    diagonal = jnp.sum(jnp.where(column == row, lower, 0.0), axis=0, keepdims=True) * scale
    factors[width:] = jnp.broadcast_to(diagonal, (factors.shape[0] - width, 2 * width))
    half = width // 2
    for q in range(query.shape[0]):
        chosen = grams[ids[q]]
        query[q, :width] = chosen[:, 2 * width :]
        in_q = chosen[:, : 2 * width]
        query[q, width:] = jnp.where(left[:half], pltpu.roll(in_q[:half], width, 1), in_q[half:])


def damped(packed):
    order = packed.shape[1] // 2
    half = order // 2
    square, diagonal = packed[:order], packed[order : order + 1]
    row, column = places(order)
    turned = square.T
    turned = jnp.concatenate([turned[:order], turned[order:]], axis=1)
    on_diagonal = column == row
    first = jnp.where(column >= row, square, turned)
    second = jnp.where(column < row, square, turned)
    second = jnp.where(on_diagonal, diagonal, second)
    first_diagonal = jnp.sum(jnp.where(on_diagonal, square, 0.0), axis=0, keepdims=True)
    shape = (LANES, LANES)
    same = (
        lax.broadcasted_iota(jnp.int32, shape, 0) // order
        == lax.broadcasted_iota(jnp.int32, shape, 1) // order
    )
    diagonals = jnp.concatenate([first_diagonal, diagonal], axis=0)
    diagonals = jnp.concatenate([diagonals] * 4, axis=0)
    scales = 1.0 / dot(diagonals, jnp.where(same, 1.0 / order, 0.0), NN)
    damping = jnp.where(on_diagonal, 0.1, 0.0)
    first = first * scales[:1] + damping
    second = second * scales[1:2] + damping
    is_low = column < half
    low = jnp.where(is_low, first, pltpu.roll(second, half, 1))
    high = jnp.where(is_low, pltpu.roll(first, LANES - half, 1), second)
    scale = jnp.where(is_low[:8], spread_row(scales, 0), pltpu.roll(spread_row(scales, 1), half, 1))
    return low, high, scale


def spread_row(x, r):
    return jnp.broadcast_to(x[r : r + 1], x.shape)


def invert(low, high, scale):
    order = low.shape[0]
    half = order // 2
    groups = order // 8
    state = [[x[8 * g : 8 * g + 8] for g in range(groups)] for x in (low, high)]
    lane = lax.broadcasted_iota(jnp.int32, (8, LANES), 1)
    row = lax.broadcasted_iota(jnp.int32, (8, LANES), 0)
    column_of_lane = lane % half
    first_lane = lane - column_of_lane
    for start in range(0, order, PANEL):
        h, first = start // half, start % half
        spread = [
            [jnp.take_along_axis(state[h][g], first_lane + (first + j), axis=1) for g in range(groups)]
            for j in range(PANEL)
        ]
        in_panel = (column_of_lane >= first) & (column_of_lane < first + PANEL)
        state[h] = [jnp.where(in_panel, 0.0, x) for x in state[h]]
        for j in range(0, PANEL, 2):
            k = start + j
            g, r = k // 8, k % 8
            first_column, second_column = spread[j], spread[j + 1]
            a, c = spread_row(first_column[g], r), spread_row(first_column[g], r + 1)
            b, d = spread_row(second_column[g], r), spread_row(second_column[g], r + 1)
            inverse_det = 1.0 / (a * d - b * c)

            def eliminate(x, unit=None):
                top, bottom = spread_row(x[g], r), spread_row(x[g], r + 1)
                if unit is not None:
                    top = jnp.where(column_of_lane == unit, 1.0, top)
                    bottom = jnp.where(column_of_lane == unit + 1, 1.0, bottom)
                one, two = (d * top - b * bottom) * inverse_det, (a * bottom - c * top) * inverse_det
                done = [x[i] - first_column[i] * one - second_column[i] * two for i in range(groups)]
                done[g] = jnp.where(row == r, one, jnp.where(row == r + 1, two, done[g]))
                return done

            state = [eliminate(state[t], first + j if t == h else None) for t in range(2)]
            for i in range(j + 2, PANEL):
                spread[i] = eliminate(spread[i])
    return [jnp.concatenate([x * scale for x in half_state], axis=0) for half_state in state]


def invert_kernel(sequences, width, first, second, grams, train, side_v, left_v):
    half = width // 2
    low, high = invert(*damped(first[...] + second[...]))
    by_lanes = [
        jnp.concatenate([low[:, p * half : (p + 1) * half], high[:, p * half : (p + 1) * half]], axis=1)
        for p in range(4)
    ]
    inverse_in, inverse_k, inverse_q, inverse_v = by_lanes
    side_v[...] = jnp.zeros_like(side_v)
    side_v[width : 2 * width, 2 * width : 3 * width] = inverse_q
    side_v[width : 2 * width, 3 * width :] = inverse_q
    side_v[2 * width : 3 * width, :width] = inverse_k
    side_v[3 * width :, width : 2 * width] = inverse_v
    left_v[...] = dot_split(grams[...].reshape(sequences * width, 4 * width), side_v[...], NN)
    on_left = lax.broadcasted_iota(jnp.int32, (half, 2 * width), 1) < width
    for s in range(sequences):
        done = dot_split(inverse_in, left_v[pl.ds(s * width, width)], NN)
        train[s, :width] = done[:, : 2 * width]
        train[s, width:] = jnp.where(on_left, done[:half, 2 * width :], done[half:, 2 * width :])


def score_kernel(offsets, own, train, *refs):
    blocks, out, partial = refs[:-2], refs[-2], refs[-1]
    me = lax.axis_index("dp")
    slot = 0
    for block in blocks:
        for i in range(block.shape[0]):
            value = block[i]
            place = ((me ^ offsets[slot // own]) * own + slot % own) * 8
            for s in range(train.shape[0]):
                product = (train[s] * value).reshape(-1, 8, train.shape[2])
                partial[s, pl.ds(pl.multiple_of(place, 8), 8)] = jnp.sum(product, axis=0)
            slot += 1
    ones = jnp.ones((8, train.shape[2]), jnp.float32)
    for s in range(train.shape[0]):
        by_query = jnp.sum(partial[s].reshape(-1, 8, train.shape[2]), axis=1)
        out[pl.ds(s, 1)] = dot(ones, by_query, NT)[:1]


def exchange(x, devices, distance):
    return lax.ppermute(x, "dp", [(i, i ^ distance) for i in range(devices)])


def per_device(acts, grad_q, grad_k, grad_v, proj_in, proj_q, proj_k, proj_v, query_ids):
    devices = lax.axis_size("dp")
    steps = devices.bit_length() - 1
    tokens, width = acts.shape[0], proj_in.shape[0]
    sequences, own_queries = tokens // LEN, query_ids.shape[0]
    queries = own_queries * devices
    f32 = jnp.float32
    in_vmem = pl.BlockSpec(memory_space=pltpu.VMEM)
    in_hbm = pl.BlockSpec(memory_space=pltpu.HBM)
    params = pltpu.CompilerParams(vmem_limit_bytes=VMEM_BYTES)
    tables = tuple(
        pltpu.with_memory_space_constraint(t, pltpu.HBM)
        for t in (acts, grad_q, grad_k, grad_v, proj_in, proj_q, proj_k, proj_v)
    )

    factors, grams, query = pl.pallas_call(
        functools.partial(front_kernel, tokens * devices, sequences, width),
        out_shape=(
            jax.ShapeDtypeStruct((width + 8, 2 * width), f32),
            jax.ShapeDtypeStruct((sequences, width, 4 * width), f32),
            jax.ShapeDtypeStruct((own_queries, 3 * width // 2, 2 * width), f32),
        ),
        in_specs=[pl.BlockSpec(memory_space=pltpu.SMEM)] + [in_hbm] * 8,
        out_specs=(in_vmem,) * 3,
        scratch_shapes=[pltpu.VMEM(t.shape, t.dtype) for t in tables]
        + [pltpu.SemaphoreType.DMA((6 + 2 * -(-tokens // HALF),))],
        compiler_params=pltpu.CompilerParams(vmem_limit_bytes=FRONT_VMEM_BYTES),
        name="front",
    )(query_ids, *tables)

    factor_bits = list(range(steps))
    if steps > 2:
        factor_bits[1], factor_bits[2] = 2, 1
    blocks, waiting, sent_queries = [query], None, 0

    def send_query():
        nonlocal sent_queries
        sent = blocks[0] if len(blocks) == 1 else jnp.concatenate(blocks, axis=0)
        sent_queries += 1
        return exchange(sent, devices, 1 << (steps - sent_queries))

    mine = factors
    for step in range(steps):
        theirs = exchange(mine, devices, 1 << factor_bits[step])
        if step == 0:
            waiting = send_query()
        elif step - 1 in OPENS and sent_queries < steps:
            waiting, _ = lax.optimization_barrier((waiting, mine))
            blocks.append(waiting)
            waiting = send_query()
        if step < steps - 1:
            mine = mine + theirs
    terms = (mine, theirs)
    offsets = [
        sum(1 << (steps - 1 - j) for j in range(steps) if slot >> j & 1) for slot in range(devices)
    ]

    while sent_queries < steps:
        waiting, _ = lax.optimization_barrier((waiting, theirs))
        blocks.append(waiting)
        waiting = send_query()
    blocks.append(waiting)

    train = pl.pallas_call(
        functools.partial(invert_kernel, sequences, width),
        out_shape=jax.ShapeDtypeStruct((sequences, 3 * width // 2, 2 * width), f32),
        in_specs=[in_vmem] * 3,
        out_specs=in_vmem,
        scratch_shapes=[
            pltpu.VMEM((4 * width, 4 * width), f32),
            pltpu.VMEM((sequences * width, 4 * width), f32),
        ],
        compiler_params=params,
        name="invert",
    )(*terms, grams)
    return pl.pallas_call(
        functools.partial(score_kernel, offsets, own_queries),
        out_shape=jax.ShapeDtypeStruct((sequences, queries), f32),
        in_specs=[in_vmem] * (1 + len(blocks)),
        out_specs=in_vmem,
        scratch_shapes=[pltpu.VMEM((sequences, queries * 8, 2 * width), f32)],
        compiler_params=params,
        name="scores",
    )(train, *blocks)


def solution(mesh):
    return jax.shard_map(
        per_device,
        mesh=mesh,
        in_specs=(
            P(("group", "dp"), None),
            P(("group", "dp"), None),
            P(("group", "dp"), None),
            P(("group", "dp"), None),
            P(),
            P(),
            P(),
            P(),
            P(("group", "dp")),
        ),
        out_specs=P(("group", "dp"), None),
        check_vma=False,
    )
```

```python
import functools

import jax
import jax.numpy as jnp
from jax import lax
from jax.experimental import pallas as pl
from jax.experimental.pallas import tpu as pltpu
from jax.sharding import PartitionSpec as P

LEN = 128
LANES = 128
PANEL = 8
HALF = 128
IN_FLIGHT = 6
MESSAGES = 4
HIGHEST = lax.Precision.HIGHEST
FRONT_VMEM_BYTES = 24 * 1024 * 1024
VMEM_BYTES = 8 * 1024 * 1024
NT = (((1,), (1,)), ((), ()))
TN = (((0,), (0,)), ((), ()))
NN = (((1,), (0,)), ((), ()))


def dot(a, b, dims, precision=HIGHEST):
    return lax.dot_general(a, b, dims, precision=precision, preferred_element_type=jnp.float32)


def places(order):
    shape = (order, 2 * order)
    lane = lax.broadcasted_iota(jnp.int32, shape, 1)
    return lax.broadcasted_iota(jnp.int32, shape, 0), lane % order


def dot_split(a, b, dims):
    a_high, b_high = a.astype(jnp.bfloat16), b.astype(jnp.bfloat16)
    a_low = (a - a_high.astype(jnp.float32)).astype(jnp.bfloat16)
    b_low = (b - b_high.astype(jnp.float32)).astype(jnp.bfloat16)
    return (
        dot(a_high, b_high, dims, None) + dot(a_low, b_high, dims, None) + dot(a_high, b_low, dims, None)
    )


def front_kernel(
    total_tokens, sequences, width,
    ids, acts, grad_q, grad_k, grad_v, proj_in, proj_q, proj_k, proj_v,
    factors, grams, query,
    acts_v, gq_v, gk_v, gv_v, pi_v, pq_v, pk_v, pv_v, sem,
):
    tokens = acts.shape[0]
    rows = min(HALF, tokens)
    moves = [(proj_k, pk_v), (grad_k, gk_v), (proj_v, pv_v), (grad_v, gv_v)]
    for first in range(0, tokens, rows):
        for src, dst, table, table_v in ((acts, acts_v, proj_in, pi_v), (grad_q, gq_v, proj_q, pq_v)):
            if first == 0:
                moves.append((table, table_v))
            box = pl.ds(first, rows)
            moves.append((src.at[box], dst.at[box]))
    copies = [pltpu.make_async_copy(src, dst, sem.at[i]) for i, (src, dst) in enumerate(moves)]
    for copy in copies[:IN_FLIGHT]:
        copy.start()
    waited = []

    def arrived(count):
        for _ in range(count):
            i = len(waited)
            copies[i].wait()
            if i + IN_FLIGHT < len(copies):
                copies[i + IN_FLIGHT].start()
            waited.append(i)

    left = lax.broadcasted_iota(jnp.int32, (width, 2 * width), 1) < width
    sums = [None, None]

    def gram_blocks(first, sides):
        coords = jnp.concatenate(sides, axis=0)
        high = coords.astype(jnp.bfloat16)
        low = (coords - high.astype(jnp.float32)).astype(jnp.bfloat16)
        for seq in range(rows // LEN):
            here = slice(seq * LEN, (seq + 1) * LEN)
            one = jnp.concatenate([high[:, here], low[:, here], high[:, here]], axis=1)
            other = jnp.concatenate([high[:, here], high[:, here], low[:, here]], axis=1)
            gram = dot(one, other, NT, None)
            grams[first // LEN + seq] = gram[:width] * (1.0 / LEN)
            squares = [gram[p * width : (p + 1) * width, p // 2 * 2 * width : (p // 2 + 1) * 2 * width] for p in range(4)]
            for i in range(2):
                pair = jnp.where(left, squares[2 * i], squares[2 * i + 1])
                sums[i] = pair if sums[i] is None else sums[i] + pair

    def projected(table, data, turned):
        return dot(data, table, NT, None).T if turned else dot(table, data, NT, None)

    arrived(4)
    coords_k = projected(pk_v[...], gk_v[...], False)
    coords_v = projected(pv_v[...], gv_v[...], True)
    ready = None
    for first in range(0, tokens, rows):
        whole = slice(first, first + rows)
        arrived(4 if first == 0 else 2)
        sides = [projected(pi_v[...], acts_v[whole], False), projected(pq_v[...], gq_v[whole], True)]
        if ready is not None:
            gram_blocks(*ready)
        ready = first, sides + [coords_k[:, whole], coords_v[:, whole]]
    gram_blocks(*ready)
    upper, lower = sums
    row, column = places(width)
    scale = 1.0 / total_tokens
    factors[:width] = jnp.where(column >= row, upper, lower) * scale
    diagonal = jnp.sum(jnp.where(column == row, lower, 0.0), axis=0, keepdims=True) * scale
    factors[width:] = jnp.broadcast_to(diagonal, (factors.shape[0] - width, 2 * width))
    half = width // 2
    for q in range(query.shape[0]):
        chosen = grams[ids[q]]
        query[q, :width] = chosen[:, 2 * width :]
        in_q = chosen[:, : 2 * width]
        query[q, width:] = jnp.where(left[:half], pltpu.roll(in_q[:half], width, 1), in_q[half:])


def damped(packed):
    order = packed.shape[1] // 2
    half = order // 2
    square, diagonal = packed[:order], packed[order : order + 1]
    row, column = places(order)
    turned = square.T
    turned = jnp.concatenate([turned[:order], turned[order:]], axis=1)
    on_diagonal = column == row
    first = jnp.where(column >= row, square, turned)
    second = jnp.where(column < row, square, turned)
    second = jnp.where(on_diagonal, diagonal, second)
    first_diagonal = jnp.sum(jnp.where(on_diagonal, square, 0.0), axis=0, keepdims=True)
    shape = (LANES, LANES)
    same = (
        lax.broadcasted_iota(jnp.int32, shape, 0) // order
        == lax.broadcasted_iota(jnp.int32, shape, 1) // order
    )
    diagonals = jnp.concatenate([first_diagonal, diagonal], axis=0)
    diagonals = jnp.concatenate([diagonals] * 4, axis=0)
    scales = 1.0 / dot(diagonals, jnp.where(same, 1.0 / order, 0.0), NN)
    damping = jnp.where(on_diagonal, 0.1, 0.0)
    first = first * scales[:1] + damping
    second = second * scales[1:2] + damping
    is_low = column < half
    low = jnp.where(is_low, first, pltpu.roll(second, half, 1))
    high = jnp.where(is_low, pltpu.roll(first, LANES - half, 1), second)
    scale = jnp.where(is_low[:8], spread_row(scales, 0), pltpu.roll(spread_row(scales, 1), half, 1))
    return low, high, scale


def spread_row(x, r):
    return jnp.broadcast_to(x[r : r + 1], x.shape)


def invert(low, high, scale):
    order = low.shape[0]
    half = order // 2
    groups = order // 8
    state = [[x[8 * g : 8 * g + 8] for g in range(groups)] for x in (low, high)]
    lane = lax.broadcasted_iota(jnp.int32, (8, LANES), 1)
    row = lax.broadcasted_iota(jnp.int32, (8, LANES), 0)
    column_of_lane = lane % half
    first_lane = lane - column_of_lane
    for start in range(0, order, PANEL):
        h, first = start // half, start % half
        spread = [
            [jnp.take_along_axis(state[h][g], first_lane + (first + j), axis=1) for g in range(groups)]
            for j in range(PANEL)
        ]
        in_panel = (column_of_lane >= first) & (column_of_lane < first + PANEL)
        state[h] = [jnp.where(in_panel, 0.0, x) for x in state[h]]
        for j in range(0, PANEL, 2):
            k = start + j
            g, r = k // 8, k % 8
            first_column, second_column = spread[j], spread[j + 1]
            a, c = spread_row(first_column[g], r), spread_row(first_column[g], r + 1)
            b, d = spread_row(second_column[g], r), spread_row(second_column[g], r + 1)
            inverse_det = 1.0 / (a * d - b * c)

            def eliminate(x, unit=None):
                top, bottom = spread_row(x[g], r), spread_row(x[g], r + 1)
                if unit is not None:
                    top = jnp.where(column_of_lane == unit, 1.0, top)
                    bottom = jnp.where(column_of_lane == unit + 1, 1.0, bottom)
                one, two = (d * top - b * bottom) * inverse_det, (a * bottom - c * top) * inverse_det
                done = [x[i] - first_column[i] * one - second_column[i] * two for i in range(groups)]
                done[g] = jnp.where(row == r, one, jnp.where(row == r + 1, two, done[g]))
                return done

            state = [eliminate(state[t], first + j if t == h else None) for t in range(2)]
            for i in range(j + 2, PANEL):
                spread[i] = eliminate(spread[i])
    return [jnp.concatenate([x * scale for x in half_state], axis=0) for half_state in state]


def invert_kernel(sequences, width, first, second, grams, train, side_v, left_v):
    half = width // 2
    low, high = invert(*damped(first[...] + second[...]))
    by_lanes = [
        jnp.concatenate([low[:, p * half : (p + 1) * half], high[:, p * half : (p + 1) * half]], axis=1)
        for p in range(4)
    ]
    inverse_in, inverse_k, inverse_q, inverse_v = by_lanes
    side_v[...] = jnp.zeros_like(side_v)
    side_v[width : 2 * width, 2 * width : 3 * width] = inverse_q
    side_v[width : 2 * width, 3 * width :] = inverse_q
    side_v[2 * width : 3 * width, :width] = inverse_k
    side_v[3 * width :, width : 2 * width] = inverse_v
    left_v[...] = dot_split(grams[...].reshape(sequences * width, 4 * width), side_v[...], NN)
    on_left = lax.broadcasted_iota(jnp.int32, (half, 2 * width), 1) < width
    for s in range(sequences):
        done = dot_split(inverse_in, left_v[pl.ds(s * width, width)], NN)
        train[s, :width] = done[:, : 2 * width]
        train[s, width:] = jnp.where(on_left, done[:half, 2 * width :], done[half:, 2 * width :])


def score_kernel(offsets, own, train, *refs):
    blocks, out, partial = refs[:-2], refs[-2], refs[-1]
    me = lax.axis_index("dp")
    slot = 0
    for block in blocks:
        for i in range(block.shape[0]):
            value = block[i]
            place = ((me ^ offsets[slot // own]) * own + slot % own) * 8
            for s in range(train.shape[0]):
                product = (train[s] * value).reshape(-1, 8, train.shape[2])
                partial[s, pl.ds(pl.multiple_of(place, 8), 8)] = jnp.sum(product, axis=0)
            slot += 1
    ones = jnp.ones((8, train.shape[2]), jnp.float32)
    for s in range(train.shape[0]):
        by_query = jnp.sum(partial[s].reshape(-1, 8, train.shape[2]), axis=1)
        out[pl.ds(s, 1)] = dot(ones, by_query, NT)[:1]


def exchange(x, devices, distance):
    return lax.ppermute(x, "dp", [(i, i ^ distance) for i in range(devices)])


def per_device(acts, grad_q, grad_k, grad_v, proj_in, proj_q, proj_k, proj_v, query_ids):
    devices = lax.axis_size("dp")
    steps = devices.bit_length() - 1
    tokens, width = acts.shape[0], proj_in.shape[0]
    sequences, own_queries = tokens // LEN, query_ids.shape[0]
    queries = own_queries * devices
    f32 = jnp.float32
    in_vmem = pl.BlockSpec(memory_space=pltpu.VMEM)
    in_hbm = pl.BlockSpec(memory_space=pltpu.HBM)
    params = pltpu.CompilerParams(vmem_limit_bytes=VMEM_BYTES)
    tables = tuple(
        pltpu.with_memory_space_constraint(t, pltpu.HBM)
        for t in (acts, grad_q, grad_k, grad_v, proj_in, proj_q, proj_k, proj_v)
    )

    factors, grams, query = pl.pallas_call(
        functools.partial(front_kernel, tokens * devices, sequences, width),
        out_shape=(
            jax.ShapeDtypeStruct((width + 8, 2 * width), f32),
            jax.ShapeDtypeStruct((sequences, width, 4 * width), f32),
            jax.ShapeDtypeStruct((own_queries, 3 * width // 2, 2 * width), f32),
        ),
        in_specs=[pl.BlockSpec(memory_space=pltpu.SMEM)] + [in_hbm] * 8,
        out_specs=(in_vmem,) * 3,
        scratch_shapes=[pltpu.VMEM(t.shape, t.dtype) for t in tables]
        + [pltpu.SemaphoreType.DMA((6 + 2 * -(-tokens // HALF),))],
        compiler_params=pltpu.CompilerParams(vmem_limit_bytes=FRONT_VMEM_BYTES),
        name="front",
    )(query_ids, *tables)

    factor_bits = list(range(steps))
    if steps > 2:
        factor_bits[1], factor_bits[2] = 2, 1
    query_bits = list(range(1, steps))[::-1]

    def send(items, bit):
        size = -(-len(items) // MESSAGES)
        groups = [items[i : i + size] for i in range(0, len(items), size)]
        return [
            (
                exchange(jnp.concatenate([x for x, _ in group], axis=0) if size > 1 else group[0][0], devices, 1 << bit),
                [offset ^ 1 << bit for _, offsets in group for offset in offsets],
            )
            for group in groups
        ]

    def after(items, token):
        arrays = lax.optimization_barrier((*[x for x, _ in items], token))[:-1]
        return [(x, offsets) for x, (_, offsets) in zip(arrays, items)]

    own = [(query, [0])]
    mine, blocks, pending, early = factors, [], [], []
    for step in range(steps):
        theirs = exchange(mine, devices, 1 << factor_bits[step])
        if step == 0:
            pending = send(own, query_bits[0])
        elif step == 1:
            early = send(after(own, mine), query_bits[-1])
        else:
            blocks += after(pending, mine)
            last = step == steps - 1
            pending = send(([] if last else after(own, mine)) + blocks, query_bits[step - 1])
        if step < steps - 1:
            mine = mine + theirs
    blocks = own + blocks + after(pending + early, theirs)
    terms = (mine, theirs)
    everything = jnp.concatenate([x for x, _ in blocks], axis=0)
    offsets = [offset for _, offsets in blocks for offset in offsets]
    blocks = [everything, exchange(everything, devices, 1)]
    offsets += [offset ^ 1 for offset in offsets]

    train = pl.pallas_call(
        functools.partial(invert_kernel, sequences, width),
        out_shape=jax.ShapeDtypeStruct((sequences, 3 * width // 2, 2 * width), f32),
        in_specs=[in_vmem] * 3,
        out_specs=in_vmem,
        scratch_shapes=[
            pltpu.VMEM((4 * width, 4 * width), f32),
            pltpu.VMEM((sequences * width, 4 * width), f32),
        ],
        compiler_params=params,
        name="invert",
    )(*terms, grams)
    return pl.pallas_call(
        functools.partial(score_kernel, offsets, own_queries),
        out_shape=jax.ShapeDtypeStruct((sequences, queries), f32),
        in_specs=[in_vmem] * (1 + len(blocks)),
        out_specs=in_vmem,
        scratch_shapes=[pltpu.VMEM((sequences, queries * 8, 2 * width), f32)],
        compiler_params=params,
        name="scores",
    )(train, *blocks)


def solution(mesh):
    return jax.shard_map(
        per_device,
        mesh=mesh,
        in_specs=(
            P(("group", "dp"), None),
            P(("group", "dp"), None),
            P(("group", "dp"), None),
            P(("group", "dp"), None),
            P(),
            P(),
            P(),
            P(),
            P(("group", "dp")),
        ),
        out_specs=P(("group", "dp"), None),
        check_vma=False,
    )
```

```python
import functools

import jax
import jax.numpy as jnp
from jax import lax
from jax.experimental import pallas as pl
from jax.experimental.pallas import tpu as pltpu
from jax.sharding import PartitionSpec as P

LEN = 128
LANES = 128
PANEL = 8
HALF = 128
IN_FLIGHT = 6
MESSAGES = 4
HIGHEST = lax.Precision.HIGHEST
FRONT_VMEM_BYTES = 24 * 1024 * 1024
VMEM_BYTES = 8 * 1024 * 1024
NT = (((1,), (1,)), ((), ()))
TN = (((0,), (0,)), ((), ()))
NN = (((1,), (0,)), ((), ()))


def dot(a, b, dims, precision=HIGHEST):
    return lax.dot_general(a, b, dims, precision=precision, preferred_element_type=jnp.float32)


def places(order):
    shape = (order, 2 * order)
    lane = lax.broadcasted_iota(jnp.int32, shape, 1)
    return lax.broadcasted_iota(jnp.int32, shape, 0), lane % order


def dot_split(a, b, dims):
    a_high, b_high = a.astype(jnp.bfloat16), b.astype(jnp.bfloat16)
    a_low = (a - a_high.astype(jnp.float32)).astype(jnp.bfloat16)
    b_low = (b - b_high.astype(jnp.float32)).astype(jnp.bfloat16)
    return (
        dot(a_high, b_high, dims, None) + dot(a_low, b_high, dims, None) + dot(a_high, b_low, dims, None)
    )


def front_kernel(
    total_tokens, sequences, width,
    ids, acts, grad_q, grad_k, grad_v, proj_in, proj_q, proj_k, proj_v,
    factors, grams, query,
    acts_v, gq_v, gk_v, gv_v, pi_v, pq_v, pk_v, pv_v, sem,
):
    tokens = acts.shape[0]
    rows = min(HALF, tokens)
    moves = [(proj_k, pk_v), (grad_k, gk_v), (proj_v, pv_v), (grad_v, gv_v)]
    for first in range(0, tokens, rows):
        for src, dst, table, table_v in ((acts, acts_v, proj_in, pi_v), (grad_q, gq_v, proj_q, pq_v)):
            if first == 0:
                moves.append((table, table_v))
            box = pl.ds(first, rows)
            moves.append((src.at[box], dst.at[box]))
    copies = [pltpu.make_async_copy(src, dst, sem.at[i]) for i, (src, dst) in enumerate(moves)]
    for copy in copies[:IN_FLIGHT]:
        copy.start()
    waited = []

    def arrived(count):
        for _ in range(count):
            i = len(waited)
            copies[i].wait()
            if i + IN_FLIGHT < len(copies):
                copies[i + IN_FLIGHT].start()
            waited.append(i)

    left = lax.broadcasted_iota(jnp.int32, (width, 2 * width), 1) < width
    sums = [None, None]

    def gram_blocks(first, sides):
        coords = jnp.concatenate(sides, axis=0)
        high = coords.astype(jnp.bfloat16)
        low = (coords - high.astype(jnp.float32)).astype(jnp.bfloat16)
        for seq in range(rows // LEN):
            here = slice(seq * LEN, (seq + 1) * LEN)
            one = jnp.concatenate([high[:, here], low[:, here], high[:, here]], axis=1)
            other = jnp.concatenate([high[:, here], high[:, here], low[:, here]], axis=1)
            gram = dot(one, other, NT, None)
            grams[first // LEN + seq] = gram[:width] * (1.0 / LEN)
            squares = [gram[p * width : (p + 1) * width, p // 2 * 2 * width : (p // 2 + 1) * 2 * width] for p in range(4)]
            for i in range(2):
                pair = jnp.where(left, squares[2 * i], squares[2 * i + 1])
                sums[i] = pair if sums[i] is None else sums[i] + pair

    def projected(table, data, turned):
        return dot(data, table, NT, None).T if turned else dot(table, data, NT, None)

    arrived(4)
    coords_k = projected(pk_v[...], gk_v[...], False)
    coords_v = projected(pv_v[...], gv_v[...], True)
    ready = None
    for first in range(0, tokens, rows):
        whole = slice(first, first + rows)
        arrived(4 if first == 0 else 2)
        sides = [projected(pi_v[...], acts_v[whole], False), projected(pq_v[...], gq_v[whole], True)]
        if ready is not None:
            gram_blocks(*ready)
        ready = first, sides + [coords_k[:, whole], coords_v[:, whole]]
    gram_blocks(*ready)
    upper, lower = sums
    row, column = places(width)
    scale = 1.0 / total_tokens
    factors[:width] = jnp.where(column >= row, upper, lower) * scale
    diagonal = jnp.sum(jnp.where(column == row, lower, 0.0), axis=0, keepdims=True) * scale
    factors[width:] = jnp.broadcast_to(diagonal, (factors.shape[0] - width, 2 * width))
    half = width // 2
    for q in range(query.shape[0]):
        chosen = grams[ids[q]]
        query[q, :width] = chosen[:, 2 * width :]
        in_q = chosen[:, : 2 * width]
        query[q, width:] = jnp.where(left[:half], pltpu.roll(in_q[:half], width, 1), in_q[half:])


def damped(packed):
    order = packed.shape[1] // 2
    half = order // 2
    square, diagonal = packed[:order], packed[order : order + 1]
    row, column = places(order)
    turned = square.T
    turned = jnp.concatenate([turned[:order], turned[order:]], axis=1)
    on_diagonal = column == row
    first = jnp.where(column >= row, square, turned)
    second = jnp.where(column < row, square, turned)
    second = jnp.where(on_diagonal, diagonal, second)
    first_diagonal = jnp.sum(jnp.where(on_diagonal, square, 0.0), axis=0, keepdims=True)
    shape = (LANES, LANES)
    same = (
        lax.broadcasted_iota(jnp.int32, shape, 0) // order
        == lax.broadcasted_iota(jnp.int32, shape, 1) // order
    )
    diagonals = jnp.concatenate([first_diagonal, diagonal], axis=0)
    diagonals = jnp.concatenate([diagonals] * 4, axis=0)
    scales = 1.0 / dot(diagonals, jnp.where(same, 1.0 / order, 0.0), NN)
    damping = jnp.where(on_diagonal, 0.1, 0.0)
    first = first * scales[:1] + damping
    second = second * scales[1:2] + damping
    is_low = column < half
    low = jnp.where(is_low, first, pltpu.roll(second, half, 1))
    high = jnp.where(is_low, pltpu.roll(first, LANES - half, 1), second)
    scale = jnp.where(is_low[:8], spread_row(scales, 0), pltpu.roll(spread_row(scales, 1), half, 1))
    return low, high, scale


def spread_row(x, r):
    return jnp.broadcast_to(x[r : r + 1], x.shape)


def invert(low, high, scale):
    order = low.shape[0]
    half = order // 2
    groups = order // 8
    state = [[x[8 * g : 8 * g + 8] for g in range(groups)] for x in (low, high)]
    lane = lax.broadcasted_iota(jnp.int32, (8, LANES), 1)
    row = lax.broadcasted_iota(jnp.int32, (8, LANES), 0)
    column_of_lane = lane % half
    first_lane = lane - column_of_lane
    for start in range(0, order, PANEL):
        h, first = start // half, start % half
        spread = [
            [jnp.take_along_axis(state[h][g], first_lane + (first + j), axis=1) for g in range(groups)]
            for j in range(PANEL)
        ]
        in_panel = (column_of_lane >= first) & (column_of_lane < first + PANEL)
        state[h] = [jnp.where(in_panel, 0.0, x) for x in state[h]]
        for j in range(0, PANEL, 2):
            k = start + j
            g, r = k // 8, k % 8
            first_column, second_column = spread[j], spread[j + 1]
            a, c = spread_row(first_column[g], r), spread_row(first_column[g], r + 1)
            b, d = spread_row(second_column[g], r), spread_row(second_column[g], r + 1)
            inverse_det = 1.0 / (a * d - b * c)

            def eliminate(x, unit=None):
                top, bottom = spread_row(x[g], r), spread_row(x[g], r + 1)
                if unit is not None:
                    top = jnp.where(column_of_lane == unit, 1.0, top)
                    bottom = jnp.where(column_of_lane == unit + 1, 1.0, bottom)
                one, two = (d * top - b * bottom) * inverse_det, (a * bottom - c * top) * inverse_det
                done = [x[i] - first_column[i] * one - second_column[i] * two for i in range(groups)]
                done[g] = jnp.where(row == r, one, jnp.where(row == r + 1, two, done[g]))
                return done

            state = [eliminate(state[t], first + j if t == h else None) for t in range(2)]
            for i in range(j + 2, PANEL):
                spread[i] = eliminate(spread[i])
    return [jnp.concatenate([x * scale for x in half_state], axis=0) for half_state in state]


def invert_kernel(sequences, width, first, second, grams, train, side_v, left_v):
    half = width // 2
    low, high = invert(*damped(first[...] + second[...]))
    by_lanes = [
        jnp.concatenate([low[:, p * half : (p + 1) * half], high[:, p * half : (p + 1) * half]], axis=1)
        for p in range(4)
    ]
    inverse_in, inverse_k, inverse_q, inverse_v = by_lanes
    side_v[...] = jnp.zeros_like(side_v)
    side_v[width : 2 * width, 2 * width : 3 * width] = inverse_q
    side_v[width : 2 * width, 3 * width :] = inverse_q
    side_v[2 * width : 3 * width, :width] = inverse_k
    side_v[3 * width :, width : 2 * width] = inverse_v
    left_v[...] = dot_split(grams[...].reshape(sequences * width, 4 * width), side_v[...], NN)
    on_left = lax.broadcasted_iota(jnp.int32, (half, 2 * width), 1) < width
    for s in range(sequences):
        done = dot_split(inverse_in, left_v[pl.ds(s * width, width)], NN)
        train[s, :width] = done[:, : 2 * width]
        train[s, width:] = jnp.where(on_left, done[:half, 2 * width :], done[half:, 2 * width :])


def score_kernel(offsets, own, train, *refs):
    blocks, out, partial = refs[:-2], refs[-2], refs[-1]
    me = lax.axis_index("dp")
    slot = 0
    for block in blocks:
        for i in range(block.shape[0]):
            value = block[i]
            place = ((me ^ offsets[slot // own]) * own + slot % own) * 8
            for s in range(train.shape[0]):
                product = (train[s] * value).reshape(-1, 8, train.shape[2])
                partial[s, pl.ds(pl.multiple_of(place, 8), 8)] = jnp.sum(product, axis=0)
            slot += 1
    ones = jnp.ones((8, train.shape[2]), jnp.float32)
    for s in range(train.shape[0]):
        by_query = jnp.sum(partial[s].reshape(-1, 8, train.shape[2]), axis=1)
        out[pl.ds(s, 1)] = dot(ones, by_query, NT)[:1]


def exchange(x, devices, distance):
    return lax.ppermute(x, "dp", [(i, i ^ distance) for i in range(devices)])


def per_device(acts, grad_q, grad_k, grad_v, proj_in, proj_q, proj_k, proj_v, query_ids):
    devices = lax.axis_size("dp")
    steps = devices.bit_length() - 1
    tokens, width = acts.shape[0], proj_in.shape[0]
    sequences, own_queries = tokens // LEN, query_ids.shape[0]
    queries = own_queries * devices
    f32 = jnp.float32
    in_vmem = pl.BlockSpec(memory_space=pltpu.VMEM)
    in_hbm = pl.BlockSpec(memory_space=pltpu.HBM)
    params = pltpu.CompilerParams(vmem_limit_bytes=VMEM_BYTES)
    tables = tuple(
        pltpu.with_memory_space_constraint(t, pltpu.HBM)
        for t in (acts, grad_q, grad_k, grad_v, proj_in, proj_q, proj_k, proj_v)
    )

    factors, grams, query = pl.pallas_call(
        functools.partial(front_kernel, tokens * devices, sequences, width),
        out_shape=(
            jax.ShapeDtypeStruct((width + 8, 2 * width), f32),
            jax.ShapeDtypeStruct((sequences, width, 4 * width), f32),
            jax.ShapeDtypeStruct((own_queries, 3 * width // 2, 2 * width), f32),
        ),
        in_specs=[pl.BlockSpec(memory_space=pltpu.SMEM)] + [in_hbm] * 8,
        out_specs=(in_vmem,) * 3,
        scratch_shapes=[pltpu.VMEM(t.shape, t.dtype) for t in tables]
        + [pltpu.SemaphoreType.DMA((6 + 2 * -(-tokens // HALF),))],
        compiler_params=pltpu.CompilerParams(vmem_limit_bytes=FRONT_VMEM_BYTES),
        name="front",
    )(query_ids, *tables)

    factor_bits = list(range(steps))
    if steps > 2:
        factor_bits[1], factor_bits[2] = 2, 1
    query_bits = list(range(1, steps))[::-1]

    def send(items, bit):
        size = -(-len(items) // MESSAGES)
        groups = [items[i : i + size] for i in range(0, len(items), size)]
        return [
            (
                exchange(jnp.concatenate([x for x, _ in group], axis=0) if size > 1 else group[0][0], devices, 1 << bit),
                [offset ^ 1 << bit for _, offsets in group for offset in offsets],
            )
            for group in groups
        ]

    def after(items, token):
        arrays = lax.optimization_barrier((*[x for x, _ in items], token))[:-1]
        return [(x, offsets) for x, (_, offsets) in zip(arrays, items)]

    own = [(query, [0])]
    mine, blocks, pending, early = factors, [], [], []
    for step in range(steps):
        theirs = exchange(mine, devices, 1 << factor_bits[step])
        if step == 0:
            pending = send(own, query_bits[0])
        elif step == 1:
            early = send(after(own, mine), query_bits[-1])
        else:
            blocks += after(pending, mine)
            last = step == steps - 1
            pending = send(([] if last else after(own, mine)) + blocks, query_bits[step - 1])
        if step < steps - 1:
            mine = mine + theirs
    terms = (mine, theirs)
    train = pl.pallas_call(
        functools.partial(invert_kernel, sequences, width),
        out_shape=jax.ShapeDtypeStruct((sequences, 3 * width // 2, 2 * width), f32),
        in_specs=[in_vmem] * 3,
        out_specs=in_vmem,
        scratch_shapes=[
            pltpu.VMEM((4 * width, 4 * width), f32),
            pltpu.VMEM((sequences * width, 4 * width), f32),
        ],
        compiler_params=params,
        name="invert",
    )(*terms, grams)
    blocks = own + blocks + after(pending + early, train)
    everything = jnp.concatenate([x for x, _ in blocks], axis=0)
    offsets = [offset for _, offsets in blocks for offset in offsets]
    blocks = [everything, exchange(everything, devices, 1)]
    offsets += [offset ^ 1 for offset in offsets]

    return pl.pallas_call(
        functools.partial(score_kernel, offsets, own_queries),
        out_shape=jax.ShapeDtypeStruct((sequences, queries), f32),
        in_specs=[in_vmem] * (1 + len(blocks)),
        out_specs=in_vmem,
        scratch_shapes=[pltpu.VMEM((sequences, queries * 8, 2 * width), f32)],
        compiler_params=params,
        name="scores",
    )(train, *blocks)


def solution(mesh):
    return jax.shard_map(
        per_device,
        mesh=mesh,
        in_specs=(
            P(("group", "dp"), None),
            P(("group", "dp"), None),
            P(("group", "dp"), None),
            P(("group", "dp"), None),
            P(),
            P(),
            P(),
            P(),
            P(("group", "dp")),
        ),
        out_specs=P(("group", "dp"), None),
        check_vma=False,
    )
```

```python
import functools

import jax
import jax.numpy as jnp
from jax import lax
from jax.experimental import pallas as pl
from jax.experimental.pallas import tpu as pltpu
from jax.sharding import PartitionSpec as P

LEN = 128
LANES = 128
PANEL = 8
HALF = 128
IN_FLIGHT = 6
MESSAGES = 4
HIGHEST = lax.Precision.HIGHEST
FRONT_VMEM_BYTES = 24 * 1024 * 1024
VMEM_BYTES = 8 * 1024 * 1024
NT = (((1,), (1,)), ((), ()))
TN = (((0,), (0,)), ((), ()))
NN = (((1,), (0,)), ((), ()))


def dot(a, b, dims, precision=HIGHEST):
    return lax.dot_general(a, b, dims, precision=precision, preferred_element_type=jnp.float32)


def places(order):
    shape = (order, 2 * order)
    lane = lax.broadcasted_iota(jnp.int32, shape, 1)
    return lax.broadcasted_iota(jnp.int32, shape, 0), lane % order


def dot_split(a, b, dims):
    a_high, b_high = a.astype(jnp.bfloat16), b.astype(jnp.bfloat16)
    a_low = (a - a_high.astype(jnp.float32)).astype(jnp.bfloat16)
    b_low = (b - b_high.astype(jnp.float32)).astype(jnp.bfloat16)
    return (
        dot(a_high, b_high, dims, None) + dot(a_low, b_high, dims, None) + dot(a_high, b_low, dims, None)
    )


def front_kernel(
    total_tokens, sequences, width,
    ids, acts, grad_q, grad_k, grad_v, proj_in, proj_q, proj_k, proj_v,
    factors, grams, query,
    acts_v, gq_v, gk_v, gv_v, pi_v, pq_v, pk_v, pv_v, sem,
):
    tokens = acts.shape[0]
    rows = min(HALF, tokens)
    moves = [(proj_k, pk_v), (grad_k, gk_v), (proj_v, pv_v), (grad_v, gv_v)]
    for first in range(0, tokens, rows):
        for src, dst, table, table_v in ((acts, acts_v, proj_in, pi_v), (grad_q, gq_v, proj_q, pq_v)):
            if first == 0:
                moves.append((table, table_v))
            box = pl.ds(first, rows)
            moves.append((src.at[box], dst.at[box]))
    copies = [pltpu.make_async_copy(src, dst, sem.at[i]) for i, (src, dst) in enumerate(moves)]
    for copy in copies[:IN_FLIGHT]:
        copy.start()
    waited = []

    def arrived(count):
        for _ in range(count):
            i = len(waited)
            copies[i].wait()
            if i + IN_FLIGHT < len(copies):
                copies[i + IN_FLIGHT].start()
            waited.append(i)

    left = lax.broadcasted_iota(jnp.int32, (width, 2 * width), 1) < width
    sums = [None, None]

    def gram_blocks(first, sides):
        coords = jnp.concatenate(sides, axis=0)
        high = coords.astype(jnp.bfloat16)
        low = (coords - high.astype(jnp.float32)).astype(jnp.bfloat16)
        for seq in range(rows // LEN):
            here = slice(seq * LEN, (seq + 1) * LEN)
            one = jnp.concatenate([high[:, here], low[:, here], high[:, here]], axis=1)
            other = jnp.concatenate([high[:, here], high[:, here], low[:, here]], axis=1)
            gram = dot(one, other, NT, None)
            grams[first // LEN + seq] = gram[:width] * (1.0 / LEN)
            squares = [gram[p * width : (p + 1) * width, p // 2 * 2 * width : (p // 2 + 1) * 2 * width] for p in range(4)]
            for i in range(2):
                pair = jnp.where(left, squares[2 * i], squares[2 * i + 1])
                sums[i] = pair if sums[i] is None else sums[i] + pair

    def projected(table, data, turned):
        return dot(data, table, NT, None).T if turned else dot(table, data, NT, None)

    arrived(4)
    coords_k = projected(pk_v[...], gk_v[...], False)
    coords_v = projected(pv_v[...], gv_v[...], True)
    ready = None
    for first in range(0, tokens, rows):
        whole = slice(first, first + rows)
        arrived(4 if first == 0 else 2)
        sides = [projected(pi_v[...], acts_v[whole], False), projected(pq_v[...], gq_v[whole], True)]
        if ready is not None:
            gram_blocks(*ready)
        ready = first, sides + [coords_k[:, whole], coords_v[:, whole]]
    gram_blocks(*ready)
    upper, lower = sums
    row, column = places(width)
    scale = 1.0 / total_tokens
    factors[:width] = jnp.where(column >= row, upper, lower) * scale
    diagonal = jnp.sum(jnp.where(column == row, lower, 0.0), axis=0, keepdims=True) * scale
    factors[width:] = jnp.broadcast_to(diagonal, (factors.shape[0] - width, 2 * width))
    half = width // 2
    for q in range(query.shape[0]):
        chosen = grams[ids[q]]
        query[q, :width] = chosen[:, 2 * width :]
        in_q = chosen[:, : 2 * width]
        query[q, width:] = jnp.where(left[:half], pltpu.roll(in_q[:half], width, 1), in_q[half:])


def damped(packed):
    order = packed.shape[1] // 2
    half = order // 2
    square, diagonal = packed[:order], packed[order : order + 1]
    row, column = places(order)
    turned = square.T
    turned = jnp.concatenate([turned[:order], turned[order:]], axis=1)
    on_diagonal = column == row
    first = jnp.where(column >= row, square, turned)
    second = jnp.where(column < row, square, turned)
    second = jnp.where(on_diagonal, diagonal, second)
    first_diagonal = jnp.sum(jnp.where(on_diagonal, square, 0.0), axis=0, keepdims=True)
    shape = (LANES, LANES)
    same = (
        lax.broadcasted_iota(jnp.int32, shape, 0) // order
        == lax.broadcasted_iota(jnp.int32, shape, 1) // order
    )
    diagonals = jnp.concatenate([first_diagonal, diagonal], axis=0)
    diagonals = jnp.concatenate([diagonals] * 4, axis=0)
    scales = 1.0 / dot(diagonals, jnp.where(same, 1.0 / order, 0.0), NN)
    damping = jnp.where(on_diagonal, 0.1, 0.0)
    first = first * scales[:1] + damping
    second = second * scales[1:2] + damping
    is_low = column < half
    low = jnp.where(is_low, first, pltpu.roll(second, half, 1))
    high = jnp.where(is_low, pltpu.roll(first, LANES - half, 1), second)
    scale = jnp.where(is_low[:8], spread_row(scales, 0), pltpu.roll(spread_row(scales, 1), half, 1))
    return low, high, scale


def spread_row(x, r):
    return jnp.broadcast_to(x[r : r + 1], x.shape)


def invert(low, high, scale):
    order = low.shape[0]
    half = order // 2
    groups = order // 8
    state = [[x[8 * g : 8 * g + 8] for g in range(groups)] for x in (low, high)]
    lane = lax.broadcasted_iota(jnp.int32, (8, LANES), 1)
    row = lax.broadcasted_iota(jnp.int32, (8, LANES), 0)
    column_of_lane = lane % half
    first_lane = lane - column_of_lane
    for start in range(0, order, PANEL):
        h, first = start // half, start % half
        spread = [
            [jnp.take_along_axis(state[h][g], first_lane + (first + j), axis=1) for g in range(groups)]
            for j in range(PANEL)
        ]
        in_panel = (column_of_lane >= first) & (column_of_lane < first + PANEL)
        state[h] = [jnp.where(in_panel, 0.0, x) for x in state[h]]
        for j in range(0, PANEL, 2):
            k = start + j
            g, r = k // 8, k % 8
            first_column, second_column = spread[j], spread[j + 1]
            a, c = spread_row(first_column[g], r), spread_row(first_column[g], r + 1)
            b, d = spread_row(second_column[g], r), spread_row(second_column[g], r + 1)
            inverse_det = 1.0 / (a * d - b * c)

            def eliminate(x, unit=None):
                top, bottom = spread_row(x[g], r), spread_row(x[g], r + 1)
                if unit is not None:
                    top = jnp.where(column_of_lane == unit, 1.0, top)
                    bottom = jnp.where(column_of_lane == unit + 1, 1.0, bottom)
                one, two = (d * top - b * bottom) * inverse_det, (a * bottom - c * top) * inverse_det
                done = [x[i] - first_column[i] * one - second_column[i] * two for i in range(groups)]
                done[g] = jnp.where(row == r, one, jnp.where(row == r + 1, two, done[g]))
                return done

            state = [eliminate(state[t], first + j if t == h else None) for t in range(2)]
            for i in range(j + 2, PANEL):
                spread[i] = eliminate(spread[i])
    return [jnp.concatenate([x * scale for x in half_state], axis=0) for half_state in state]


def invert_kernel(sequences, width, first, second, grams, train, side_v, left_v):
    half = width // 2
    low, high = invert(*damped(first[...] + second[...]))
    by_lanes = [
        jnp.concatenate([low[:, p * half : (p + 1) * half], high[:, p * half : (p + 1) * half]], axis=1)
        for p in range(4)
    ]
    inverse_in, inverse_k, inverse_q, inverse_v = by_lanes
    side_v[...] = jnp.zeros_like(side_v)
    side_v[width : 2 * width, 2 * width : 3 * width] = inverse_q
    side_v[width : 2 * width, 3 * width :] = inverse_q
    side_v[2 * width : 3 * width, :width] = inverse_k
    side_v[3 * width :, width : 2 * width] = inverse_v
    left_v[...] = dot_split(grams[...].reshape(sequences * width, 4 * width), side_v[...], NN)
    on_left = lax.broadcasted_iota(jnp.int32, (half, 2 * width), 1) < width
    for s in range(sequences):
        done = dot_split(inverse_in, left_v[pl.ds(s * width, width)], NN)
        train[s, :width] = done[:, : 2 * width]
        train[s, width:] = jnp.where(on_left, done[:half, 2 * width :], done[half:, 2 * width :])


def score_kernel(offsets, own, train, *refs):
    blocks, out, partial = refs[:-2], refs[-2], refs[-1]
    me = lax.axis_index("dp")
    slot = 0
    for block in blocks:
        for i in range(block.shape[0]):
            value = block[i]
            place = ((me ^ offsets[slot // own]) * own + slot % own) * 8
            for s in range(train.shape[0]):
                product = (train[s] * value).reshape(-1, 8, train.shape[2])
                partial[s, pl.ds(pl.multiple_of(place, 8), 8)] = jnp.sum(product, axis=0)
            slot += 1
    ones = jnp.ones((8, train.shape[2]), jnp.float32)
    for s in range(train.shape[0]):
        by_query = jnp.sum(partial[s].reshape(-1, 8, train.shape[2]), axis=1)
        out[pl.ds(s, 1)] = dot(ones, by_query, NT)[:1]


def exchange(x, devices, distance):
    return lax.ppermute(x, "dp", [(i, i ^ distance) for i in range(devices)])


def per_device(acts, grad_q, grad_k, grad_v, proj_in, proj_q, proj_k, proj_v, query_ids):
    devices = lax.axis_size("dp")
    steps = devices.bit_length() - 1
    tokens, width = acts.shape[0], proj_in.shape[0]
    sequences, own_queries = tokens // LEN, query_ids.shape[0]
    queries = own_queries * devices
    f32 = jnp.float32
    in_vmem = pl.BlockSpec(memory_space=pltpu.VMEM)
    in_hbm = pl.BlockSpec(memory_space=pltpu.HBM)
    params = pltpu.CompilerParams(vmem_limit_bytes=VMEM_BYTES)
    tables = tuple(
        pltpu.with_memory_space_constraint(t, pltpu.HBM)
        for t in (acts, grad_q, grad_k, grad_v, proj_in, proj_q, proj_k, proj_v)
    )

    factors, grams, query = pl.pallas_call(
        functools.partial(front_kernel, tokens * devices, sequences, width),
        out_shape=(
            jax.ShapeDtypeStruct((width + 8, 2 * width), f32),
            jax.ShapeDtypeStruct((sequences, width, 4 * width), f32),
            jax.ShapeDtypeStruct((own_queries, 3 * width // 2, 2 * width), f32),
        ),
        in_specs=[pl.BlockSpec(memory_space=pltpu.SMEM)] + [in_hbm] * 8,
        out_specs=(in_vmem,) * 3,
        scratch_shapes=[pltpu.VMEM(t.shape, t.dtype) for t in tables]
        + [pltpu.SemaphoreType.DMA((6 + 2 * -(-tokens // HALF),))],
        compiler_params=pltpu.CompilerParams(vmem_limit_bytes=FRONT_VMEM_BYTES),
        name="front",
    )(query_ids, *tables)

    query_bits = list(range(1, steps))[::-1]

    def send(items, bit):
        size = -(-len(items) // MESSAGES)
        groups = [items[i : i + size] for i in range(0, len(items), size)]
        return [
            (
                exchange(jnp.concatenate([x for x, _ in group], axis=0) if size > 1 else group[0][0], devices, 1 << bit),
                [offset ^ 1 << bit for _, offsets in group for offset in offsets],
            )
            for group in groups
        ]

    def after(items, token):
        arrays = lax.optimization_barrier((*[x for x, _ in items], token))[:-1]
        return [(x, offsets) for x, (_, offsets) in zip(arrays, items)]

    own = [(query, [0])]
    mine, blocks, pending, early = factors, [], [], []
    for step in range(steps):
        theirs = exchange(mine, devices, 1 << step)
        if step == 0:
            pending = send(own, query_bits[0])
        elif step > 1:
            if step == 2:
                early = send(after(own, mine), query_bits[-1])
            blocks += after(pending, mine)
            last = step == steps - 1
            pending = send(([] if last else after(own, mine)) + blocks, query_bits[step - 1])
        if step < steps - 1:
            mine = mine + theirs
    terms = (mine, theirs)
    train = pl.pallas_call(
        functools.partial(invert_kernel, sequences, width),
        out_shape=jax.ShapeDtypeStruct((sequences, 3 * width // 2, 2 * width), f32),
        in_specs=[in_vmem] * 3,
        out_specs=in_vmem,
        scratch_shapes=[
            pltpu.VMEM((4 * width, 4 * width), f32),
            pltpu.VMEM((sequences * width, 4 * width), f32),
        ],
        compiler_params=params,
        name="invert",
    )(*terms, grams)
    blocks = own + blocks + after(pending + early, train)
    everything = jnp.concatenate([x for x, _ in blocks], axis=0)
    offsets = [offset for _, offsets in blocks for offset in offsets]
    blocks = [everything, exchange(everything, devices, 1)]
    offsets += [offset ^ 1 for offset in offsets]

    return pl.pallas_call(
        functools.partial(score_kernel, offsets, own_queries),
        out_shape=jax.ShapeDtypeStruct((sequences, queries), f32),
        in_specs=[in_vmem] * (1 + len(blocks)),
        out_specs=in_vmem,
        scratch_shapes=[pltpu.VMEM((sequences, queries * 8, 2 * width), f32)],
        compiler_params=params,
        name="scores",
    )(train, *blocks)


def solution(mesh):
    return jax.shard_map(
        per_device,
        mesh=mesh,
        in_specs=(
            P(("group", "dp"), None),
            P(("group", "dp"), None),
            P(("group", "dp"), None),
            P(("group", "dp"), None),
            P(),
            P(),
            P(),
            P(),
            P(("group", "dp")),
        ),
        out_specs=P(("group", "dp"), None),
        check_vma=False,
    )
```

```python
import functools

import jax
import jax.numpy as jnp
from jax import lax
from jax.experimental import pallas as pl
from jax.experimental.pallas import tpu as pltpu
from jax.sharding import PartitionSpec as P

LEN = 128
LANES = 128
PANEL = 8
HALF = 128
IN_FLIGHT = 6
MESSAGES = 4
HIGHEST = lax.Precision.HIGHEST
FRONT_VMEM_BYTES = 24 * 1024 * 1024
VMEM_BYTES = 8 * 1024 * 1024
NT = (((1,), (1,)), ((), ()))
TN = (((0,), (0,)), ((), ()))
NN = (((1,), (0,)), ((), ()))


def dot(a, b, dims, precision=HIGHEST):
    return lax.dot_general(a, b, dims, precision=precision, preferred_element_type=jnp.float32)


def places(order):
    shape = (order, 2 * order)
    lane = lax.broadcasted_iota(jnp.int32, shape, 1)
    return lax.broadcasted_iota(jnp.int32, shape, 0), lane % order


def dot_split(a, b, dims):
    a_high, b_high = a.astype(jnp.bfloat16), b.astype(jnp.bfloat16)
    a_low = (a - a_high.astype(jnp.float32)).astype(jnp.bfloat16)
    b_low = (b - b_high.astype(jnp.float32)).astype(jnp.bfloat16)
    return (
        dot(a_high, b_high, dims, None) + dot(a_low, b_high, dims, None) + dot(a_high, b_low, dims, None)
    )


def front_kernel(
    total_tokens, sequences, width,
    ids, acts, grad_q, grad_k, grad_v, proj_in, proj_q, proj_k, proj_v,
    factors, grams, query,
    acts_v, gq_v, gk_v, gv_v, pi_v, pq_v, pk_v, pv_v, sem,
):
    tokens = acts.shape[0]
    rows = min(HALF, tokens)
    moves = [(proj_k, pk_v), (grad_k, gk_v), (proj_v, pv_v), (grad_v, gv_v)]
    for first in range(0, tokens, rows):
        for src, dst, table, table_v in ((acts, acts_v, proj_in, pi_v), (grad_q, gq_v, proj_q, pq_v)):
            if first == 0:
                moves.append((table, table_v))
            box = pl.ds(first, rows)
            moves.append((src.at[box], dst.at[box]))
    copies = [pltpu.make_async_copy(src, dst, sem.at[i]) for i, (src, dst) in enumerate(moves)]
    for copy in copies[:IN_FLIGHT]:
        copy.start()
    waited = []

    def arrived(count):
        for _ in range(count):
            i = len(waited)
            copies[i].wait()
            if i + IN_FLIGHT < len(copies):
                copies[i + IN_FLIGHT].start()
            waited.append(i)

    left = lax.broadcasted_iota(jnp.int32, (width, 2 * width), 1) < width
    sums = [None, None]

    def gram_blocks(first, sides):
        coords = jnp.concatenate(sides, axis=0)
        high = coords.astype(jnp.bfloat16)
        low = (coords - high.astype(jnp.float32)).astype(jnp.bfloat16)
        for seq in range(rows // LEN):
            here = slice(seq * LEN, (seq + 1) * LEN)
            one = jnp.concatenate([high[:, here], low[:, here], high[:, here]], axis=1)
            other = jnp.concatenate([high[:, here], high[:, here], low[:, here]], axis=1)
            gram = dot(one, other, NT, None)
            grams[first // LEN + seq] = gram[:width] * (1.0 / LEN)
            squares = [gram[p * width : (p + 1) * width, p // 2 * 2 * width : (p // 2 + 1) * 2 * width] for p in range(4)]
            for i in range(2):
                pair = jnp.where(left, squares[2 * i], squares[2 * i + 1])
                sums[i] = pair if sums[i] is None else sums[i] + pair

    def projected(table, data, turned):
        return dot(data, table, NT, None).T if turned else dot(table, data, NT, None)

    arrived(4)
    coords_k = projected(pk_v[...], gk_v[...], False)
    coords_v = projected(pv_v[...], gv_v[...], True)
    ready = None
    for first in range(0, tokens, rows):
        whole = slice(first, first + rows)
        arrived(4 if first == 0 else 2)
        sides = [projected(pi_v[...], acts_v[whole], False), projected(pq_v[...], gq_v[whole], True)]
        if ready is not None:
            gram_blocks(*ready)
        ready = first, sides + [coords_k[:, whole], coords_v[:, whole]]
    gram_blocks(*ready)
    upper, lower = sums
    row, column = places(width)
    scale = 1.0 / total_tokens
    factors[:width] = jnp.where(column >= row, upper, lower) * scale
    diagonal = jnp.sum(jnp.where(column == row, lower, 0.0), axis=0, keepdims=True) * scale
    factors[width:] = jnp.broadcast_to(diagonal, (factors.shape[0] - width, 2 * width))
    half = width // 2
    for q in range(query.shape[0]):
        chosen = grams[ids[q]]
        query[q, :width] = chosen[:, 2 * width :]
        in_q = chosen[:, : 2 * width]
        query[q, width:] = jnp.where(left[:half], pltpu.roll(in_q[:half], width, 1), in_q[half:])


def damped(packed):
    order = packed.shape[1] // 2
    half = order // 2
    square, diagonal = packed[:order], packed[order : order + 1]
    row, column = places(order)
    turned = square.T
    turned = jnp.concatenate([turned[:order], turned[order:]], axis=1)
    on_diagonal = column == row
    first = jnp.where(column >= row, square, turned)
    second = jnp.where(column < row, square, turned)
    second = jnp.where(on_diagonal, diagonal, second)
    first_diagonal = jnp.sum(jnp.where(on_diagonal, square, 0.0), axis=0, keepdims=True)
    shape = (LANES, LANES)
    same = (
        lax.broadcasted_iota(jnp.int32, shape, 0) // order
        == lax.broadcasted_iota(jnp.int32, shape, 1) // order
    )
    diagonals = jnp.concatenate([first_diagonal, diagonal], axis=0)
    diagonals = jnp.concatenate([diagonals] * 4, axis=0)
    scales = 1.0 / dot(diagonals, jnp.where(same, 1.0 / order, 0.0), NN)
    damping = jnp.where(on_diagonal, 0.1, 0.0)
    first = first * scales[:1] + damping
    second = second * scales[1:2] + damping
    is_low = column < half
    low = jnp.where(is_low, first, pltpu.roll(second, half, 1))
    high = jnp.where(is_low, pltpu.roll(first, LANES - half, 1), second)
    scale = jnp.where(is_low[:8], spread_row(scales, 0), pltpu.roll(spread_row(scales, 1), half, 1))
    return low, high, scale


def spread_row(x, r):
    return jnp.broadcast_to(x[r : r + 1], x.shape)


def invert(low, high, scale):
    order = low.shape[0]
    half = order // 2
    groups = order // 8
    state = [[x[8 * g : 8 * g + 8] for g in range(groups)] for x in (low, high)]
    lane = lax.broadcasted_iota(jnp.int32, (8, LANES), 1)
    row = lax.broadcasted_iota(jnp.int32, (8, LANES), 0)
    column_of_lane = lane % half
    first_lane = lane - column_of_lane
    for start in range(0, order, PANEL):
        h, first = start // half, start % half
        spread = [
            [jnp.take_along_axis(state[h][g], first_lane + (first + j), axis=1) for g in range(groups)]
            for j in range(PANEL)
        ]
        in_panel = (column_of_lane >= first) & (column_of_lane < first + PANEL)
        state[h] = [jnp.where(in_panel, 0.0, x) for x in state[h]]
        for j in range(0, PANEL, 2):
            k = start + j
            g, r = k // 8, k % 8
            first_column, second_column = spread[j], spread[j + 1]
            a, c = spread_row(first_column[g], r), spread_row(first_column[g], r + 1)
            b, d = spread_row(second_column[g], r), spread_row(second_column[g], r + 1)
            inverse_det = 1.0 / (a * d - b * c)

            def eliminate(x, unit=None):
                top, bottom = spread_row(x[g], r), spread_row(x[g], r + 1)
                if unit is not None:
                    top = jnp.where(column_of_lane == unit, 1.0, top)
                    bottom = jnp.where(column_of_lane == unit + 1, 1.0, bottom)
                one, two = (d * top - b * bottom) * inverse_det, (a * bottom - c * top) * inverse_det
                done = [x[i] - first_column[i] * one - second_column[i] * two for i in range(groups)]
                done[g] = jnp.where(row == r, one, jnp.where(row == r + 1, two, done[g]))
                return done

            state = [eliminate(state[t], first + j if t == h else None) for t in range(2)]
            for i in range(j + 2, PANEL):
                spread[i] = eliminate(spread[i])
    return [jnp.concatenate([x * scale for x in half_state], axis=0) for half_state in state]


def invert_kernel(sequences, width, first, second, grams, train, side_v, left_v):
    half = width // 2
    low, high = invert(*damped(first[...] + second[...]))
    by_lanes = [
        jnp.concatenate([low[:, p * half : (p + 1) * half], high[:, p * half : (p + 1) * half]], axis=1)
        for p in range(4)
    ]
    inverse_in, inverse_k, inverse_q, inverse_v = by_lanes
    side_v[...] = jnp.zeros_like(side_v)
    side_v[width : 2 * width, 2 * width : 3 * width] = inverse_q
    side_v[width : 2 * width, 3 * width :] = inverse_q
    side_v[2 * width : 3 * width, :width] = inverse_k
    side_v[3 * width :, width : 2 * width] = inverse_v
    left_v[...] = dot_split(grams[...].reshape(sequences * width, 4 * width), side_v[...], NN)
    on_left = lax.broadcasted_iota(jnp.int32, (half, 2 * width), 1) < width
    for s in range(sequences):
        done = dot_split(inverse_in, left_v[pl.ds(s * width, width)], NN)
        train[s, :width] = done[:, : 2 * width]
        train[s, width:] = jnp.where(on_left, done[:half, 2 * width :], done[half:, 2 * width :])


def score_kernel(offsets, own, train, *refs):
    blocks, out, partial = refs[:-2], refs[-2], refs[-1]
    me = lax.axis_index("dp")
    slot = 0
    for block in blocks:
        for i in range(block.shape[0]):
            value = block[i]
            place = ((me ^ offsets[slot // own]) * own + slot % own) * 8
            for s in range(train.shape[0]):
                product = (train[s] * value).reshape(-1, 8, train.shape[2])
                partial[s, pl.ds(pl.multiple_of(place, 8), 8)] = jnp.sum(product, axis=0)
            slot += 1
    ones = jnp.ones((8, train.shape[2]), jnp.float32)
    for s in range(train.shape[0]):
        by_query = jnp.sum(partial[s].reshape(-1, 8, train.shape[2]), axis=1)
        out[pl.ds(s, 1)] = dot(ones, by_query, NT)[:1]


def exchange(x, devices, distance):
    return lax.ppermute(x, "dp", [(i, i ^ distance) for i in range(devices)])


def per_device(acts, grad_q, grad_k, grad_v, proj_in, proj_q, proj_k, proj_v, query_ids):
    devices = lax.axis_size("dp")
    steps = devices.bit_length() - 1
    tokens, width = acts.shape[0], proj_in.shape[0]
    sequences, own_queries = tokens // LEN, query_ids.shape[0]
    queries = own_queries * devices
    f32 = jnp.float32
    in_vmem = pl.BlockSpec(memory_space=pltpu.VMEM)
    in_hbm = pl.BlockSpec(memory_space=pltpu.HBM)
    params = pltpu.CompilerParams(vmem_limit_bytes=VMEM_BYTES)
    tables = tuple(
        pltpu.with_memory_space_constraint(t, pltpu.HBM)
        for t in (acts, grad_q, grad_k, grad_v, proj_in, proj_q, proj_k, proj_v)
    )

    factors, grams, query = pl.pallas_call(
        functools.partial(front_kernel, tokens * devices, sequences, width),
        out_shape=(
            jax.ShapeDtypeStruct((width + 8, 2 * width), f32),
            jax.ShapeDtypeStruct((sequences, width, 4 * width), f32),
            jax.ShapeDtypeStruct((own_queries, 3 * width // 2, 2 * width), f32),
        ),
        in_specs=[pl.BlockSpec(memory_space=pltpu.SMEM)] + [in_hbm] * 8,
        out_specs=(in_vmem,) * 3,
        scratch_shapes=[pltpu.VMEM(t.shape, t.dtype) for t in tables]
        + [pltpu.SemaphoreType.DMA((6 + 2 * -(-tokens // HALF),))],
        compiler_params=pltpu.CompilerParams(vmem_limit_bytes=FRONT_VMEM_BYTES),
        name="front",
    )(query_ids, *tables)

    query_bits = list(range(1, steps))[::-1]

    def send(items, bit):
        size = -(-len(items) // MESSAGES)
        groups = [items[i : i + size] for i in range(0, len(items), size)]
        return [
            (
                exchange(jnp.concatenate([x for x, _ in group], axis=0) if size > 1 else group[0][0], devices, 1 << bit),
                [offset ^ 1 << bit for _, offsets in group for offset in offsets],
            )
            for group in groups
        ]

    def after(items, token):
        arrays = lax.optimization_barrier((*[x for x, _ in items], token))[:-1]
        return [(x, offsets) for x, (_, offsets) in zip(arrays, items)]

    def both_cores(items):
        joined = jnp.concatenate([x for x, _ in items], axis=0)
        offsets = [offset for _, part in items for offset in part]
        return [(joined, offsets), (exchange(joined, devices, 1), [offset ^ 1 for offset in offsets])]

    own = [(query, [0])]
    mine, blocks, pending, early = factors, [], [], []
    for step in range(steps):
        theirs = exchange(mine, devices, 1 << step)
        if step == 0:
            pending = send(own, query_bits[0])
        elif step == 1:
            early = send(after(own, mine), query_bits[-1])
        else:
            blocks += after(pending, mine)
            last = step == steps - 1
            pending = send(([] if last else after(own, mine)) + blocks, query_bits[step - 1])
            if last:
                first = both_cores(own + blocks)
        if step < steps - 1:
            mine = mine + theirs
    terms = (mine, theirs)
    train = pl.pallas_call(
        functools.partial(invert_kernel, sequences, width),
        out_shape=jax.ShapeDtypeStruct((sequences, 3 * width // 2, 2 * width), f32),
        in_specs=[in_vmem] * 3,
        out_specs=in_vmem,
        scratch_shapes=[
            pltpu.VMEM((4 * width, 4 * width), f32),
            pltpu.VMEM((sequences * width, 4 * width), f32),
        ],
        compiler_params=params,
        name="invert",
    )(*terms, grams)
    last = both_cores(after(pending + early, train))
    blocks = [x for x, _ in first + last]
    offsets = [offset for _, offsets in first + last for offset in offsets]

    return pl.pallas_call(
        functools.partial(score_kernel, offsets, own_queries),
        out_shape=jax.ShapeDtypeStruct((sequences, queries), f32),
        in_specs=[in_vmem] * (1 + len(blocks)),
        out_specs=in_vmem,
        scratch_shapes=[pltpu.VMEM((sequences, queries * 8, 2 * width), f32)],
        compiler_params=params,
        name="scores",
    )(train, *blocks)


def solution(mesh):
    return jax.shard_map(
        per_device,
        mesh=mesh,
        in_specs=(
            P(("group", "dp"), None),
            P(("group", "dp"), None),
            P(("group", "dp"), None),
            P(("group", "dp"), None),
            P(),
            P(),
            P(),
            P(),
            P(("group", "dp")),
        ),
        out_specs=P(("group", "dp"), None),
        check_vma=False,
    )
```

```python
import functools

import jax
import jax.numpy as jnp
from jax import lax
from jax.experimental import pallas as pl
from jax.experimental.pallas import tpu as pltpu
from jax.sharding import PartitionSpec as P

LEN = 128
LANES = 128
PANEL = 8
HALF = 128
IN_FLIGHT = 6
MESSAGES = 4
HIGHEST = lax.Precision.HIGHEST
FRONT_VMEM_BYTES = 24 * 1024 * 1024
VMEM_BYTES = 8 * 1024 * 1024
NT = (((1,), (1,)), ((), ()))
TN = (((0,), (0,)), ((), ()))
NN = (((1,), (0,)), ((), ()))


def dot(a, b, dims, precision=HIGHEST):
    return lax.dot_general(a, b, dims, precision=precision, preferred_element_type=jnp.float32)


def places(order):
    shape = (order, 2 * order)
    lane = lax.broadcasted_iota(jnp.int32, shape, 1)
    return lax.broadcasted_iota(jnp.int32, shape, 0), lane % order


def dot_split(a, b, dims):
    a_high, b_high = a.astype(jnp.bfloat16), b.astype(jnp.bfloat16)
    a_low = (a - a_high.astype(jnp.float32)).astype(jnp.bfloat16)
    b_low = (b - b_high.astype(jnp.float32)).astype(jnp.bfloat16)
    return (
        dot(a_high, b_high, dims, None) + dot(a_low, b_high, dims, None) + dot(a_high, b_low, dims, None)
    )


def front_kernel(
    total_tokens, sequences, width,
    ids, acts, grad_q, grad_k, grad_v, proj_in, proj_q, proj_k, proj_v,
    factors, grams, query,
    acts_v, gq_v, gk_v, gv_v, pi_v, pq_v, pk_v, pv_v, sem,
):
    tokens = acts.shape[0]
    rows = min(HALF, tokens)
    moves = [(proj_k, pk_v), (grad_k, gk_v), (proj_v, pv_v), (grad_v, gv_v)]
    for first in range(0, tokens, rows):
        for src, dst, table, table_v in ((acts, acts_v, proj_in, pi_v), (grad_q, gq_v, proj_q, pq_v)):
            if first == 0:
                moves.append((table, table_v))
            box = pl.ds(first, rows)
            moves.append((src.at[box], dst.at[box]))
    copies = [pltpu.make_async_copy(src, dst, sem.at[i]) for i, (src, dst) in enumerate(moves)]
    for copy in copies[:IN_FLIGHT]:
        copy.start()
    waited = []

    def arrived(count):
        for _ in range(count):
            i = len(waited)
            copies[i].wait()
            if i + IN_FLIGHT < len(copies):
                copies[i + IN_FLIGHT].start()
            waited.append(i)

    left = lax.broadcasted_iota(jnp.int32, (width, 2 * width), 1) < width
    sums = [None, None]

    def gram_blocks(first, sides):
        coords = jnp.concatenate(sides, axis=0)
        high = coords.astype(jnp.bfloat16)
        low = (coords - high.astype(jnp.float32)).astype(jnp.bfloat16)
        for seq in range(rows // LEN):
            here = slice(seq * LEN, (seq + 1) * LEN)
            one = jnp.concatenate([high[:, here], low[:, here], high[:, here]], axis=1)
            other = jnp.concatenate([high[:, here], high[:, here], low[:, here]], axis=1)
            gram = dot(one, other, NT, None)
            grams[first // LEN + seq] = gram[:width] * (1.0 / LEN)
            squares = [gram[p * width : (p + 1) * width, p // 2 * 2 * width : (p // 2 + 1) * 2 * width] for p in range(4)]
            for i in range(2):
                pair = jnp.where(left, squares[2 * i], squares[2 * i + 1])
                sums[i] = pair if sums[i] is None else sums[i] + pair

    def projected(table, data, turned):
        return dot(data, table, NT, None).T if turned else dot(table, data, NT, None)

    arrived(4)
    coords_k = projected(pk_v[...], gk_v[...], False)
    coords_v = projected(pv_v[...], gv_v[...], True)
    ready = None
    for first in range(0, tokens, rows):
        whole = slice(first, first + rows)
        arrived(4 if first == 0 else 2)
        sides = [projected(pi_v[...], acts_v[whole], False), projected(pq_v[...], gq_v[whole], True)]
        if ready is not None:
            gram_blocks(*ready)
        ready = first, sides + [coords_k[:, whole], coords_v[:, whole]]
    gram_blocks(*ready)
    upper, lower = sums
    row, column = places(width)
    scale = 1.0 / total_tokens
    factors[:width] = jnp.where(column >= row, upper, lower) * scale
    diagonal = jnp.sum(jnp.where(column == row, lower, 0.0), axis=0, keepdims=True) * scale
    factors[width:] = jnp.broadcast_to(diagonal, (factors.shape[0] - width, 2 * width))
    half = width // 2
    for q in range(query.shape[0]):
        chosen = grams[ids[q]]
        query[q, :width] = chosen[:, 2 * width :]
        in_q = chosen[:, : 2 * width]
        query[q, width:] = jnp.where(left[:half], pltpu.roll(in_q[:half], width, 1), in_q[half:])


def damped(packed):
    order = packed.shape[1] // 2
    half = order // 2
    square, diagonal = packed[:order], packed[order : order + 1]
    row, column = places(order)
    turned = square.T
    turned = jnp.concatenate([turned[:order], turned[order:]], axis=1)
    on_diagonal = column == row
    first = jnp.where(column >= row, square, turned)
    second = jnp.where(column < row, square, turned)
    second = jnp.where(on_diagonal, diagonal, second)
    first_diagonal = jnp.sum(jnp.where(on_diagonal, square, 0.0), axis=0, keepdims=True)
    shape = (LANES, LANES)
    same = (
        lax.broadcasted_iota(jnp.int32, shape, 0) // order
        == lax.broadcasted_iota(jnp.int32, shape, 1) // order
    )
    diagonals = jnp.concatenate([first_diagonal, diagonal], axis=0)
    diagonals = jnp.concatenate([diagonals] * 4, axis=0)
    scales = 1.0 / dot(diagonals, jnp.where(same, 1.0 / order, 0.0), NN)
    damping = jnp.where(on_diagonal, 0.1, 0.0)
    first = first * scales[:1] + damping
    second = second * scales[1:2] + damping
    is_low = column < half
    low = jnp.where(is_low, first, pltpu.roll(second, half, 1))
    high = jnp.where(is_low, pltpu.roll(first, LANES - half, 1), second)
    scale = jnp.where(is_low[:8], spread_row(scales, 0), pltpu.roll(spread_row(scales, 1), half, 1))
    return low, high, scale


def spread_row(x, r):
    return jnp.broadcast_to(x[r : r + 1], x.shape)


def invert(low, high, scale):
    order = low.shape[0]
    half = order // 2
    groups = order // 8
    state = [[x[8 * g : 8 * g + 8] for g in range(groups)] for x in (low, high)]
    lane = lax.broadcasted_iota(jnp.int32, (8, LANES), 1)
    row = lax.broadcasted_iota(jnp.int32, (8, LANES), 0)
    column_of_lane = lane % half
    first_lane = lane - column_of_lane
    for start in range(0, order, PANEL):
        h, first = start // half, start % half
        spread = [
            [jnp.take_along_axis(state[h][g], first_lane + (first + j), axis=1) for g in range(groups)]
            for j in range(PANEL)
        ]
        in_panel = (column_of_lane >= first) & (column_of_lane < first + PANEL)
        state[h] = [jnp.where(in_panel, 0.0, x) for x in state[h]]
        for j in range(0, PANEL, 2):
            k = start + j
            g, r = k // 8, k % 8
            first_column, second_column = spread[j], spread[j + 1]
            a, c = spread_row(first_column[g], r), spread_row(first_column[g], r + 1)
            b, d = spread_row(second_column[g], r), spread_row(second_column[g], r + 1)
            inverse_det = 1.0 / (a * d - b * c)

            def eliminate(x, unit=None):
                top, bottom = spread_row(x[g], r), spread_row(x[g], r + 1)
                if unit is not None:
                    top = jnp.where(column_of_lane == unit, 1.0, top)
                    bottom = jnp.where(column_of_lane == unit + 1, 1.0, bottom)
                one, two = (d * top - b * bottom) * inverse_det, (a * bottom - c * top) * inverse_det
                done = [x[i] - first_column[i] * one - second_column[i] * two for i in range(groups)]
                done[g] = jnp.where(row == r, one, jnp.where(row == r + 1, two, done[g]))
                return done

            state = [eliminate(state[t], first + j if t == h else None) for t in range(2)]
            for i in range(j + 2, PANEL):
                spread[i] = eliminate(spread[i])
    return [jnp.concatenate([x * scale for x in half_state], axis=0) for half_state in state]


def invert_kernel(sequences, width, first, second, grams, train, side_v, left_v):
    half = width // 2
    low, high = invert(*damped(first[...] + second[...]))
    by_lanes = [
        jnp.concatenate([low[:, p * half : (p + 1) * half], high[:, p * half : (p + 1) * half]], axis=1)
        for p in range(4)
    ]
    inverse_in, inverse_k, inverse_q, inverse_v = by_lanes
    side_v[...] = jnp.zeros_like(side_v)
    side_v[width : 2 * width, 2 * width : 3 * width] = inverse_q
    side_v[width : 2 * width, 3 * width :] = inverse_q
    side_v[2 * width : 3 * width, :width] = inverse_k
    side_v[3 * width :, width : 2 * width] = inverse_v
    left_v[...] = dot_split(grams[...].reshape(sequences * width, 4 * width), side_v[...], NN)
    on_left = lax.broadcasted_iota(jnp.int32, (half, 2 * width), 1) < width
    for s in range(sequences):
        done = dot_split(inverse_in, left_v[pl.ds(s * width, width)], NN)
        train[s, :width] = done[:, : 2 * width]
        train[s, width:] = jnp.where(on_left, done[:half, 2 * width :], done[half:, 2 * width :])


def score_kernel(offsets, own, train, *refs):
    blocks, out, partial = refs[:-2], refs[-2], refs[-1]
    me = lax.axis_index("dp")
    slot = 0
    for block in blocks:
        for i in range(block.shape[0]):
            value = block[i]
            place = ((me ^ offsets[slot // own]) * own + slot % own) * 8
            for s in range(train.shape[0]):
                product = (train[s] * value).reshape(-1, 8, train.shape[2])
                partial[s, pl.ds(pl.multiple_of(place, 8), 8)] = jnp.sum(product, axis=0)
            slot += 1
    sequences, _, lanes = partial.shape
    queries = out.shape[1]
    by_query = jnp.sum(partial[...].reshape(sequences * queries, 8, lanes), axis=1)
    sums = dot(jnp.ones((8, lanes), jnp.float32), by_query, NT)
    for s in range(sequences):
        out[pl.ds(s, 1)] = sums[:1, s * queries : (s + 1) * queries]


def exchange(x, devices, distance):
    return lax.ppermute(x, "dp", [(i, i ^ distance) for i in range(devices)])


def per_device(acts, grad_q, grad_k, grad_v, proj_in, proj_q, proj_k, proj_v, query_ids):
    devices = lax.axis_size("dp")
    steps = devices.bit_length() - 1
    tokens, width = acts.shape[0], proj_in.shape[0]
    sequences, own_queries = tokens // LEN, query_ids.shape[0]
    queries = own_queries * devices
    f32 = jnp.float32
    in_vmem = pl.BlockSpec(memory_space=pltpu.VMEM)
    in_hbm = pl.BlockSpec(memory_space=pltpu.HBM)
    params = pltpu.CompilerParams(vmem_limit_bytes=VMEM_BYTES)
    tables = tuple(
        pltpu.with_memory_space_constraint(t, pltpu.HBM)
        for t in (acts, grad_q, grad_k, grad_v, proj_in, proj_q, proj_k, proj_v)
    )

    factors, grams, query = pl.pallas_call(
        functools.partial(front_kernel, tokens * devices, sequences, width),
        out_shape=(
            jax.ShapeDtypeStruct((width + 8, 2 * width), f32),
            jax.ShapeDtypeStruct((sequences, width, 4 * width), f32),
            jax.ShapeDtypeStruct((own_queries, 3 * width // 2, 2 * width), f32),
        ),
        in_specs=[pl.BlockSpec(memory_space=pltpu.SMEM)] + [in_hbm] * 8,
        out_specs=(in_vmem,) * 3,
        scratch_shapes=[pltpu.VMEM(t.shape, t.dtype) for t in tables]
        + [pltpu.SemaphoreType.DMA((6 + 2 * -(-tokens // HALF),))],
        compiler_params=pltpu.CompilerParams(vmem_limit_bytes=FRONT_VMEM_BYTES),
        name="front",
    )(query_ids, *tables)

    query_bits = list(range(1, steps))[::-1]

    def send(items, bit):
        size = -(-len(items) // MESSAGES)
        groups = [items[i : i + size] for i in range(0, len(items), size)]
        return [
            (
                exchange(jnp.concatenate([x for x, _ in group], axis=0) if size > 1 else group[0][0], devices, 1 << bit),
                [offset ^ 1 << bit for _, offsets in group for offset in offsets],
            )
            for group in groups
        ]

    def after(items, token):
        arrays = lax.optimization_barrier((*[x for x, _ in items], token))[:-1]
        return [(x, offsets) for x, (_, offsets) in zip(arrays, items)]

    def both_cores(items):
        joined = jnp.concatenate([x for x, _ in items], axis=0)
        offsets = [offset for _, part in items for offset in part]
        return [(joined, offsets), (exchange(joined, devices, 1), [offset ^ 1 for offset in offsets])]

    own = [(query, [0])]
    mine, blocks, pending, early = factors, [], [], []
    for step in range(steps):
        theirs = exchange(mine, devices, 1 << step)
        if step == 0:
            pending = send(own, query_bits[0])
        elif step == 1:
            early = send(after(own, mine), query_bits[-1])
        else:
            blocks += after(pending, mine)
            last = step == steps - 1
            pending = send(([] if last else after(own, mine)) + blocks, query_bits[step - 1])
            if last:
                first = both_cores(own + blocks)
        if step < steps - 1:
            mine = mine + theirs
    terms = (mine, theirs)
    train = pl.pallas_call(
        functools.partial(invert_kernel, sequences, width),
        out_shape=jax.ShapeDtypeStruct((sequences, 3 * width // 2, 2 * width), f32),
        in_specs=[in_vmem] * 3,
        out_specs=in_vmem,
        scratch_shapes=[
            pltpu.VMEM((4 * width, 4 * width), f32),
            pltpu.VMEM((sequences * width, 4 * width), f32),
        ],
        compiler_params=params,
        name="invert",
    )(*terms, grams)
    last = both_cores(after(pending + early, train))
    blocks = [x for x, _ in first + last]
    offsets = [offset for _, offsets in first + last for offset in offsets]

    return pl.pallas_call(
        functools.partial(score_kernel, offsets, own_queries),
        out_shape=jax.ShapeDtypeStruct((sequences, queries), f32),
        in_specs=[in_vmem] * (1 + len(blocks)),
        out_specs=in_vmem,
        scratch_shapes=[pltpu.VMEM((sequences, queries * 8, 2 * width), f32)],
        compiler_params=params,
        name="scores",
    )(train, *blocks)


def solution(mesh):
    return jax.shard_map(
        per_device,
        mesh=mesh,
        in_specs=(
            P(("group", "dp"), None),
            P(("group", "dp"), None),
            P(("group", "dp"), None),
            P(("group", "dp"), None),
            P(),
            P(),
            P(),
            P(),
            P(("group", "dp")),
        ),
        out_specs=P(("group", "dp"), None),
        check_vma=False,
    )
```

```python
import functools

import jax
import jax.numpy as jnp
from jax import lax
from jax.experimental import pallas as pl
from jax.experimental.pallas import tpu as pltpu
from jax.sharding import PartitionSpec as P

LEN = 128
LANES = 128
PANEL = 8
HALF = 128
IN_FLIGHT = 12
MESSAGES = 4
HIGHEST = lax.Precision.HIGHEST
FRONT_VMEM_BYTES = 24 * 1024 * 1024
VMEM_BYTES = 8 * 1024 * 1024
NT = (((1,), (1,)), ((), ()))
TN = (((0,), (0,)), ((), ()))
NN = (((1,), (0,)), ((), ()))


def dot(a, b, dims, precision=HIGHEST):
    return lax.dot_general(a, b, dims, precision=precision, preferred_element_type=jnp.float32)


def places(order):
    shape = (order, 2 * order)
    lane = lax.broadcasted_iota(jnp.int32, shape, 1)
    return lax.broadcasted_iota(jnp.int32, shape, 0), lane % order


def dot_split(a, b, dims):
    a_high, b_high = a.astype(jnp.bfloat16), b.astype(jnp.bfloat16)
    a_low = (a - a_high.astype(jnp.float32)).astype(jnp.bfloat16)
    b_low = (b - b_high.astype(jnp.float32)).astype(jnp.bfloat16)
    return (
        dot(a_high, b_high, dims, None) + dot(a_low, b_high, dims, None) + dot(a_high, b_low, dims, None)
    )


def front_kernel(
    total_tokens, sequences, width,
    ids, acts, grad_q, grad_k, grad_v, proj_in, proj_q, proj_k, proj_v,
    factors, grams, query,
    acts_v, gq_v, gk_v, gv_v, pi_v, pq_v, pk_v, pv_v, sem,
):
    tokens = acts.shape[0]
    rows = min(HALF, tokens)
    moves = [(proj_k, pk_v), (grad_k, gk_v), (proj_v, pv_v), (grad_v, gv_v)]
    for first in range(0, tokens, rows):
        for src, dst, table, table_v in ((acts, acts_v, proj_in, pi_v), (grad_q, gq_v, proj_q, pq_v)):
            if first == 0:
                moves.append((table, table_v))
            box = pl.ds(first, rows)
            moves.append((src.at[box], dst.at[box]))
    copies = [pltpu.make_async_copy(src, dst, sem.at[i]) for i, (src, dst) in enumerate(moves)]
    for copy in copies[:IN_FLIGHT]:
        copy.start()
    waited = []

    def arrived(count):
        for _ in range(count):
            i = len(waited)
            copies[i].wait()
            if i + IN_FLIGHT < len(copies):
                copies[i + IN_FLIGHT].start()
            waited.append(i)

    left = lax.broadcasted_iota(jnp.int32, (width, 2 * width), 1) < width
    sums = [None, None]

    def gram_blocks(first, sides):
        coords = jnp.concatenate(sides, axis=0)
        high = coords.astype(jnp.bfloat16)
        low = (coords - high.astype(jnp.float32)).astype(jnp.bfloat16)
        for seq in range(rows // LEN):
            here = slice(seq * LEN, (seq + 1) * LEN)
            one = jnp.concatenate([high[:, here], low[:, here], high[:, here]], axis=1)
            other = jnp.concatenate([high[:, here], high[:, here], low[:, here]], axis=1)
            gram = dot(one, other, NT, None)
            grams[first // LEN + seq] = gram[:width] * (1.0 / LEN)
            squares = [gram[p * width : (p + 1) * width, p // 2 * 2 * width : (p // 2 + 1) * 2 * width] for p in range(4)]
            for i in range(2):
                pair = jnp.where(left, squares[2 * i], squares[2 * i + 1])
                sums[i] = pair if sums[i] is None else sums[i] + pair

    def projected(table, data, turned):
        return dot(data, table, NT, None).T if turned else dot(table, data, NT, None)

    arrived(4)
    coords_k = projected(pk_v[...], gk_v[...], False)
    coords_v = projected(pv_v[...], gv_v[...], True)
    ready = None
    for first in range(0, tokens, rows):
        whole = slice(first, first + rows)
        arrived(4 if first == 0 else 2)
        sides = [projected(pi_v[...], acts_v[whole], False), projected(pq_v[...], gq_v[whole], True)]
        if ready is not None:
            gram_blocks(*ready)
        ready = first, sides + [coords_k[:, whole], coords_v[:, whole]]
    gram_blocks(*ready)
    upper, lower = sums
    row, column = places(width)
    scale = 1.0 / total_tokens
    factors[:width] = jnp.where(column >= row, upper, lower) * scale
    diagonal = jnp.sum(jnp.where(column == row, lower, 0.0), axis=0, keepdims=True) * scale
    factors[width:] = jnp.broadcast_to(diagonal, (factors.shape[0] - width, 2 * width))
    half = width // 2
    for q in range(query.shape[0]):
        chosen = grams[ids[q]]
        query[q, :width] = chosen[:, 2 * width :]
        in_q = chosen[:, : 2 * width]
        query[q, width:] = jnp.where(left[:half], pltpu.roll(in_q[:half], width, 1), in_q[half:])


def damped(packed):
    order = packed.shape[1] // 2
    half = order // 2
    square, diagonal = packed[:order], packed[order : order + 1]
    row, column = places(order)
    turned = square.T
    turned = jnp.concatenate([turned[:order], turned[order:]], axis=1)
    on_diagonal = column == row
    first = jnp.where(column >= row, square, turned)
    second = jnp.where(column < row, square, turned)
    second = jnp.where(on_diagonal, diagonal, second)
    first_diagonal = jnp.sum(jnp.where(on_diagonal, square, 0.0), axis=0, keepdims=True)
    shape = (LANES, LANES)
    same = (
        lax.broadcasted_iota(jnp.int32, shape, 0) // order
        == lax.broadcasted_iota(jnp.int32, shape, 1) // order
    )
    diagonals = jnp.concatenate([first_diagonal, diagonal], axis=0)
    diagonals = jnp.concatenate([diagonals] * 4, axis=0)
    scales = 1.0 / dot(diagonals, jnp.where(same, 1.0 / order, 0.0), NN)
    damping = jnp.where(on_diagonal, 0.1, 0.0)
    first = first * scales[:1] + damping
    second = second * scales[1:2] + damping
    is_low = column < half
    low = jnp.where(is_low, first, pltpu.roll(second, half, 1))
    high = jnp.where(is_low, pltpu.roll(first, LANES - half, 1), second)
    scale = jnp.where(is_low[:8], spread_row(scales, 0), pltpu.roll(spread_row(scales, 1), half, 1))
    return low, high, scale


def spread_row(x, r):
    return jnp.broadcast_to(x[r : r + 1], x.shape)


def invert(low, high, scale):
    order = low.shape[0]
    half = order // 2
    groups = order // 8
    state = [[x[8 * g : 8 * g + 8] for g in range(groups)] for x in (low, high)]
    lane = lax.broadcasted_iota(jnp.int32, (8, LANES), 1)
    row = lax.broadcasted_iota(jnp.int32, (8, LANES), 0)
    column_of_lane = lane % half
    first_lane = lane - column_of_lane
    for start in range(0, order, PANEL):
        h, first = start // half, start % half
        spread = [
            [jnp.take_along_axis(state[h][g], first_lane + (first + j), axis=1) for g in range(groups)]
            for j in range(PANEL)
        ]
        in_panel = (column_of_lane >= first) & (column_of_lane < first + PANEL)
        state[h] = [jnp.where(in_panel, 0.0, x) for x in state[h]]
        for j in range(0, PANEL, 2):
            k = start + j
            g, r = k // 8, k % 8
            first_column, second_column = spread[j], spread[j + 1]
            a, c = spread_row(first_column[g], r), spread_row(first_column[g], r + 1)
            b, d = spread_row(second_column[g], r), spread_row(second_column[g], r + 1)
            inverse_det = 1.0 / (a * d - b * c)

            def eliminate(x, unit=None):
                top, bottom = spread_row(x[g], r), spread_row(x[g], r + 1)
                if unit is not None:
                    top = jnp.where(column_of_lane == unit, 1.0, top)
                    bottom = jnp.where(column_of_lane == unit + 1, 1.0, bottom)
                one, two = (d * top - b * bottom) * inverse_det, (a * bottom - c * top) * inverse_det
                done = [x[i] - first_column[i] * one - second_column[i] * two for i in range(groups)]
                done[g] = jnp.where(row == r, one, jnp.where(row == r + 1, two, done[g]))
                return done

            state = [eliminate(state[t], first + j if t == h else None) for t in range(2)]
            for i in range(j + 2, PANEL):
                spread[i] = eliminate(spread[i])
    return [jnp.concatenate([x * scale for x in half_state], axis=0) for half_state in state]


def invert_kernel(sequences, width, first, second, grams, train, side_v, left_v):
    half = width // 2
    low, high = invert(*damped(first[...] + second[...]))
    by_lanes = [
        jnp.concatenate([low[:, p * half : (p + 1) * half], high[:, p * half : (p + 1) * half]], axis=1)
        for p in range(4)
    ]
    inverse_in, inverse_k, inverse_q, inverse_v = by_lanes
    side_v[...] = jnp.zeros_like(side_v)
    side_v[width : 2 * width, 2 * width : 3 * width] = inverse_q
    side_v[width : 2 * width, 3 * width :] = inverse_q
    side_v[2 * width : 3 * width, :width] = inverse_k
    side_v[3 * width :, width : 2 * width] = inverse_v
    left_v[...] = dot_split(grams[...].reshape(sequences * width, 4 * width), side_v[...], NN)
    on_left = lax.broadcasted_iota(jnp.int32, (half, 2 * width), 1) < width
    for s in range(sequences):
        done = dot_split(inverse_in, left_v[pl.ds(s * width, width)], NN)
        train[s, :width] = done[:, : 2 * width]
        train[s, width:] = jnp.where(on_left, done[:half, 2 * width :], done[half:, 2 * width :])


def score_kernel(offsets, own, train, *refs):
    blocks, out, partial = refs[:-2], refs[-2], refs[-1]
    me = lax.axis_index("dp")
    slot = 0
    for block in blocks:
        for i in range(block.shape[0]):
            value = block[i]
            place = ((me ^ offsets[slot // own]) * own + slot % own) * 8
            for s in range(train.shape[0]):
                product = (train[s] * value).reshape(-1, 8, train.shape[2])
                partial[s, pl.ds(pl.multiple_of(place, 8), 8)] = jnp.sum(product, axis=0)
            slot += 1
    ones = jnp.ones((8, train.shape[2]), jnp.float32)
    for s in range(train.shape[0]):
        by_query = jnp.sum(partial[s].reshape(-1, 8, train.shape[2]), axis=1)
        out[pl.ds(s, 1)] = dot(ones, by_query, NT)[:1]


def exchange(x, devices, distance):
    return lax.ppermute(x, "dp", [(i, i ^ distance) for i in range(devices)])


def per_device(acts, grad_q, grad_k, grad_v, proj_in, proj_q, proj_k, proj_v, query_ids):
    devices = lax.axis_size("dp")
    steps = devices.bit_length() - 1
    tokens, width = acts.shape[0], proj_in.shape[0]
    sequences, own_queries = tokens // LEN, query_ids.shape[0]
    queries = own_queries * devices
    f32 = jnp.float32
    in_vmem = pl.BlockSpec(memory_space=pltpu.VMEM)
    in_hbm = pl.BlockSpec(memory_space=pltpu.HBM)
    params = pltpu.CompilerParams(vmem_limit_bytes=VMEM_BYTES)
    tables = tuple(
        pltpu.with_memory_space_constraint(t, pltpu.HBM)
        for t in (acts, grad_q, grad_k, grad_v, proj_in, proj_q, proj_k, proj_v)
    )

    factors, grams, query = pl.pallas_call(
        functools.partial(front_kernel, tokens * devices, sequences, width),
        out_shape=(
            jax.ShapeDtypeStruct((width + 8, 2 * width), f32),
            jax.ShapeDtypeStruct((sequences, width, 4 * width), f32),
            jax.ShapeDtypeStruct((own_queries, 3 * width // 2, 2 * width), f32),
        ),
        in_specs=[pl.BlockSpec(memory_space=pltpu.SMEM)] + [in_hbm] * 8,
        out_specs=(in_vmem,) * 3,
        scratch_shapes=[pltpu.VMEM(t.shape, t.dtype) for t in tables]
        + [pltpu.SemaphoreType.DMA((6 + 2 * -(-tokens // HALF),))],
        compiler_params=pltpu.CompilerParams(vmem_limit_bytes=FRONT_VMEM_BYTES),
        name="front",
    )(query_ids, *tables)

    query_bits = list(range(1, steps))[::-1]

    def send(items, bit):
        size = -(-len(items) // MESSAGES)
        groups = [items[i : i + size] for i in range(0, len(items), size)]
        return [
            (
                exchange(jnp.concatenate([x for x, _ in group], axis=0) if size > 1 else group[0][0], devices, 1 << bit),
                [offset ^ 1 << bit for _, offsets in group for offset in offsets],
            )
            for group in groups
        ]

    def after(items, token):
        arrays = lax.optimization_barrier((*[x for x, _ in items], token))[:-1]
        return [(x, offsets) for x, (_, offsets) in zip(arrays, items)]

    def both_cores(items):
        joined = jnp.concatenate([x for x, _ in items], axis=0)
        offsets = [offset for _, part in items for offset in part]
        return [(joined, offsets), (exchange(joined, devices, 1), [offset ^ 1 for offset in offsets])]

    own = [(query, [0])]
    mine, blocks, pending, early = factors, [], [], []
    for step in range(steps):
        theirs = exchange(mine, devices, 1 << step)
        if step == 0:
            pending = send(own, query_bits[0])
        elif step == 1:
            early = send(after(own, mine), query_bits[-1])
        else:
            blocks += after(pending, mine)
            last = step == steps - 1
            pending = send(([] if last else after(own, mine)) + blocks, query_bits[step - 1])
            if last:
                first = both_cores(own + blocks)
        if step < steps - 1:
            mine = mine + theirs
    terms = (mine, theirs)
    train = pl.pallas_call(
        functools.partial(invert_kernel, sequences, width),
        out_shape=jax.ShapeDtypeStruct((sequences, 3 * width // 2, 2 * width), f32),
        in_specs=[in_vmem] * 3,
        out_specs=in_vmem,
        scratch_shapes=[
            pltpu.VMEM((4 * width, 4 * width), f32),
            pltpu.VMEM((sequences * width, 4 * width), f32),
        ],
        compiler_params=params,
        name="invert",
    )(*terms, grams)
    last = both_cores(after(pending + early, train))
    blocks = [x for x, _ in first + last]
    offsets = [offset for _, offsets in first + last for offset in offsets]

    return pl.pallas_call(
        functools.partial(score_kernel, offsets, own_queries),
        out_shape=jax.ShapeDtypeStruct((sequences, queries), f32),
        in_specs=[in_vmem] * (1 + len(blocks)),
        out_specs=in_vmem,
        scratch_shapes=[pltpu.VMEM((sequences, queries * 8, 2 * width), f32)],
        compiler_params=params,
        name="scores",
    )(train, *blocks)


def solution(mesh):
    return jax.shard_map(
        per_device,
        mesh=mesh,
        in_specs=(
            P(("group", "dp"), None),
            P(("group", "dp"), None),
            P(("group", "dp"), None),
            P(("group", "dp"), None),
            P(),
            P(),
            P(),
            P(),
            P(("group", "dp")),
        ),
        out_specs=P(("group", "dp"), None),
        check_vma=False,
    )
```
